256 devices in a mesh: tile: 32 (over z, x_hi, core), src: 2 (over x_lo), elec: 4 (over y).
Axes of the slice: x: 4 (x_hi: 2, x_lo: 2; x = x_hi * 2 + x_lo), y: 4, z: 8, core: 2. Of those that a mesh axis runs over, the one named last changes fastest.
Arguments:
- potential: float32 [8, 256, 512, 256], P('src', 'tile', 'elec'), may hold values from -6 to 6
- source_term: float32 [8, 256, 512, 256], P('src', 'tile', 'elec'), may hold values from -6 to 6
- conductivity: float32 [256, 512, 256], P('tile', 'elec'), may hold values from 0.1 to 10
- contact_map: int32 [256, 512], P('tile', 'elec'), may hold values from 0 to 2048, as said below
- admittance: float32 [2048], replicated, may hold values from 0.5 to 5
- impedance: float32 [16, 128, 128], P('elec'), may hold values from -2 to 2
- source_pairs: int32 [8, 2], P('src'), may hold values from 0 to 2047, as said below
- amplitudes: float32 [8], P('src'), may hold values from 1 to 4
Outputs:
- relaxed_potential: float32 [8, 256, 512, 256], P('src', 'tile', 'elec')
- electrode_volts: float32 [8, 2048], P('src', 'elec')
The draws below stay inside these ranges and needn't reach their ends.
Inputs may be any that keep to these rules, and one draw needn't show every extreme that they name: `contact_map`: values below 2048 name the touching electrode; 2048 marks an untouched row. `source_pairs`: the anode and cathode of a source differ.
All inputs are finite; a program needn't handle non-finite values.
Results may differ from the reference program's by a relative error of at most 0.0003.
Values sent between devices are 32-bit elements; how exact they have to be, the bound alone decides.
No kernel may reach another device: no remote copies, remote signals or barrier semaphores. Data moves between devices by JAX's collectives and lax.ppermute only.
A program may use at most 128 MiB of HBM per device.

```python
import math
import jax
import jax.numpy as jnp
from jax import lax

NZ = 256
SWEEPS = 2
BLK = 128
NX = 256
NY = 512
SRC = 8
NB = 16
NE = 2048


def draw_contact_map(key, part):
    key_level = jax.random.fold_in(key, 11)
    key_which = jax.random.fold_in(key, 12)
    x_index = lax.broadcasted_iota(jnp.int32, (NX, NY), 0)
    draw_level = jax.random.randint(key_level, (NX, NY), 0, NX)
    electrode_draw = jax.random.randint(key_which, (NX, NY), 0, NE)
    return jnp.where(draw_level < x_index, electrode_draw, NE).astype(jnp.int32)


def draw_source_pairs(key, part):
    key_anode = jax.random.fold_in(key, 21)
    key_offset = jax.random.fold_in(key, 22)
    key_pick = jax.random.fold_in(key, 23)
    key_low = jax.random.fold_in(key, 24)
    key_high = jax.random.fold_in(key, 25)
    anodes = jax.random.randint(key_anode, (SRC,), 0, NE)
    offset = jax.random.randint(key_offset, (SRC,), 1, NE)
    cathode = (anodes + offset) % NE
    source_index = jnp.arange(SRC, dtype=jnp.int32)
    picked = jax.random.randint(key_pick, (), 0, SRC)
    second = (picked + 1) % SRC
    low_anode = jax.random.randint(key_low, (), 0, NE - 1)
    high_cathode = jax.random.randint(key_high, (), 1, NE)
    anodes = jnp.where(source_index == picked, low_anode, anodes)
    cathode = jnp.where(source_index == picked, NE - 1, cathode)
    anodes = jnp.where(source_index == second, 0, anodes)
    cathode = jnp.where(source_index == second, high_cathode, cathode)
    return jnp.stack([anodes, cathode], axis=1).astype(jnp.int32)


def shard_levels(rng, extent, pieces, least, largest):
    loudness, own = 1.0, jax.random.fold_in(rng, 6)
    for axis_at, shards_of in pieces:
        steps = jnp.exp(jax.random.uniform(jax.random.fold_in(own, axis_at), (shards_of,), jnp.float32, least / len(pieces), largest / len(pieces)))
        loudness = loudness * jnp.repeat(steps, extent[axis_at] // shards_of).reshape([-1 if axis == axis_at else 1 for axis in range(len(extent))])
    return loudness


def scatter_about(stream_key, extent, width, bound, cuts=(), kind=jnp.bfloat16):
    result = jax.random.normal(stream_key, extent, jnp.float32) * width
    if len(cuts) > 0:
        result = shard_levels(stream_key, extent, cuts, -0.22, 0.18) * result
    return jnp.clip(result, min=-bound, max=bound).astype(kind)


def setup_inputs(seed: int = 0) -> dict:
    key_list = jax.random.split(jax.random.key(seed), 9)
    potential = scatter_about(key_list[0], (SRC, NX, NY, NZ), 1.0, 6.0, ((0, 2), (1, 32), (2, 4)), jnp.float32)
    source_term = scatter_about(key_list[1], (SRC, NX, NY, NZ), 1.0, 6.0, ((0, 2), (1, 32), (2, 4)), jnp.float32)
    conductivity = jnp.clip(jnp.exp(math.log(10.0) - 4.6051702 * jax.random.uniform(key_list[2], (NX, NY, NZ), jnp.float32) ** shard_levels(key_list[2], (NX, NY, NZ), ((0, 32), (1, 4)), -0.2, 0.2)), 0.1, 10.0)
    contact_map = draw_contact_map(jax.random.fold_in(key_list[8], 71), 0)
    admittance = jnp.clip(jnp.exp(jax.random.uniform(key_list[4], (NE,), jnp.float32, math.log(0.5), math.log(5.0))), 0.5, 5.0)
    impedance = scatter_about(key_list[5], (NB, BLK, BLK), (BLK // 16) ** -0.5, 2.0, ((0, 4),), jnp.float32)
    source_pairs = draw_source_pairs(jax.random.fold_in(key_list[8], 71), 0)
    amplitudes = jnp.clip(jnp.exp(math.log(4.0) - 1.3862944 * jax.random.uniform(key_list[7], (SRC,), jnp.float32) ** shard_levels(key_list[7], (SRC,), ((0, 2),), -0.2, 0.2)), 1.0, 4.0)
    return {"potential": potential, "source_term": source_term, "conductivity": conductivity, "contact_map": contact_map, "admittance": admittance, "impedance": impedance, "source_pairs": source_pairs, "amplitudes": amplitudes}


OMEGA = 0.8
EXACT = lax.Precision.HIGHEST


def neighbours(padded):
    return [padded[:-2, 1:-1, 1:-1], padded[2:, 1:-1, 1:-1],
            padded[1:-1, :-2, 1:-1], padded[1:-1, 2:, 1:-1],
            padded[1:-1, 1:-1, :-2], padded[1:-1, 1:-1, 2:]]


def face_weights(middle, padded):
    return [2.0 * middle * neighbour / (middle + neighbour) for neighbour in neighbours(padded)]


def reference(potential, source_term, conductivity, contact_map, admittance, impedance, source_pairs, amplitudes):
    weights = face_weights(conductivity, jnp.pad(conductivity, 1))
    row_ids = contact_map.reshape(-1)
    touched = row_ids < NE
    clipped = jnp.minimum(row_ids, NE - 1)
    zeta_rows = jnp.where(touched, admittance[clipped], jnp.float32(0.0))
    zeta = zeta_rows.reshape(NX, NY, 1)
    diagonal = weights[0] + weights[1] + weights[2] + weights[3] + weights[4] + weights[5] + zeta
    electrode_ids = jnp.arange(NE, dtype=jnp.int32)

    def one_source(inputs):
        current, source, amplitude, electrode_pair = inputs
        for sweep in range(SWEEPS):
            others = neighbours(jnp.pad(current, 1))
            pulled = weights[0] * others[0]
            for number in range(1, 6):
                pulled = pulled + weights[number] * others[number]
            current = current + OMEGA * (source - diagonal * current + pulled) / diagonal
        row_means = jnp.mean(current, axis=-1).reshape(-1)
        contact = jax.ops.segment_sum(row_means, row_ids, num_segments=NE + 1)[:NE]
        injected = amplitude * (electrode_ids == electrode_pair[0]).astype(jnp.float32) - amplitude * (electrode_ids == electrode_pair[1]).astype(jnp.float32)
        charges = (contact + injected).reshape(NB, BLK)
        voltages = jnp.einsum("bij,bj->bi", impedance, charges, precision=EXACT).reshape(NE)
        row_volts = jnp.where(touched, voltages[clipped], jnp.float32(0.0)).reshape(NX, NY, 1)
        relaxed = current + zeta * (row_volts - current) / diagonal
        return relaxed, voltages

    relaxed_potential, electrode_volts = lax.map(one_source, (potential, source_term, amplitudes, source_pairs))
    return relaxed_potential, electrode_volts
```

```python
import jax
import jax.numpy as jnp
from jax import lax
from jax.experimental import pallas as pl
from jax.experimental.pallas import tpu as pltpu
from jax.sharding import Mesh
from jax.sharding import PartitionSpec as P

OMEGA = 0.8
KEEP = 1.0 - OMEGA
TINY = 1e-30
F32 = jnp.float32
EXACT = lax.Precision.HIGHEST
VMEM_LIMIT = 24 * 1024 * 1024
TILE = ("zx", "core")

NT = (((1,), (1,)), ((), ()))


def params():
    return pltpu.CompilerParams(vmem_limit_bytes=VMEM_LIMIT)


def vmem():
    return pl.BlockSpec(memory_space=pltpu.VMEM)


def smem():
    return pl.BlockSpec(memory_space=pltpu.SMEM)


def hbm():
    return pl.BlockSpec(memory_space=pl.ANY)


def f32(*shape):
    return jax.ShapeDtypeStruct(shape, F32)


def kept(*shape):
    return pltpu.VMEM(shape, F32)


def face(a, b):
    return 2.0 * a * b / jnp.maximum(a + b, TINY)


def iota(shape, dim):
    return lax.broadcasted_iota(jnp.int32, shape, dim)


def shift_up(a, axis):
    return pltpu.roll(a, a.shape[axis] - 1, axis)


def shift_down(a, axis):
    return pltpu.roll(a, 1, axis)


def in_line(flux_weight, u, axis):
    return flux_weight * shift_up(u, axis) + shift_down(flux_weight * u, axis)


def line_weight(c, axis):
    w = face(c, shift_up(c, axis))
    return jnp.where(iota(c.shape, axis) < c.shape[axis] - 1, w, 0.0)


def both_sides(w, axis):
    return w + shift_down(w, axis)


def row_sums(slabs):
    folded = jnp.concatenate([p[:, :128] + p[:, 128:] for p in slabs], axis=0)
    head = folded.astype(jnp.bfloat16)
    rest = (folded - head.astype(F32)).astype(jnp.bfloat16)
    ones = jnp.ones((8, 128), jnp.bfloat16)
    total = lax.dot_general(ones, head, NT, preferred_element_type=F32)
    total = total + lax.dot_general(ones, rest, NT, preferred_element_type=F32)
    return jnp.concatenate([total[0:1, 128 * s : 128 * s + 128] for s in range(4)], axis=0)


def to_lanes(column):
    mask = iota((8, 128), 0) == iota((8, 128), 1)
    return jnp.sum(jnp.where(mask, column, jnp.zeros_like(column)), axis=0, keepdims=True)


def gather_rows(ids, table):
    block = lax.shift_right_logical(ids, 7)
    lane = lax.bitwise_and(ids, 127)
    found = jnp.zeros(ids.shape, F32)
    for b in range(16):
        row = jnp.broadcast_to(table[b : b + 1], ids.shape)
        got = jnp.take_along_axis(row, lane, axis=1)
        found = jnp.where(block == b, got, found)
    return found


def edges_kernel(u_lo, u_hi, c_lo, c_hi, cmap, out_lo, out_hi):
    for out, u, c, near, far, lane in (
        (out_lo, u_lo, c_lo, 0, 1, 0),
        (out_hi, u_hi, c_hi, 7, 6, 127),
    ):
        for x in range(8):
            for s in range(4):
                out[8 * s + x : 8 * s + x + 1, :] = u[s, x, near : near + 1, :]
            out[32 + x : 33 + x, :] = c[x, near : near + 1, :]
            out[40 + x : 41 + x, :] = c[x, far : far + 1, :]
        out[48:56, :] = jnp.zeros((8, 256), F32)
        out[48:49, 0:128] = to_lanes(cmap[:, lane : lane + 1].astype(F32))


def edges(u, c, cmap):
    return pl.pallas_call(
        edges_kernel,
        grid=(1,),
        in_specs=[
            pl.BlockSpec((4, 8, 8, 256), lambda i: (0, 0, 0, 0)),
            pl.BlockSpec((4, 8, 8, 256), lambda i: (0, 0, 15, 0)),
            pl.BlockSpec((8, 8, 256), lambda i: (0, 0, 0)),
            pl.BlockSpec((8, 8, 256), lambda i: (0, 15, 0)),
            pl.BlockSpec((8, 128), lambda i: (0, 0)),
        ],
        out_specs=[pl.BlockSpec((56, 256), lambda i: (0, 0))] * 2,
        out_shape=[f32(56, 256)] * 2,
        compiler_params=params(),
        name="edges",
    )(u, u, c, c, cmap)


def faces_kernel(c0, c1, c6, c7, cmap, y_lo, y_hi, down, up):
    for out, near, far, x in ((down, c0, c1, 0), (up, c7, c6, 7)):
        out[0:128, :] = near[0]
        out[128:256, :] = far[0]
        out[256:272, :] = jnp.zeros((16, 256), F32)
        out[256:257, :] = y_lo[32 + x : 33 + x, :]
        out[257:258, :] = y_hi[32 + x : 33 + x, :]
        out[258:259, 0:128] = cmap[x : x + 1, :].astype(F32)


def faces(c, cmap, y_lo, y_hi):
    def row(x):
        return pl.BlockSpec((1, 128, 256), lambda i: (x, 0, 0))

    edge = pl.BlockSpec((56, 256), lambda i: (0, 0))
    return pl.pallas_call(
        faces_kernel,
        grid=(1,),
        in_specs=[row(0), row(1), row(6), row(7), pl.BlockSpec((8, 128), lambda i: (0, 0)), edge, edge],
        out_specs=[pl.BlockSpec((272, 256), lambda i: (0, 0))] * 2,
        out_shape=[f32(272, 256)] * 2,
        compiler_params=params(),
        name="faces",
    )(c, c, c, c, cmap, y_lo, y_hi)


def local_sweep(u, below, above, f, w_below, w_above, wy, wz, gain):
    pulled = f + in_line(wy, u, 0)
    pulled = pulled + in_line(wz, u, 1)
    if below is not None:
        pulled = pulled + w_below * below
    if above is not None:
        pulled = pulled + w_above * above
    return KEEP * u + gain * pulled


def inner_kernel(
    u_hbm, f_hbm, c_hbm, cmap, admittance, y_lo, y_hi,
    u1, u2, wx, wy, wz, gain, wyl, wyh, zeta_t, sums,
    u, f, c, sems,
):
    copy_c = pltpu.make_async_copy(c_hbm, c, sems.at[0])
    copy_u = pltpu.make_async_copy(u_hbm, u, sems.at[1])
    copy_f = pltpu.make_async_copy(f_hbm, f, sems.at[2])
    copy_c.start()
    copy_u.start()
    copy_f.start()
    zeta = gather_rows(cmap[...], admittance[...])
    padded = jnp.concatenate([zeta, jnp.zeros((120, 128), F32)], axis=0)
    zeta_t[...] = jnp.transpose(padded)
    copy_c.wait()
    for x in range(8):
        here = c[x]
        if x < 7:
            wx[x] = face(here, c[x + 1])
        along_y = line_weight(here, 0)
        along_z = line_weight(here, 1)
        wy[x] = along_y
        wz[x] = along_z
        low = face(here[0:1], y_lo[32 + x : 33 + x, :])
        high = face(here[127:128], y_hi[32 + x : 33 + x, :])
        wyl[x : x + 1, :] = low
        wyh[x : x + 1, :] = high
        diag = both_sides(along_y, 0) + both_sides(along_z, 1) + zeta_t[:, x : x + 1]
        row = iota((128, 256), 0)
        diag = diag + jnp.where(row == 0, low, 0.0) + jnp.where(row == 127, high, 0.0)
        if x > 0:
            diag = diag + wx[x - 1]
        if x < 7:
            diag = diag + wx[x]
        gain[x] = diag if x in (0, 7) else OMEGA / diag
    copy_u.wait()
    copy_f.wait()

    def first(x, carry):
        for s in range(4):
            new = local_sweep(
                u[s, x], u[s, x - 1], u[s, x + 1], f[s, x], wx[x - 1], wx[x], wy[x], wz[x], gain[x]
            )
            u1[s, x] = new
            u1[s, x, 0:1, :] = (
                u1[s, x, 0:1, :] + gain[x, 0:1, :] * wyl[pl.ds(x, 1), :] * y_lo[pl.ds(8 * s + x, 1), :]
            )
            u1[s, x, 127:128, :] = (
                u1[s, x, 127:128, :] + gain[x, 127:128, :] * wyh[pl.ds(x, 1), :] * y_hi[pl.ds(8 * s + x, 1), :]
            )
        return carry

    lax.fori_loop(1, 7, first, 0)

    def second(x, carry):
        slabs = []
        for s in range(4):
            new = local_sweep(
                u1[s, x], u1[s, x - 1], u1[s, x + 1], f[s, x], wx[x - 1], wx[x], wy[x], wz[x], gain[x]
            )
            u2[s, x - 2] = new
            slabs.append(new)
        sums[x - 2] = row_sums(slabs)
        return carry

    lax.fori_loop(2, 6, second, 0)


def inner(u, f, c, cmap, admittance, y_lo, y_hi):
    outs = [
        kept(4, 8, 128, 256), kept(4, 4, 128, 256), kept(7, 128, 256), kept(8, 128, 256), kept(8, 128, 256),
        kept(8, 128, 256), kept(8, 256), kept(8, 256), kept(128, 128), kept(4, 4, 128),
    ]
    return pl.pallas_call(
        inner_kernel,
        in_specs=[hbm()] * 3 + [vmem()] * 4,
        out_specs=[vmem()] * len(outs),
        out_shape=outs,
        scratch_shapes=[
            pltpu.VMEM((4, 8, 128, 256), F32),
            pltpu.VMEM((4, 8, 128, 256), F32),
            pltpu.VMEM((8, 128, 256), F32),
            pltpu.SemaphoreType.DMA((3,)),
        ],
        compiler_params=params(),
        cost_estimate=pl.CostEstimate(flops=100_000_000, bytes_accessed=30_000_000, transcendentals=0),
        name="inner",
    )(u, f, c, cmap, admittance, y_lo, y_hi)


def outer_kernel(
    core, u_hbm, f_hbm, c_hbm, cmap, admittance, y_lo, y_hi, x_lo, x_hi, uh_lo, uh_hi,
    u1, wx, wy, wz, gain, wyl, wyh, sums,
    face_lo, face_hi, edge_lo, edge_hi, u2, gain_out, wxf, mine, other,
    u, f, c, ids, sems,
):
    copies = []
    for n, x in enumerate((0, 1, 6, 7)):
        copies.append(pltpu.make_async_copy(u_hbm.at[:, x], u.at[n], sems.at[0, n]))
        copies.append(pltpu.make_async_copy(f_hbm.at[:, x], f.at[n], sems.at[1, n]))
    for n, x in enumerate((0, 7)):
        copies.append(pltpu.make_async_copy(c_hbm.at[x], c.at[n], sems.at[2, n]))
    for copy in copies:
        copy.start()
    ids[0:8, :] = cmap[...]
    ids[8:16, :] = jnp.full((8, 128), 2048, jnp.int32)
    ids[8:9, :] = x_lo[258:259, 0:128].astype(jnp.int32)
    ids[9:10, :] = x_hi[258:259, 0:128].astype(jnp.int32)
    lanes = iota((1, 128), 1)
    low_ids = y_lo[48:49, 0:128].astype(jnp.int32)
    high_ids = pltpu.roll(y_hi[48:49, 0:128], 8, 1).astype(jnp.int32)
    ids[10:11, :] = jnp.where(lanes < 8, low_ids, jnp.where(lanes < 16, high_ids, 2048))
    table = admittance[...]
    zeta = gather_rows(ids[8:16, :], table)
    zeta_t = jnp.transpose(jnp.concatenate([zeta, jnp.zeros((120, 128), F32)], axis=0))
    for copy in copies:
        copy.wait()
    row = iota((128, 256), 0)

    pushed = []
    for n, (x, msg, halo, inside, out) in enumerate(
        ((0, x_lo, uh_lo, 1, face_lo), (7, x_hi, uh_hi, 2, face_hi))
    ):
        here = c[n]
        there = msg[0:128, :]
        outside = face(here, there)
        wxf[n] = outside
        g = OMEGA / (gain[x] + outside)
        gain_out[n] = g
        for s in range(4):
            new = local_sweep(
                u[3 * n, s], halo[s], u[inside, s], f[3 * n, s], outside, wx[0 if n == 0 else 6], wy[x], wz[x], g
            )
            out[s] = new
            out[s, 0:1, :] = out[s, 0:1, :] + g[0:1] * wyl[x : x + 1, :] * y_lo[8 * s + x : 8 * s + x + 1, :]
            out[s, 127:128, :] = (
                out[s, 127:128, :] + g[127:128] * wyh[x : x + 1, :] * y_hi[8 * s + x : 8 * s + x + 1, :]
            )
        beyond = face(there, msg[128:256, :])
        along_y = line_weight(there, 0)
        diag = both_sides(along_y, 0) + both_sides(line_weight(there, 1), 1) + zeta_t[:, n : n + 1]
        diag = diag + outside + beyond
        diag = diag + jnp.where(row == 0, face(there[0:1], msg[256:257, :]), 0.0)
        diag = diag + jnp.where(row == 127, face(there[127:128], msg[257:258, :]), 0.0)
        factor = OMEGA * outside / jnp.maximum(diag, TINY)
        pushed.append(row_sums([factor * out[s] for s in range(4)]))

    edge_sums = jnp.zeros((4, 128), F32)
    for n, (msg, own, ext, edge, y) in enumerate(
        ((y_lo, wyl, 256, edge_lo, 0), (y_hi, wyh, 257, edge_hi, 127))
    ):
        for s in range(4):
            edge[8 * s : 8 * s + 1, :] = face_lo[s, y : y + 1, :]
            for x in range(1, 7):
                edge[8 * s + x : 8 * s + x + 1, :] = u1[s, x, y : y + 1, :]
            edge[8 * s + 7 : 8 * s + 8, :] = face_hi[s, y : y + 1, :]
        there = msg[32:40, :]
        beyond = face(there, msg[40:48, :])
        along_x = line_weight(there, 0)
        x_rows = iota((8, 256), 0)
        diag = both_sides(along_x, 0) + both_sides(line_weight(there, 1), 1) + own[...] + beyond
        diag = diag + jnp.where(x_rows == 0, face(there[0:1], x_lo[ext : ext + 1, :]), 0.0)
        diag = diag + jnp.where(x_rows == 7, face(there[7:8], x_hi[ext : ext + 1, :]), 0.0)
        diag = diag + zeta_t[8 * n : 8 * n + 8, 2:3]
        factor = OMEGA * own[...] / jnp.maximum(diag, TINY)
        lined = []
        for s in range(4):
            line = to_lanes(jnp.sum(factor * edge[8 * s : 8 * s + 8, :], axis=1, keepdims=True))
            lined.append(pltpu.roll(line, 8 * n, 1) if n else line)
        edge_sums = edge_sums + jnp.concatenate(lined, axis=0)

    own_sums = {}
    for n, (x, below, at, above, w_below, w_above, g) in enumerate(
        (
            (0, None, lambda s: face_lo[s], lambda s: u1[s, 1], None, 0, gain_out[0]),
            (1, lambda s: face_lo[s], lambda s: u1[s, 1], lambda s: u1[s, 2], 0, 1, gain[1]),
            (6, lambda s: u1[s, 5], lambda s: u1[s, 6], lambda s: face_hi[s], 5, 6, gain[6]),
            (7, lambda s: u1[s, 6], lambda s: face_hi[s], None, 6, None, gain_out[1]),
        )
    ):
        slabs = []
        for s in range(4):
            new = local_sweep(
                at(s),
                None if below is None else below(s),
                None if above is None else above(s),
                f[n, s],
                None if below is None else wx[w_below],
                None if above is None else wx[w_above],
                wy[x],
                wz[x],
                g,
            )
            u2[s, n] = new
            slabs.append(new)
        own_sums[x] = row_sums(slabs)
    for x in range(2, 6):
        own_sums[x] = sums[x - 2]
    rows = [own_sums[x] for x in range(8)] + pushed + [edge_sums]

    place = iota((64, 128), 0)
    block_of = 4 * ((place // 8) % 4) + 2 * (place // 32) + (place // 4) % 2
    total = jnp.zeros((192, 128), F32)
    for k, values in enumerate(rows):
        id_row = ids[k : k + 1, :]
        hit = lax.shift_right_logical(id_row, 7) == block_of
        spread = jnp.where(hit, jnp.concatenate([values] * 16, axis=0), 0.0)
        lane_hit = lax.bitwise_and(id_row, 127) == iota((128, 128), 0)
        onehot = jnp.where(lane_hit, 1.0, 0.0).astype(jnp.bfloat16)
        a = spread.astype(jnp.bfloat16)
        spread = spread - a.astype(F32)
        b = spread.astype(jnp.bfloat16)
        spread = spread - b.astype(F32)
        parts = jnp.concatenate([a, b, spread.astype(jnp.bfloat16)], axis=0)
        total = total + lax.dot_general(parts, onehot, NT, preferred_element_type=F32)
    contact = (total[0:64] + total[64:128] + total[128:192]) * (1.0 / 256.0)
    first_half = core[0] == 0
    mine[...] = jnp.where(first_half, contact[0:32], contact[32:64])
    other[...] = jnp.where(first_half, contact[32:64], contact[0:32])


def outer(core, u, f, c, cmap, admittance, y_lo, y_hi, x_lo, x_hi, uh_lo, uh_hi, u1, wx, wy, wz, gain, wyl, wyh, sums):
    outs = [
        kept(4, 128, 256), kept(4, 128, 256), kept(32, 256), kept(32, 256),
        kept(4, 4, 128, 256), kept(2, 128, 256), kept(2, 128, 256), f32(32, 128), f32(32, 128),
    ]
    return pl.pallas_call(
        outer_kernel,
        in_specs=[smem()] + [hbm()] * 3 + [vmem()] * 16,
        out_specs=[vmem()] * len(outs),
        out_shape=outs,
        scratch_shapes=[
            pltpu.VMEM((4, 4, 128, 256), F32),
            pltpu.VMEM((4, 4, 128, 256), F32),
            pltpu.VMEM((2, 128, 256), F32),
            pltpu.VMEM((16, 128), jnp.int32),
            pltpu.SemaphoreType.DMA((3, 4)),
        ],
        compiler_params=params(),
        cost_estimate=pl.CostEstimate(flops=50_000_000, bytes_accessed=15_000_000, transcendentals=0),
        name="outer",
    )(core, u, f, c, cmap, admittance, y_lo, y_hi, x_lo, x_hi, uh_lo, uh_hi, u1, wx, wy, wz, gain, wyl, wyh, sums)


def spread_kernel(mine, got, out):
    both = mine[...] + got[...]
    for n in range(out.shape[0]):
        out[n] = both


def spread(mine, got, count):
    return pl.pallas_call(
        spread_kernel,
        in_specs=[vmem()] * 2,
        out_specs=vmem(),
        out_shape=f32(count, 32, 128),
        compiler_params=params(),
        name="spread",
    )(mine, got)


def gathered_kernel(parts, out):
    out[...] = jnp.sum(parts[...], axis=0)


def gathered(parts):
    return pl.pallas_call(
        gathered_kernel,
        in_specs=[vmem()],
        out_specs=vmem(),
        out_shape=f32(32, 128),
        compiler_params=params(),
        name="gathered",
    )(parts)


def blocks_kernel(place, pairs, amplitudes, a0, a1, a2, a3, i0, i1, i2, i3, out, charges):
    core, elec = place[0], place[1]
    row = iota((32, 128), 0)
    electrode = (4 * (row // 8) + 2 * core + (row // 4) % 2) * 128 + iota((32, 128), 1)
    total = a0[...] + a1[...] + a2[...] + a3[...]
    for s in range(4):
        at = row % 4 == s
        amount = amplitudes[s]
        total = total + jnp.where(at & (electrode == pairs[s, 0]), amount, 0.0)
        total = total - jnp.where(at & (electrode == pairs[s, 1]), amount, 0.0)
    for e in range(4):
        charges[e] = total[8 * e : 8 * e + 8]
    upper = iota((8, 128), 0) < 4
    for turn, blocks in ((0, i0), (3, i1), (1, i2), (2, i3)):
        e = lax.rem(elec + turn, 4)
        charge = charges[e]
        first = lax.dot_general(charge, blocks[0], NT, precision=EXACT, preferred_element_type=F32)
        second = lax.dot_general(charge, blocks[1], NT, precision=EXACT, preferred_element_type=F32)
        out[e] = jnp.where(upper, first, second)


def blocks(place, pairs, amplitudes, parts, impedances):
    return pl.pallas_call(
        blocks_kernel,
        in_specs=[smem()] * 3 + [vmem()] * 8,
        out_specs=vmem(),
        out_shape=f32(4, 8, 128),
        scratch_shapes=[pltpu.VMEM((4, 8, 128), F32)],
        compiler_params=params(),
        name="blocks",
    )(place, pairs, amplitudes, *parts, *impedances)


def correct_kernel(
    place, cmap, own, got, u2a, u2b, gain, gain_b, wxf, wyl, wyh, zeta_t, uh_lo, uh_hi, e_lo, e_hi,
    out_hbm, volts, table, buf, sems,
):
    core, elec = place[0], place[1]
    table[core] = own[...]
    table[1 - core] = got[...]
    for h in range(2):
        for j in range(2):
            volts[:, 128 * (2 * h + j) : 128 * (2 * h + j) + 128] = table[h, elec, 4 * j : 4 * j + 4, :]
    ids = cmap[...]
    block = lax.shift_right_logical(ids, 7)
    lane = lax.bitwise_and(ids, 127)
    touched = []
    for s in range(4):
        found = jnp.zeros((8, 128), F32)
        for b in range(16):
            e, h, j = b // 4, (b // 2) % 2, b % 2
            row = jnp.broadcast_to(table[h, e, 4 * j + s : 4 * j + s + 1, :], (8, 128))
            found = jnp.where(block == b, jnp.take_along_axis(row, lane, axis=1), found)
        touched.append(found)
    stacked = jnp.concatenate(touched + [jnp.zeros((96, 128), F32)], axis=0)
    volts_t = jnp.transpose(stacked)
    copies = []
    for x in (2, 3, 4, 5, 1, 6, 0, 7):
        if x in (0, 7):
            g = gain_b[x // 7]
        else:
            g = gain[x]
        pull = (1.0 / OMEGA) * zeta_t[:, x : x + 1] * g
        for s in range(4):
            if 2 <= x <= 5:
                u = u2a[s, x - 2]
            else:
                u = u2b[s, {0: 0, 1: 1, 6: 2, 7: 3}[x]]
            if x == 0:
                u = u + g * wxf[0] * uh_lo[s]
            if x == 7:
                u = u + g * wxf[1] * uh_hi[s]
            buf[s, x] = u
            buf[s, x, 0:1, :] = u[0:1] + g[0:1] * wyl[x : x + 1, :] * e_lo[8 * s + x : 8 * s + x + 1, :]
            buf[s, x, 127:128, :] = u[127:128] + g[127:128] * wyh[x : x + 1, :] * e_hi[8 * s + x : 8 * s + x + 1, :]
            u = buf[s, x]
            buf[s, x] = u + pull * (volts_t[:, 8 * s + x : 8 * s + x + 1] - u)
        copy = pltpu.make_async_copy(buf.at[:, x], out_hbm.at[:, x], sems.at[x])
        copy.start()
        copies.append(copy)
    for copy in copies:
        copy.wait()


def correct(place, cmap, own, got, u2a, u2b, gain, gain_b, wxf, wyl, wyh, zeta_t, uh_lo, uh_hi, e_lo, e_hi):
    return pl.pallas_call(
        correct_kernel,
        in_specs=[smem()] + [vmem()] * 15,
        out_specs=[hbm(), vmem()],
        out_shape=[f32(4, 8, 128, 256), f32(4, 512)],
        scratch_shapes=[
            pltpu.VMEM((2, 4, 8, 128), F32),
            pltpu.VMEM((4, 8, 128, 256), F32),
            pltpu.SemaphoreType.DMA((8,)),
        ],
        compiler_params=params(),
        name="correct",
    )(place, cmap, own, got, u2a, u2b, gain, gain_b, wxf, wyl, wyh, zeta_t, uh_lo, uh_hi, e_lo, e_hi)


def per_device(u, f, c, cmap, admittance, impedance, pairs, amplitudes):
    tiles = lax.axis_size(TILE)
    groups = lax.axis_size("zx")
    elecs = lax.axis_size("elec")
    core = lax.axis_index("core")
    elec = lax.axis_index("elec")
    place = jnp.stack([core, elec]).astype(jnp.int32)
    admittance = admittance.reshape(16, 128)

    def from_below(a, axis, count):
        return lax.ppermute(a, axis, [(i, i + 1) for i in range(count - 1)])

    def from_above(a, axis, count):
        return lax.ppermute(a, axis, [(i + 1, i) for i in range(count - 1)])

    def rotated(a, turn):
        return lax.ppermute(a, "elec", [(i, (i + turn) % elecs) for i in range(elecs)])

    def swapped(a):
        return lax.ppermute(a, "core", [(0, 1), (1, 0)])

    def around(a):
        return [a, rotated(a, 1), rotated(a, elecs - 1), rotated(a, 2)]

    own_lo, own_hi = edges(u, c, cmap)
    y_lo = from_below(own_hi, "elec", elecs)
    y_hi = from_above(own_lo, "elec", elecs)
    uh_lo = from_below(u[:, 7], TILE, tiles)
    uh_hi = from_above(u[:, 0], TILE, tiles)
    down, up = faces(c, cmap, y_lo, y_hi)
    x_lo = from_below(up, TILE, tiles)
    x_hi = from_above(down, TILE, tiles)
    impedances = around(lax.dynamic_slice_in_dim(impedance, 2 * core, 2, axis=0))

    u1, u2a, wx, wy, wz, gain, wyl, wyh, zeta_t, sums = inner(u, f, c, cmap, admittance, y_lo, y_hi)
    face_lo, face_hi, edge_lo, edge_hi, u2b, gain_b, wxf, mine, other = outer(
        place, u, f, c, cmap, admittance, y_lo, y_hi, x_lo, x_hi, uh_lo, uh_hi,
        u1, wx, wy, wz, gain, wyl, wyh, sums,
    )
    parts = spread(mine, swapped(other), groups)
    parts = lax.all_to_all(parts, "zx", 0, 0, tiled=True)
    summed = gathered(parts)
    h_lo = from_below(face_hi, TILE, tiles)
    h_hi = from_above(face_lo, TILE, tiles)
    e_lo = from_below(edge_hi, "elec", elecs)
    e_hi = from_above(edge_lo, "elec", elecs)
    own = blocks(place, pairs, amplitudes, around(summed), impedances)
    got = swapped(own)
    out, volts = correct(
        place, cmap, own, got, u2a, u2b, gain, gain_b, wxf, wyl, wyh, zeta_t, h_lo, h_hi, e_lo, e_hi
    )
    return out, volts


def solution(mesh):
    tile, src, elec = mesh.devices.shape
    cut = Mesh(mesh.devices.reshape(tile // 2, 2, src, elec), ("zx", "core", "src", "elec"))
    placed = (
        P("src", TILE, "elec", None),
        P("src", TILE, "elec", None),
        P(TILE, "elec", None),
        P(TILE, "elec"),
        P(),
        P("elec", None, None),
        P("src", None),
        P("src"),
    )
    return jax.shard_map(
        per_device,
        mesh=cut,
        in_specs=placed,
        out_specs=(P("src", TILE, "elec", None), P("src", "elec")),
        check_vma=False,
    )
```

```python
import jax
import jax.numpy as jnp
from jax import lax
from jax.experimental import pallas as pl
from jax.experimental.pallas import tpu as pltpu
from jax.sharding import Mesh
from jax.sharding import PartitionSpec as P

OMEGA = 0.8
KEEP = 1.0 - OMEGA
TINY = 1e-30
F32 = jnp.float32
EXACT = lax.Precision.HIGHEST
MIB = 1024 * 1024
TILE = ("zx", "core")

NT = (((1,), (1,)), ((), ()))


def params(mib):
    return pltpu.CompilerParams(vmem_limit_bytes=mib * MIB)


def vmem():
    return pl.BlockSpec(memory_space=pltpu.VMEM)


def hbm():
    return pl.BlockSpec(memory_space=pltpu.HBM)


def f32(*shape):
    return jax.ShapeDtypeStruct(shape, F32)


def kept(*shape):
    return pltpu.VMEM(shape, F32)


def stored(*shape):
    return pltpu.HBM(shape, F32)


def in_hbm(a):
    return pltpu.with_memory_space_constraint(a, pltpu.HBM)


def inverse(a):
    r = pl.reciprocal(a, approx=True)
    return r * (2.0 - a * r)


def face(a, b):
    return (2.0 * a * b) * inverse(a + b)


def outer_face(a, b):
    return (2.0 * a * b) * inverse(jnp.maximum(a + b, TINY))


def iota(shape, dim):
    return lax.broadcasted_iota(jnp.int32, shape, dim)


def shift_up(a, axis):
    return pltpu.roll(a, a.shape[axis] - 1, axis)


def shift_down(a, axis):
    return pltpu.roll(a, 1, axis)


def in_line(flux_weight, u, axis):
    return flux_weight * shift_up(u, axis) + shift_down(flux_weight * u, axis)


def line_weight(c, axis):
    w = face(c, shift_up(c, axis))
    return jnp.where(iota(c.shape, axis) < c.shape[axis] - 1, w, 0.0)


def both_sides(w, axis):
    return w + shift_down(w, axis)


def row_sums(slabs):
    folded = jnp.concatenate([p[:, :128] + p[:, 128:] for p in slabs], axis=0)
    head = folded.astype(jnp.bfloat16)
    rest = (folded - head.astype(F32)).astype(jnp.bfloat16)
    ones = jnp.ones((8, 128), jnp.bfloat16)
    total = lax.dot_general(ones, head, NT, preferred_element_type=F32)
    total = total + lax.dot_general(ones, rest, NT, preferred_element_type=F32)
    return jnp.concatenate([total[0:1, 128 * s : 128 * s + 128] for s in range(4)], axis=0)


def to_lanes(column):
    mask = iota((8, 128), 0) == iota((8, 128), 1)
    return jnp.sum(jnp.where(mask, column, jnp.zeros_like(column)), axis=0, keepdims=True)


def gather_rows(ids, table):
    block = lax.shift_right_logical(ids, 7)
    lane = lax.bitwise_and(ids, 127)
    found = jnp.zeros(ids.shape, F32)
    for b in range(16):
        row = jnp.broadcast_to(table[b : b + 1], ids.shape)
        got = jnp.take_along_axis(row, lane, axis=1)
        found = jnp.where(block == b, got, found)
    return found


def scatter(id_rows, values):
    place = iota((64, 128), 0)
    block_of = 4 * ((place // 8) % 4) + 2 * (place // 32) + (place // 4) % 2
    total = jnp.zeros((192, 128), F32)
    for id_row, value in zip(id_rows, values):
        hit = lax.shift_right_logical(id_row, 7) == block_of
        spread = jnp.where(hit, jnp.concatenate([value] * 16, axis=0), 0.0)
        lane_hit = lax.bitwise_and(id_row, 127) == iota((128, 128), 0)
        onehot = jnp.where(lane_hit, 1.0, 0.0).astype(jnp.bfloat16)
        a = spread.astype(jnp.bfloat16)
        spread = spread - a.astype(F32)
        b = spread.astype(jnp.bfloat16)
        spread = spread - b.astype(F32)
        parts = jnp.concatenate([a, b, spread.astype(jnp.bfloat16)], axis=0)
        total = total + lax.dot_general(parts, onehot, NT, preferred_element_type=F32)
    return total[0:64] + total[64:128] + total[128:192]


ROW_C = 512
ROW_C2 = 640
ROW_MAP = 768
ROWS = 776


def sides():
    core = lax.axis_index("core")
    return 1 - core, core


def edges_kernel(
    u_hbm, c_hbm, imp_hbm, cmap_hbm, out_lo, out_hi, near_out, far_out, blocks, u, c, cmap, imp, sems, whole_sems
):
    core = lax.axis_index("core")
    copies = [pltpu.make_async_copy(cmap_hbm, cmap, sems.at[4])]
    for n, y in enumerate((0, 120)):
        copies.append(pltpu.make_async_copy(u_hbm.at[:, :, pl.ds(y, 8)], u.at[n], sems.at[2 * n]))
        copies.append(pltpu.make_async_copy(c_hbm.at[:, pl.ds(y, 8)], c.at[n], sems.at[2 * n + 1]))
    whole = []
    for n, (out, side) in enumerate(zip((near_out, far_out), sides())):
        for s in range(4):
            whole.append((u_hbm.at[s, 7 * side], out.at[pl.ds(128 * s, 128)], whole_sems.at[n, s]))
        whole.append((c_hbm.at[7 * side], out.at[pl.ds(ROW_C, 128)], whole_sems.at[n, 4]))
        whole.append((c_hbm.at[1 + 5 * side], out.at[pl.ds(ROW_C2, 128)], whole_sems.at[n, 5]))
    whole.append((imp_hbm.at[2 * core], imp.at[0], whole_sems.at[0, 7]))
    whole.append((imp_hbm.at[2 * core + 1], imp.at[1], whole_sems.at[1, 7]))
    whole = [pltpu.make_async_copy(*copy) for copy in whole]
    for copy in copies + whole:
        copy.start()
    for copy in copies:
        copy.wait()
    for n, out, near, far, lane in ((0, out_lo, 0, 1, 0), (1, out_hi, 7, 6, 127)):
        for x in range(8):
            for s in range(4):
                out[8 * s + x : 8 * s + x + 1, :] = u[n, s, x, near : near + 1, :]
            out[32 + x : 33 + x, :] = c[n, x, near : near + 1, :]
            out[40 + x : 41 + x, :] = c[n, x, far : far + 1, :]
        out[48:56, :] = jnp.zeros((8, 256), F32)
        out[48:49, 0:128] = to_lanes(cmap[:, lane : lane + 1].astype(F32))
    for out, side in zip((near_out, far_out), sides()):
        out[ROW_MAP:ROWS, :] = jnp.zeros((8, 256), F32)
        out[ROW_MAP : ROW_MAP + 1, 0:128] = cmap[pl.ds(7 * side, 1), :].astype(F32)
    for copy in whole:
        copy.wait()
    blocks[:, 0:128] = imp[0]
    blocks[:, 128:256] = imp[1]


def edges(u, c, impedance, cmap):
    return pl.pallas_call(
        edges_kernel,
        in_specs=[hbm()] * 4,
        out_specs=[vmem()] * 5,
        out_shape=[f32(56, 256), f32(56, 256), f32(ROWS, 256), f32(ROWS, 256), f32(128, 256)],
        scratch_shapes=[
            pltpu.VMEM((2, 4, 8, 8, 256), F32),
            pltpu.VMEM((2, 8, 8, 256), F32),
            pltpu.VMEM((8, 128), jnp.int32),
            pltpu.VMEM((2, 128, 128), F32),
            pltpu.SemaphoreType.DMA((5,)),
            pltpu.SemaphoreType.DMA((2, 8)),
        ],
        compiler_params=params(4),
        name="edges",
    )(u, c, impedance, cmap)


def corners_kernel(y_lo, y_hi, near_out, far_out):
    for out, side in zip((near_out, far_out), sides()):
        out[...] = jnp.zeros((8, 256), F32)
        out[0:1, :] = y_lo[pl.ds(32 + 7 * side, 1), :]
        out[1:2, :] = y_hi[pl.ds(32 + 7 * side, 1), :]


def corners(y_lo, y_hi):
    return pl.pallas_call(
        corners_kernel,
        in_specs=[vmem()] * 2,
        out_specs=[vmem()] * 2,
        out_shape=[f32(8, 256)] * 2,
        compiler_params=params(2),
        name="corners",
    )(y_lo, y_hi)


def weights_kernel(u_hbm, f_hbm, c_hbm, cmap, admittance, u, f, wx, wy, wz, diag, zeta_t, c, sems):
    copy = pltpu.make_async_copy(c_hbm, c, sems.at[0])
    later = [pltpu.make_async_copy(u_hbm, u, sems.at[1]), pltpu.make_async_copy(f_hbm, f, sems.at[2])]
    copy.start()
    for other in later:
        other.start()
    zeta = gather_rows(cmap[...], admittance[...])
    zeta_t[...] = jnp.transpose(jnp.concatenate([zeta, jnp.zeros((120, 128), F32)], axis=0))
    copy.wait()
    for x in range(8):
        here = c[x]
        if x < 7:
            wx[x] = face(here, c[x + 1])
        along_y = line_weight(here, 0)
        along_z = line_weight(here, 1)
        wy[x] = along_y
        wz[x] = along_z
        total = both_sides(along_y, 0) + both_sides(along_z, 1) + zeta_t[:, x : x + 1]
        if x > 0:
            total = total + wx[x - 1]
        if x < 7:
            total = total + wx[x]
        diag[x] = total
    for other in later:
        other.wait()


def weights(u, f, c, cmap, admittance):
    outs = [
        kept(4, 8, 128, 256), kept(4, 8, 128, 256),
        kept(7, 128, 256), kept(8, 128, 256), kept(8, 128, 256), kept(8, 128, 256), kept(128, 128),
    ]
    return pl.pallas_call(
        weights_kernel,
        in_specs=[hbm()] * 3 + [vmem()] * 2,
        out_specs=[vmem()] * len(outs),
        out_shape=outs,
        scratch_shapes=[pltpu.VMEM((8, 128, 256), F32), pltpu.SemaphoreType.DMA((3,))],
        compiler_params=params(8),
        cost_estimate=pl.CostEstimate(flops=20_000_000, bytes_accessed=6_000_000, transcendentals=0),
        name="weights",
    )(u, f, c, cmap, admittance)


def inner_kernel(
    u, f, cmap, own_lo, own_hi, y_lo, y_hi, wx, wy, wz, diag,
    u2, gain, wyl, wyh, pulled1, keep1, pulled2, edge_lo, edge_hi, contact,
    u1, sums,
):
    wyl[...] = outer_face(own_lo[32:40, :], y_lo[32:40, :])
    wyh[...] = outer_face(own_hi[32:40, :], y_hi[32:40, :])
    for x in range(8):
        gain[x] = diag[x]
        gain[x, 0:1, :] = gain[x, 0:1, :] + wyl[x : x + 1, :]
        gain[x, 127:128, :] = gain[x, 127:128, :] + wyh[x : x + 1, :]
        if x not in (0, 7):
            gain[x] = OMEGA * inverse(gain[x])

    for n, x in enumerate((0, 7)):
        for s in range(4):
            pulled = f[s, x] + in_line(wy[x], u[s, x], 0)
            pulled = pulled + in_line(wz[x], u[s, x], 1)
            pulled = pulled + (wx[0] * u[s, 1] if x == 0 else wx[6] * u[s, 6])
            pulled1[n, s] = pulled
            pulled1[n, s, 0:1, :] = pulled1[n, s, 0:1, :] + wyl[x : x + 1, :] * y_lo[8 * s + x : 8 * s + x + 1, :]
            pulled1[n, s, 127:128, :] = (
                pulled1[n, s, 127:128, :] + wyh[x : x + 1, :] * y_hi[8 * s + x : 8 * s + x + 1, :]
            )
            keep1[n, s] = KEEP * u[s, x]

    def first(x, carry):
        for s in range(4):
            pulled = f[s, x] + in_line(wy[x], u[s, x], 0)
            pulled = pulled + in_line(wz[x], u[s, x], 1)
            pulled = pulled + wx[x - 1] * u[s, x - 1] + wx[x] * u[s, x + 1]
            u1[s, x] = KEEP * u[s, x] + gain[x] * pulled
            low = u1[s, x, 0:1, :] + gain[x, 0:1, :] * wyl[pl.ds(x, 1), :] * y_lo[pl.ds(8 * s + x, 1), :]
            high = u1[s, x, 127:128, :] + gain[x, 127:128, :] * wyh[pl.ds(x, 1), :] * y_hi[pl.ds(8 * s + x, 1), :]
            u1[s, x, 0:1, :] = low
            u1[s, x, 127:128, :] = high
            edge_lo[pl.ds(8 * s + x, 1), :] = low
            edge_hi[pl.ds(8 * s + x, 1), :] = high
        return carry

    lax.fori_loop(1, 7, first, 0)

    for s in range(4):
        pulled2[0, s] = f[s, 0] + wx[0] * u1[s, 1]
        pulled2[1, s] = f[s, 7] + wx[6] * u1[s, 6]
        u1[s, 0] = jnp.zeros((128, 256), F32)
        u1[s, 7] = jnp.zeros((128, 256), F32)

    def second(x, carry):
        slabs = []
        for s in range(4):
            pulled = f[s, x] + in_line(wy[x], u1[s, x], 0)
            pulled = pulled + in_line(wz[x], u1[s, x], 1)
            pulled = pulled + wx[x - 1] * u1[s, x - 1] + wx[x] * u1[s, x + 1]
            new = KEEP * u1[s, x] + gain[x] * pulled
            u2[s, x - 1] = new
            slabs.append(new)
        sums[x] = row_sums(slabs)
        return carry

    lax.fori_loop(1, 7, second, 0)
    contact[...] = scatter([cmap[x : x + 1, :] for x in range(1, 7)], [sums[x] for x in range(1, 7)])


def inner(u, f, cmap, own_lo, own_hi, y_lo, y_hi, wx, wy, wz, diag):
    outs = [
        kept(4, 6, 128, 256), kept(8, 128, 256), kept(8, 256), kept(8, 256),
        kept(2, 4, 128, 256), kept(2, 4, 128, 256), kept(2, 4, 128, 256),
        kept(32, 256), kept(32, 256), kept(64, 128),
    ]
    return pl.pallas_call(
        inner_kernel,
        in_specs=[vmem()] * 11,
        out_specs=[vmem()] * len(outs),
        out_shape=outs,
        scratch_shapes=[
            pltpu.VMEM((4, 8, 128, 256), F32),
            pltpu.VMEM((8, 4, 128), F32),
        ],
        compiler_params=params(12),
        cost_estimate=pl.CostEstimate(flops=100_000_000, bytes_accessed=25_000_000, transcendentals=0),
        name="inner",
    )(u, f, cmap, own_lo, own_hi, y_lo, y_hi, wx, wy, wz, diag)


def outer_kernel(
    pairs, amplitudes, cmap, admittance, blocks, near, far, y_lo, y_hi, x_near, x_far, ends_near, ends_far,
    wx, wy, wz, gain, wyl, wyh, u2, pulled1, keep1, pulled2, e_lo, e_hi, contact, zeta_in,
    face_near_out, face_far_out, edge_lo_out, edge_hi_out, u2_out, gain_out, wxf_out, misc_out, zeta_out, mine, other,
    ids, face_near, face_far, edge_lo, edge_hi, u2b, gain_b, wxf, misc, c_own, sems, u2_sems,
):
    copies = []
    rows_in = [
        pltpu.make_async_copy(source.at[pl.ds(ROW_C, 128)], c_own.at[n], sems.at[11 + n])
        for n, source in enumerate((near, far))
    ]
    for copy in rows_in:
        copy.start()

    def send(source, target, sem):
        copy = pltpu.make_async_copy(source, target, sem)
        copy.start()
        copies.append(copy)

    send(gain.at[pl.ds(1, 6)], gain_out.at[pl.ds(1, 6)], sems.at[0])
    send(zeta_in, zeta_out, sems.at[1])
    send(u2.at[:, pl.ds(1, 4)], u2_out.at[:, pl.ds(2, 4)], sems.at[2])
    misc[0:8, :] = wyl[...]
    misc[8:16, :] = wyh[...]
    send(misc, misc_out, sems.at[3])
    ids[0:8, :] = jnp.full((8, 128), 2048, jnp.int32)
    ids[0:1, :] = x_near[ROW_MAP : ROW_MAP + 1, 0:128].astype(jnp.int32)
    ids[1:2, :] = x_far[ROW_MAP : ROW_MAP + 1, 0:128].astype(jnp.int32)
    lanes = iota((1, 128), 1)
    low_ids = y_lo[48:49, 0:128].astype(jnp.int32)
    high_ids = pltpu.roll(y_hi[48:49, 0:128], 8, 1).astype(jnp.int32)
    ids[2:3, :] = jnp.where(lanes < 8, low_ids, jnp.where(lanes < 16, high_ids, 2048))
    zeta = gather_rows(ids[...], admittance[...])
    zeta_t = jnp.transpose(jnp.concatenate([zeta, jnp.zeros((120, 128), F32)], axis=0))
    row = iota((128, 256), 0)

    id_rows = []
    values = []
    for copy in rows_in:
        copy.wait()
    for n, (side, msg, ends, out, sent) in enumerate(
        zip(sides(), (x_near, x_far), (ends_near, ends_far), (face_near, face_far), (face_near_out, face_far_out))
    ):
        x = 7 * side
        there = msg[ROW_C : ROW_C + 128, :]
        outside = outer_face(c_own[n], there)
        wxf[n] = outside
        g = OMEGA * inverse(gain[x] + outside)
        gain_b[n] = g
        for s in range(4):
            out[s] = keep1[side, s] + g * (pulled1[side, s] + outside * msg[128 * s : 128 * s + 128, :])
        send(out, sent, sems.at[4 + n])
        send(gain_b.at[n], gain_out.at[x], sems.at[6 + n])
        spare = jnp.maximum(there, TINY)
        diag = both_sides(line_weight(spare, 0), 0) + both_sides(line_weight(spare, 1), 1) + zeta_t[:, n : n + 1]
        diag = diag + outside + outer_face(there, msg[ROW_C2 : ROW_C2 + 128, :])
        diag = diag + jnp.where(row == 0, outer_face(there[0:1], ends[0:1, :]), 0.0)
        diag = diag + jnp.where(row == 127, outer_face(there[127:128], ends[1:2, :]), 0.0)
        factor = OMEGA * outside * inverse(jnp.maximum(diag, TINY))
        id_rows.append(ids[n : n + 1, :])
        values.append(row_sums([factor * out[s] for s in range(4)]))
        inside = 1 + 5 * side
        factor = gain[inside] * wx[6 * side]
        slabs = []
        for s in range(4):
            new = factor * out[s]
            u2b[2 * n + 1, s] = u2[s, 5 * side] + new
            slabs.append(new)
        send(u2b.at[2 * n + 1], u2_out.at[:, inside], u2_sems.at[2 * n + 1])
        id_rows.append(cmap[pl.ds(inside, 1), :])
        values.append(row_sums(slabs))
        slabs = []
        for s in range(4):
            pulled = pulled2[side, s] + in_line(wy[x], out[s], 0)
            pulled = pulled + in_line(wz[x], out[s], 1)
            new = KEEP * out[s] + g * pulled
            u2b[2 * n, s] = new
            slabs.append(new)
        send(u2b.at[2 * n], u2_out.at[:, x], u2_sems.at[2 * n])
        id_rows.append(cmap[pl.ds(x, 1), :])
        values.append(row_sums(slabs))

    send(wxf, wxf_out, sems.at[8])

    edge_sums = jnp.zeros((4, 128), F32)
    for n, (msg, own, inside, edge, y, sent) in enumerate(
        ((y_lo, wyl, e_lo, edge_lo, 0, edge_lo_out), (y_hi, wyh, e_hi, edge_hi, 127, edge_hi_out))
    ):
        edge[0:32, :] = inside[...]
        for s in range(4):
            for side, out in zip(sides(), (face_near, face_far)):
                edge[pl.ds(8 * s + 7 * side, 1), :] = out[s, y : y + 1, :]
        edge[32:160, :] = blocks[...]
        send(edge, sent, sems.at[9 + n])
        there = msg[32:40, :]
        x_rows = iota((8, 256), 0)
        spare = jnp.maximum(there, TINY)
        diag = both_sides(line_weight(spare, 0), 0) + both_sides(line_weight(spare, 1), 1) + own[...]
        diag = diag + outer_face(there, msg[40:48, :])
        for side, ends in zip(sides(), (ends_near, ends_far)):
            diag = diag + jnp.where(x_rows == 7 * side, outer_face(there, ends[n : n + 1, :]), 0.0)
        diag = diag + zeta_t[8 * n : 8 * n + 8, 2:3]
        factor = OMEGA * own[...] * inverse(jnp.maximum(diag, TINY))
        lined = []
        for s in range(4):
            line = to_lanes(jnp.sum(factor * edge[8 * s : 8 * s + 8, :], axis=1, keepdims=True))
            lined.append(pltpu.roll(line, 8 * n, 1) if n else line)
        edge_sums = edge_sums + jnp.concatenate(lined, axis=0)
    id_rows.append(ids[2:3, :])
    values.append(edge_sums)

    total = (contact[...] + scatter(id_rows, values)) * (1.0 / 256.0)
    place = iota((64, 128), 0)
    electrode = (4 * ((place // 8) % 4) + 2 * (place // 32) + (place // 4) % 2) * 128 + iota((64, 128), 1)
    adds = jnp.logical_and(lax.axis_index("zx") == 0, lax.axis_index("elec") == 0)
    adds = jnp.logical_and(adds, lax.axis_index("core") == 0)
    for s in range(4):
        at = place % 4 == s
        amount = jnp.where(adds, amplitudes[s], 0.0)
        total = total + jnp.where(at & (electrode == pairs[2 * s]), amount, 0.0)
        total = total - jnp.where(at & (electrode == pairs[2 * s + 1]), amount, 0.0)
    first_half = lax.axis_index("core") == 0
    mine[...] = jnp.where(first_half, total[0:32], total[32:64])
    other[...] = jnp.where(first_half, total[32:64], total[0:32])
    for copy in copies:
        copy.wait()


def outer(pairs, amplitudes, *args):
    outs = [
        stored(4, 128, 256), stored(4, 128, 256), stored(160, 256), stored(160, 256),
        stored(4, 8, 128, 256), stored(8, 128, 256), stored(2, 128, 256), stored(16, 256), stored(128, 128),
        f32(32, 128), f32(32, 128),
    ]
    specs = [vmem()] * len(args)
    specs[3] = specs[4] = hbm()
    return pl.pallas_call(
        outer_kernel,
        in_specs=[pl.BlockSpec(memory_space=pltpu.SMEM)] * 2 + specs,
        out_specs=[hbm()] * 9 + [vmem()] * 2,
        out_shape=outs,
        scratch_shapes=[
            pltpu.VMEM((8, 128), jnp.int32),
            pltpu.VMEM((4, 128, 256), F32),
            pltpu.VMEM((4, 128, 256), F32),
            pltpu.VMEM((160, 256), F32),
            pltpu.VMEM((160, 256), F32),
            pltpu.VMEM((4, 4, 128, 256), F32),
            pltpu.VMEM((2, 128, 256), F32),
            pltpu.VMEM((2, 128, 256), F32),
            pltpu.VMEM((16, 256), F32),
            pltpu.VMEM((2, 128, 256), F32),
            pltpu.SemaphoreType.DMA((13,)),
            pltpu.SemaphoreType.DMA((4,)),
        ],
        compiler_params=params(32),
        cost_estimate=pl.CostEstimate(flops=50_000_000, bytes_accessed=15_000_000, transcendentals=0),
        name="outer",
    )(pairs, amplitudes, *args)


def spread_kernel(mine, got, out, both, sems):
    both[...] = mine[...] + got[...]
    copies = [pltpu.make_async_copy(both, out.at[n], sems.at[n]) for n in range(out.shape[0])]
    for copy in copies:
        copy.start()
    for copy in copies:
        copy.wait()


def spread(mine, got, count):
    return pl.pallas_call(
        spread_kernel,
        in_specs=[vmem()] * 2,
        out_specs=hbm(),
        out_shape=stored(count, 32, 128),
        scratch_shapes=[pltpu.VMEM((32, 128), F32), pltpu.SemaphoreType.DMA((count,))],
        compiler_params=params(2),
        name="spread",
    )(mine, got)


def blocks_kernel(a0, a1, a2, a3, i0, i1, i2, i3, pull, out, charges):
    elec = lax.axis_index("elec")
    total = a0[...] + a1[...] + a2[...] + a3[...]
    for e in range(4):
        charges[e] = total[8 * e : 8 * e + 8]
    upper = iota((8, 128), 0) < 4
    for turn, blocks in ((0, i0), (3, i1), (1, i2), (2, i3)):
        e = lax.rem(elec + turn, 4)
        charge = charges[e]
        start = blocks.shape[0] - 128
        both = blocks[start : start + 128, :]
        first = lax.dot_general(charge, both[:, 0:128], NT, precision=EXACT, preferred_element_type=F32)
        second = lax.dot_general(charge, both[:, 128:256], NT, precision=EXACT, preferred_element_type=F32)
        out[e] = jnp.where(upper, first, second)


def blocks(parts, impedances, pull):
    return pl.pallas_call(
        blocks_kernel,
        in_specs=[vmem()] * 8 + [pl.BlockSpec(memory_space=pl.ANY)],
        out_specs=vmem(),
        out_shape=f32(4, 8, 128),
        scratch_shapes=[pltpu.VMEM((4, 8, 128), F32)],
        compiler_params=params(4),
        name="blocks",
    )(*parts, *impedances, pull)


def ready_kernel(
    u2_hbm, gain_hbm, wxf_hbm, misc_hbm, zeta_hbm, h_near, h_far, e_lo, e_hi, base, pull,
    gain, wxf, misc, zeta_t, sems, small_sems,
):
    order = (2, 3, 4, 5, 1, 6, 0, 7)
    copies = {x: pltpu.make_async_copy(u2_hbm.at[:, x], base.at[:, x], sems.at[x]) for x in order}
    small = [
        pltpu.make_async_copy(source, target, small_sems.at[n])
        for n, (source, target) in enumerate(
            ((zeta_hbm, zeta_t), (misc_hbm, misc), (gain_hbm, gain), (wxf_hbm, wxf))
        )
    ]
    for copy in small:
        copy.start()
    for x in order:
        copies[x].start()
    for copy in small:
        copy.wait()
    for x in order:
        g = gain[x]
        part = (1.0 / OMEGA) * zeta_t[:, x : x + 1] * g
        pull[x] = part
        low = g[0:1] * misc[x : x + 1, :]
        high = g[127:128] * misc[8 + x : 9 + x, :]
        copies[x].wait()
        for s in range(4):
            at = 8 * s + x
            if x in (0, 7):
                from_near = sides()[0] == x // 7
                halo = jnp.where(from_near, wxf[0] * h_near[s], wxf[1] * h_far[s])
                base[s, x] = base[s, x] + g * halo
            base[s, x, 0:1, :] = base[s, x, 0:1, :] + low * e_lo[at : at + 1, :]
            base[s, x, 127:128, :] = base[s, x, 127:128, :] + high * e_hi[at : at + 1, :]
            u = base[s, x]
            base[s, x] = u - part * u


def ready(*args):
    return pl.pallas_call(
        ready_kernel,
        in_specs=[hbm()] * 5 + [vmem()] * 4,
        out_specs=[vmem()] * 2,
        out_shape=[kept(4, 8, 128, 256), kept(8, 128, 256)],
        scratch_shapes=[
            pltpu.VMEM((8, 128, 256), F32),
            pltpu.VMEM((2, 128, 256), F32),
            pltpu.VMEM((16, 256), F32),
            pltpu.VMEM((128, 128), F32),
            pltpu.SemaphoreType.DMA((8,)),
            pltpu.SemaphoreType.DMA((4,)),
        ],
        compiler_params=params(8),
        cost_estimate=pl.CostEstimate(flops=10_000_000, bytes_accessed=8_000_000, transcendentals=0),
        name="ready",
    )(*args)


def correct_kernel(cmap, own, got, base, pull, out_hbm, volts, table, buf, sems):
    core = lax.axis_index("core")
    elec = lax.axis_index("elec")
    table[core] = own[...]
    table[1 - core] = got[...]
    for h in range(2):
        for j in range(2):
            volts[:, 128 * (2 * h + j) : 128 * (2 * h + j) + 128] = table[h, elec, 4 * j : 4 * j + 4, :]
    ids = cmap[...]
    block = lax.shift_right_logical(ids, 7)
    lane = lax.bitwise_and(ids, 127)
    touched = []
    for s in range(4):
        found = jnp.zeros((8, 128), F32)
        for b in range(16):
            e, h, j = b // 4, (b // 2) % 2, b % 2
            row = jnp.broadcast_to(table[h, e, 4 * j + s : 4 * j + s + 1, :], (8, 128))
            found = jnp.where(block == b, jnp.take_along_axis(row, lane, axis=1), found)
        touched.append(found)
    stacked = jnp.concatenate(touched + [jnp.zeros((96, 128), F32)], axis=0)
    volts_t = jnp.transpose(stacked)
    copies = []
    for x in range(8):
        for s in range(4):
            buf[s, x] = base[s, x] + pull[x] * volts_t[:, 8 * s + x : 8 * s + x + 1]
        copy = pltpu.make_async_copy(buf.at[:, x], out_hbm.at[:, x], sems.at[x])
        copy.start()
        copies.append(copy)
    for copy in copies:
        copy.wait()


def correct(*args):
    return pl.pallas_call(
        correct_kernel,
        in_specs=[vmem()] * 5,
        out_specs=[hbm(), vmem()],
        out_shape=[f32(4, 8, 128, 256), f32(4, 512)],
        scratch_shapes=[
            pltpu.VMEM((2, 4, 8, 128), F32),
            pltpu.VMEM((4, 8, 128, 256), F32),
            pltpu.SemaphoreType.DMA((8,)),
        ],
        compiler_params=params(8),
        name="correct",
    )(*args)


def per_device(u, f, c, cmap, admittance, impedance, pairs, amplitudes):
    tiles = lax.axis_size(TILE)
    groups = lax.axis_size("zx")
    elecs = lax.axis_size("elec")
    admittance = admittance.reshape(16, 128)
    u, f, c, impedance = in_hbm(u), in_hbm(f), in_hbm(c), in_hbm(impedance)

    def from_below(a):
        return lax.ppermute(a, "elec", [(i, i + 1) for i in range(elecs - 1)])

    def from_above(a):
        return lax.ppermute(a, "elec", [(i + 1, i) for i in range(elecs - 1)])

    def rotated(a, turn):
        return lax.ppermute(a, "elec", [(i, (i + turn) % elecs) for i in range(elecs)])

    def near(a):
        return lax.ppermute(a, "core", [(0, 1), (1, 0)])

    def far(a):
        pairs = [(i, i + 1) for i in range(1, tiles - 1, 2)]
        return lax.ppermute(a, TILE, pairs + [(j, i) for i, j in pairs])

    own_lo, own_hi, row_near, row_far, side = edges(u, c, impedance, in_hbm(cmap))
    y_lo = from_below(own_hi)
    y_hi = from_above(own_lo)
    x_far = far(row_far)
    x_near = near(row_near)
    opposite = rotated(side, 2)
    ends_near, ends_far = corners(y_lo, y_hi)
    ends_far = far(ends_far)
    ends_near = near(ends_near)

    u, f, wx, wy, wz, diag, zeta_t = weights(u, f, c, cmap, admittance)
    u2, gain, wyl, wyh, pulled1, keep1, pulled2, e_lo, e_hi, contact = inner(
        u, f, cmap, own_lo, own_hi, y_lo, y_hi, wx, wy, wz, diag
    )
    face_near, face_far, edge_lo, edge_hi, u2, gain, wxf, misc, zeta_t, mine, other = outer(
        pairs.reshape(-1), amplitudes, cmap, admittance, side, in_hbm(row_near), in_hbm(row_far),
        y_lo, y_hi, x_near, x_far, ends_near, ends_far,
        wx, wy, wz, gain, wyl, wyh, u2, pulled1, keep1, pulled2, e_lo, e_hi, contact, zeta_t,
    )
    parts = spread(mine, near(other), groups)
    parts = lax.all_to_all(parts, "zx", 0, 0, tiled=True)
    summed = jnp.sum(parts, axis=0)
    h_far = far(face_far)
    h_near = near(face_near)
    e_lo = rotated(edge_hi, 1)
    e_hi = rotated(edge_lo, elecs - 1)
    base, pull = ready(
        in_hbm(u2), in_hbm(gain), in_hbm(wxf), in_hbm(misc), in_hbm(zeta_t), h_near, h_far, e_lo, e_hi
    )
    around = (summed, rotated(summed, 1), rotated(summed, elecs - 1), rotated(summed, 2))
    own = blocks(around, (side, e_lo, e_hi, opposite), pull)
    got = near(own)
    out, volts = correct(cmap, own, got, base, pull)
    return out, volts


def solution(mesh):
    tile, src, elec = mesh.devices.shape
    cut = Mesh(mesh.devices.reshape(tile // 2, 2, src, elec), ("zx", "core", "src", "elec"))
    placed = (
        P("src", TILE, "elec", None),
        P("src", TILE, "elec", None),
        P(TILE, "elec", None),
        P(TILE, "elec"),
        P(),
        P("elec", None, None),
        P("src", None),
        P("src"),
    )
    return jax.shard_map(
        per_device,
        mesh=cut,
        in_specs=placed,
        out_specs=(P("src", TILE, "elec", None), P("src", "elec")),
        check_vma=False,
    )
```

```python
import jax
import jax.numpy as jnp
from jax import lax
from jax.experimental import pallas as pl
from jax.experimental.pallas import tpu as pltpu
from jax.sharding import Mesh
from jax.sharding import PartitionSpec as P

OMEGA = 0.8
KEEP = 1.0 - OMEGA
TINY = 1e-30
F32 = jnp.float32
EXACT = lax.Precision.HIGHEST
MIB = 1024 * 1024
TILE = ("zx", "core")

NT = (((1,), (1,)), ((), ()))


def params(mib):
    return pltpu.CompilerParams(vmem_limit_bytes=mib * MIB)


def vmem():
    return pl.BlockSpec(memory_space=pltpu.VMEM)


def hbm():
    return pl.BlockSpec(memory_space=pltpu.HBM)


def f32(*shape):
    return jax.ShapeDtypeStruct(shape, F32)


def kept(*shape):
    return pltpu.VMEM(shape, F32)


def stored(*shape):
    return pltpu.HBM(shape, F32)


def in_hbm(a):
    return pltpu.with_memory_space_constraint(a, pltpu.HBM)


def inverse(a):
    r = pl.reciprocal(a, approx=True)
    return r * (2.0 - a * r)


def face(a, b):
    return (2.0 * a * b) * inverse(a + b)


def outer_face(a, b):
    return (2.0 * a * b) * inverse(jnp.maximum(a + b, TINY))


def iota(shape, dim):
    return lax.broadcasted_iota(jnp.int32, shape, dim)


def shift_up(a, axis):
    return pltpu.roll(a, a.shape[axis] - 1, axis)


def shift_down(a, axis):
    return pltpu.roll(a, 1, axis)


def in_line(flux_weight, u, axis):
    return flux_weight * shift_up(u, axis) + shift_down(flux_weight * u, axis)


def line_weight(c, axis):
    w = face(c, shift_up(c, axis))
    return jnp.where(iota(c.shape, axis) < c.shape[axis] - 1, w, 0.0)


def both_sides(w, axis):
    return w + shift_down(w, axis)


def row_sums(slabs):
    folded = jnp.concatenate([p[:, :128] + p[:, 128:] for p in slabs], axis=0)
    head = folded.astype(jnp.bfloat16)
    rest = (folded - head.astype(F32)).astype(jnp.bfloat16)
    ones = jnp.ones((8, 128), jnp.bfloat16)
    total = lax.dot_general(ones, head, NT, preferred_element_type=F32)
    total = total + lax.dot_general(ones, rest, NT, preferred_element_type=F32)
    return jnp.concatenate([total[0:1, 128 * s : 128 * s + 128] for s in range(4)], axis=0)


def to_lanes(column):
    mask = iota((8, 128), 0) == iota((8, 128), 1)
    return jnp.sum(jnp.where(mask, column, jnp.zeros_like(column)), axis=0, keepdims=True)


def gather_rows(ids, table):
    block = lax.shift_right_logical(ids, 7)
    lane = lax.bitwise_and(ids, 127)
    found = jnp.zeros(ids.shape, F32)
    for b in range(16):
        row = jnp.broadcast_to(table[b : b + 1], ids.shape)
        got = jnp.take_along_axis(row, lane, axis=1)
        found = jnp.where(block == b, got, found)
    return found


def scatter(id_rows, values):
    place = iota((64, 128), 0)
    block_of = 4 * ((place // 8) % 4) + 2 * (place // 32) + (place // 4) % 2
    total = jnp.zeros((192, 128), F32)
    for id_row, value in zip(id_rows, values):
        hit = lax.shift_right_logical(id_row, 7) == block_of
        spread = jnp.where(hit, jnp.concatenate([value] * 16, axis=0), 0.0)
        lane_hit = lax.bitwise_and(id_row, 127) == iota((128, 128), 0)
        onehot = jnp.where(lane_hit, 1.0, 0.0).astype(jnp.bfloat16)
        a = spread.astype(jnp.bfloat16)
        spread = spread - a.astype(F32)
        b = spread.astype(jnp.bfloat16)
        spread = spread - b.astype(F32)
        parts = jnp.concatenate([a, b, spread.astype(jnp.bfloat16)], axis=0)
        total = total + lax.dot_general(parts, onehot, NT, preferred_element_type=F32)
    return total[0:64] + total[64:128] + total[128:192]


ROW_C = 512
ROW_C2 = 640
ROW_MAP = 768
ROWS = 776


def sides():
    core = lax.axis_index("core")
    return 1 - core, core


def has_elecs():
    elec = lax.axis_index("elec")
    last = lax.axis_size("elec") - 1
    return jnp.where(elec > 0, 1.0, 0.0), jnp.where(elec < last, 1.0, 0.0)


def edges_kernel(
    u_hbm, c_hbm, imp_hbm, cmap_hbm, out_lo, out_hi, near_out, far_out, blocks, u, c, cmap, imp, side_by_side, sems, whole_sems
):
    core = lax.axis_index("core")
    copies = []
    for n, y in enumerate((0, 120)):
        copies.append(pltpu.make_async_copy(u_hbm.at[:, :, pl.ds(y, 8)], u.at[n], sems.at[2 * n]))
        copies.append(pltpu.make_async_copy(c_hbm.at[:, pl.ds(y, 8)], c.at[n], sems.at[2 * n + 1]))
    whole = []
    for n, (out, side) in enumerate(zip((near_out, far_out), sides())):
        for s in range(4):
            whole.append((u_hbm.at[s, 7 * side], out.at[pl.ds(128 * s, 128)], whole_sems.at[n, s]))
        whole.append((c_hbm.at[7 * side], out.at[pl.ds(ROW_C, 128)], whole_sems.at[n, 4]))
        whole.append((c_hbm.at[1 + 5 * side], out.at[pl.ds(ROW_C2, 128)], whole_sems.at[n, 5]))
    rows_of_blocks = [
        pltpu.make_async_copy(imp_hbm.at[2 * core + n], imp.at[n], whole_sems.at[n, 7]) for n in range(2)
    ]
    whole = [pltpu.make_async_copy(*copy) for copy in whole]
    copies.append(pltpu.make_async_copy(cmap_hbm, cmap, sems.at[4]))
    for copy in copies + rows_of_blocks + whole:
        copy.start()
    for copy in copies + rows_of_blocks:
        copy.wait()
    side_by_side[:, 0:128] = imp[0]
    side_by_side[:, 128:256] = imp[1]
    copy_blocks = pltpu.make_async_copy(side_by_side, blocks, sems.at[5])
    copy_blocks.start()
    for n, out, near, far, lane in ((0, out_lo, 0, 1, 0), (1, out_hi, 7, 6, 127)):
        out[56:184, 0:128] = imp[0]
        out[56:184, 128:256] = imp[1]
        for x in range(8):
            for s in range(4):
                out[8 * s + x : 8 * s + x + 1, :] = u[n, s, x, near : near + 1, :]
            out[32 + x : 33 + x, :] = c[n, x, near : near + 1, :]
            out[40 + x : 41 + x, :] = c[n, x, far : far + 1, :]
        out[48:56, :] = jnp.zeros((8, 256), F32)
        out[48:49, 0:128] = to_lanes(cmap[:, lane : lane + 1].astype(F32))
    for out, side in zip((near_out, far_out), sides()):
        out[ROW_MAP:ROWS, :] = jnp.zeros((8, 256), F32)
        out[ROW_MAP : ROW_MAP + 1, 0:128] = cmap[pl.ds(7 * side, 1), :].astype(F32)
    for copy in whole:
        copy.wait()
    copy_blocks.wait()


def edges(u, c, impedance, cmap):
    return pl.pallas_call(
        edges_kernel,
        in_specs=[hbm()] * 4,
        out_specs=[vmem()] * 4 + [hbm()],
        out_shape=[f32(184, 256), f32(184, 256), f32(ROWS, 256), f32(ROWS, 256), stored(128, 256)],
        scratch_shapes=[
            pltpu.VMEM((2, 4, 8, 8, 256), F32),
            pltpu.VMEM((2, 8, 8, 256), F32),
            pltpu.VMEM((8, 128), jnp.int32),
            pltpu.VMEM((2, 128, 128), F32),
            pltpu.VMEM((128, 256), F32),
            pltpu.SemaphoreType.DMA((6,)),
            pltpu.SemaphoreType.DMA((2, 8)),
        ],
        compiler_params=params(4),
        name="edges",
    )(u, c, impedance, cmap)


def corners_kernel(y_lo, y_hi, near_out, far_out):
    below, above = has_elecs()
    for out, side in zip((near_out, far_out), sides()):
        out[...] = jnp.zeros((8, 256), F32)
        out[0:1, :] = below * y_lo[pl.ds(32 + 7 * side, 1), :]
        out[1:2, :] = above * y_hi[pl.ds(32 + 7 * side, 1), :]


def corners(y_lo, y_hi):
    return pl.pallas_call(
        corners_kernel,
        in_specs=[vmem()] * 2,
        out_specs=[vmem()] * 2,
        out_shape=[f32(8, 256)] * 2,
        compiler_params=params(2),
        name="corners",
    )(y_lo, y_hi)


def weights_kernel(
    u_hbm, f_hbm, c_hbm, cmap_hbm, admittance_hbm, u, f, wx, wy, wz, diag, zeta_t, c, cmap, admittance, sems
):
    small = [
        pltpu.make_async_copy(cmap_hbm, cmap, sems.at[3]),
        pltpu.make_async_copy(admittance_hbm, admittance, sems.at[4]),
    ]
    copy = pltpu.make_async_copy(c_hbm, c, sems.at[0])
    later = [pltpu.make_async_copy(u_hbm, u, sems.at[1]), pltpu.make_async_copy(f_hbm, f, sems.at[2])]
    for other in small:
        other.start()
    copy.start()
    for other in later:
        other.start()
    for other in small:
        other.wait()
    zeta = gather_rows(cmap[...], admittance[...])
    zeta_t[...] = jnp.transpose(jnp.concatenate([zeta, jnp.zeros((120, 128), F32)], axis=0))
    copy.wait()
    for x in range(8):
        here = c[x]
        if x < 7:
            wx[x] = face(here, c[x + 1])
        along_y = line_weight(here, 0)
        along_z = line_weight(here, 1)
        wy[x] = along_y
        wz[x] = along_z
        total = both_sides(along_y, 0) + both_sides(along_z, 1) + zeta_t[:, x : x + 1]
        if x > 0:
            total = total + wx[x - 1]
        if x < 7:
            total = total + wx[x]
        diag[x] = total
    for other in later:
        other.wait()


def weights(u, f, c, cmap, admittance):
    outs = [
        kept(4, 8, 128, 256), kept(4, 8, 128, 256),
        kept(7, 128, 256), kept(8, 128, 256), kept(8, 128, 256), kept(8, 128, 256), kept(128, 128),
    ]
    return pl.pallas_call(
        weights_kernel,
        in_specs=[hbm()] * 5,
        out_specs=[vmem()] * len(outs),
        out_shape=outs,
        scratch_shapes=[
            pltpu.VMEM((8, 128, 256), F32),
            pltpu.VMEM((8, 128), jnp.int32),
            pltpu.VMEM((16, 128), F32),
            pltpu.SemaphoreType.DMA((5,)),
        ],
        compiler_params=params(8),
        cost_estimate=pl.CostEstimate(flops=20_000_000, bytes_accessed=6_000_000, transcendentals=0),
        name="weights",
    )(u, f, c, cmap, admittance)


def inner_kernel(
    u, f, cmap, own_lo, own_hi, y_lo, y_hi, wx, wy, wz, diag,
    u2, u2_out, gain, wyl, wyh, pulled1, keep1, pulled2, edge_lo, edge_hi, contact,
    u1, sums, middle, sems,
):
    below, above = has_elecs()
    wyl[...] = outer_face(own_lo[32:40, :], below * y_lo[32:40, :])
    wyh[...] = outer_face(own_hi[32:40, :], above * y_hi[32:40, :])
    for x in range(8):
        gain[x] = diag[x]
        gain[x, 0:1, :] = gain[x, 0:1, :] + wyl[x : x + 1, :]
        gain[x, 127:128, :] = gain[x, 127:128, :] + wyh[x : x + 1, :]
        if x not in (0, 7):
            gain[x] = OMEGA * inverse(gain[x])

    for n, x in enumerate((0, 7)):
        for s in range(4):
            pulled = f[s, x] + in_line(wy[x], u[s, x], 0)
            pulled = pulled + in_line(wz[x], u[s, x], 1)
            pulled = pulled + (wx[0] * u[s, 1] if x == 0 else wx[6] * u[s, 6])
            pulled1[n, s] = pulled
            pulled1[n, s, 0:1, :] = pulled1[n, s, 0:1, :] + wyl[x : x + 1, :] * y_lo[8 * s + x : 8 * s + x + 1, :]
            pulled1[n, s, 127:128, :] = (
                pulled1[n, s, 127:128, :] + wyh[x : x + 1, :] * y_hi[8 * s + x : 8 * s + x + 1, :]
            )
            keep1[n, s] = KEEP * u[s, x]

    def first(x, carry):
        for s in range(4):
            pulled = f[s, x] + in_line(wy[x], u[s, x], 0)
            pulled = pulled + in_line(wz[x], u[s, x], 1)
            pulled = pulled + wx[x - 1] * u[s, x - 1] + wx[x] * u[s, x + 1]
            u1[s, x] = KEEP * u[s, x] + gain[x] * pulled
            low = u1[s, x, 0:1, :] + gain[x, 0:1, :] * wyl[pl.ds(x, 1), :] * y_lo[pl.ds(8 * s + x, 1), :]
            high = u1[s, x, 127:128, :] + gain[x, 127:128, :] * wyh[pl.ds(x, 1), :] * y_hi[pl.ds(8 * s + x, 1), :]
            u1[s, x, 0:1, :] = low
            u1[s, x, 127:128, :] = high
            edge_lo[pl.ds(8 * s + x, 1), :] = low
            edge_hi[pl.ds(8 * s + x, 1), :] = high
        return carry

    lax.fori_loop(1, 7, first, 0)

    for s in range(4):
        pulled2[0, s] = f[s, 0] + wx[0] * u1[s, 1]
        pulled2[1, s] = f[s, 7] + wx[6] * u1[s, 6]
        u1[s, 0] = jnp.zeros((128, 256), F32)
        u1[s, 7] = jnp.zeros((128, 256), F32)

    def second(x, target):
        slabs = []
        for s in range(4):
            pulled = f[s, x] + in_line(wy[x], u1[s, x], 0)
            pulled = pulled + in_line(wz[x], u1[s, x], 1)
            pulled = pulled + wx[x - 1] * u1[s, x - 1] + wx[x] * u1[s, x + 1]
            new = KEEP * u1[s, x] + gain[x] * pulled
            target[s] = new
            slabs.append(new)
        sums[x] = row_sums(slabs)

    def second_middle(x, carry):
        second(x, middle.at[x - 2])
        pltpu.make_async_copy(middle.at[x - 2], u2_out.at[:, x - 2], sems.at[x - 2]).start()
        return carry

    lax.fori_loop(2, 6, second_middle, 0)
    second(1, u2.at[0])
    second(6, u2.at[1])
    contact[...] = scatter([cmap[x : x + 1, :] for x in range(1, 7)], [sums[x] for x in range(1, 7)])
    for n in range(4):
        pltpu.make_async_copy(middle.at[n], u2_out.at[:, n], sems.at[n]).wait()


def inner(u, f, cmap, own_lo, own_hi, y_lo, y_hi, wx, wy, wz, diag):
    outs = [
        kept(2, 4, 128, 256), stored(4, 4, 128, 256), kept(8, 128, 256), kept(8, 256), kept(8, 256),
        kept(2, 4, 128, 256), kept(2, 4, 128, 256), kept(2, 4, 128, 256),
        kept(32, 256), kept(32, 256), kept(64, 128),
    ]
    return pl.pallas_call(
        inner_kernel,
        in_specs=[vmem()] * 11,
        out_specs=[vmem(), hbm()] + [vmem()] * (len(outs) - 2),
        out_shape=outs,
        scratch_shapes=[
            pltpu.VMEM((4, 8, 128, 256), F32),
            pltpu.VMEM((8, 4, 128), F32),
            pltpu.VMEM((4, 4, 128, 256), F32),
            pltpu.SemaphoreType.DMA((4,)),
        ],
        compiler_params=params(16),
        cost_estimate=pl.CostEstimate(flops=100_000_000, bytes_accessed=25_000_000, transcendentals=0),
        name="inner",
    )(u, f, cmap, own_lo, own_hi, y_lo, y_hi, wx, wy, wz, diag)


def outer_kernel(
    pairs, amplitudes, cmap, admittance, near, far, y_lo, y_hi, x_near, x_far, ends_near, ends_far,
    wx, wy, wz, gain, wyl, wyh, u2, pulled1, keep1, pulled2, e_lo, e_hi, contact, zeta_in,
    face_near_out, face_far_out, edge_lo_out, edge_hi_out, u2_out, gain_out, wxf_out, misc_out, zeta_out, mine,
    ids, face_near, face_far, edge_lo, edge_hi, u2b, gain_b, wxf, misc, c_own, passed, sems, u2_sems, near_sems, edge_sems,
):
    copies = []
    rows_in = [
        pltpu.make_async_copy(source.at[pl.ds(ROW_C, 128)], c_own.at[n], sems.at[11 + n])
        for n, source in enumerate((near, far))
    ]
    for copy in rows_in:
        copy.start()

    def send(source, target, sem):
        copy = pltpu.make_async_copy(source, target, sem)
        copy.start()
        copies.append(copy)

    send(gain.at[pl.ds(1, 6)], gain_out.at[pl.ds(1, 6)], sems.at[0])
    send(zeta_in, zeta_out, sems.at[1])
    misc[0:8, :] = wyl[...]
    misc[8:16, :] = wyh[...]
    send(misc, misc_out, sems.at[3])
    ids[0:8, :] = jnp.full((8, 128), 2048, jnp.int32)
    ids[0:1, :] = x_near[ROW_MAP : ROW_MAP + 1, 0:128].astype(jnp.int32)
    ids[1:2, :] = x_far[ROW_MAP : ROW_MAP + 1, 0:128].astype(jnp.int32)
    lanes = iota((1, 128), 1)
    low_ids = y_lo[48:49, 0:128].astype(jnp.int32)
    high_ids = pltpu.roll(y_hi[48:49, 0:128], 8, 1).astype(jnp.int32)
    ids[2:3, :] = jnp.where(lanes < 8, low_ids, jnp.where(lanes < 16, high_ids, 2048))
    zeta = gather_rows(ids[...], admittance[...])
    zeta_t = jnp.transpose(jnp.concatenate([zeta, jnp.zeros((120, 128), F32)], axis=0))
    row = iota((128, 256), 0)

    id_rows = []
    values = []
    for copy in rows_in:
        copy.wait()
    for n, (side, msg, ends, out, sent) in enumerate(
        zip(sides(), (x_near, x_far), (ends_near, ends_far), (face_near, face_far), (face_near_out, face_far_out))
    ):
        x = 7 * side
        there = msg[ROW_C : ROW_C + 128, :]
        outside = outer_face(c_own[n], there)
        wxf[n] = outside
        g = OMEGA * inverse(gain[x] + outside)
        gain_b[n] = g
        for s in range(4):
            out[s] = keep1[side, s] + g * (pulled1[side, s] + outside * msg[128 * s : 128 * s + 128, :])
        if n:
            send(out, sent, sems.at[4])
        else:
            for s in range(4):
                send(out.at[s], sent.at[pl.ds(128 * s, 128)], near_sems.at[s])
        send(gain_b.at[n], gain_out.at[x], sems.at[6 + n])
        spare = jnp.maximum(there, TINY)
        diag = both_sides(line_weight(spare, 0), 0) + both_sides(line_weight(spare, 1), 1) + zeta_t[:, n : n + 1]
        diag = diag + outside + outer_face(there, msg[ROW_C2 : ROW_C2 + 128, :])
        diag = diag + jnp.where(row == 0, outer_face(there[0:1], ends[0:1, :]), 0.0)
        diag = diag + jnp.where(row == 127, outer_face(there[127:128], ends[1:2, :]), 0.0)
        factor = OMEGA * outside * inverse(jnp.maximum(diag, TINY))
        id_rows.append(ids[n : n + 1, :])
        values.append(row_sums([factor * out[s] for s in range(4)]))
        inside = 1 + 5 * side
        factor = gain[inside] * wx[6 * side]
        slabs = []
        for s in range(4):
            new = factor * out[s]
            u2b[2 * n + 1, s] = u2[side, s] + new
            slabs.append(new)
        send(u2b.at[2 * n + 1], u2_out.at[2 * side + 1], u2_sems.at[2 * n + 1])
        id_rows.append(cmap[pl.ds(inside, 1), :])
        values.append(row_sums(slabs))
        slabs = []
        for s in range(4):
            pulled = pulled2[side, s] + in_line(wy[x], out[s], 0)
            pulled = pulled + in_line(wz[x], out[s], 1)
            new = KEEP * out[s] + g * pulled
            u2b[2 * n, s] = new
            slabs.append(new)
        send(u2b.at[2 * n], u2_out.at[2 * side], u2_sems.at[2 * n])
        id_rows.append(cmap[pl.ds(x, 1), :])
        values.append(row_sums(slabs))

    send(wxf, wxf_out, sems.at[8])

    edge_sums = jnp.zeros((4, 128), F32)
    for n, (msg, own, inside, edge, y, sent) in enumerate(
        ((y_lo, wyl, e_lo, edge_lo, 0, edge_lo_out), (y_hi, wyh, e_hi, edge_hi, 127, edge_hi_out))
    ):
        edge[0:32, :] = inside[...]
        for s in range(4):
            for side, out in zip(sides(), (face_near, face_far)):
                edge[pl.ds(8 * s + 7 * side, 1), :] = out[s, y : y + 1, :]
        send(edge, sent, edge_sems.at[n])
        there = msg[32:40, :]
        x_rows = iota((8, 256), 0)
        spare = jnp.maximum(there, TINY)
        diag = both_sides(line_weight(spare, 0), 0) + both_sides(line_weight(spare, 1), 1) + own[...]
        diag = diag + outer_face(there, msg[40:48, :])
        for side, ends in zip(sides(), (ends_near, ends_far)):
            diag = diag + jnp.where(x_rows == 7 * side, outer_face(there, ends[n : n + 1, :]), 0.0)
        diag = diag + zeta_t[8 * n : 8 * n + 8, 2:3]
        factor = OMEGA * own[...] * inverse(jnp.maximum(diag, TINY))
        lined = []
        for s in range(4):
            line = to_lanes(jnp.sum(factor * edge[8 * s : 8 * s + 8, :], axis=1, keepdims=True))
            lined.append(pltpu.roll(line, 8 * n, 1) if n else line)
        edge_sums = edge_sums + jnp.concatenate(lined, axis=0)
    id_rows.append(ids[2:3, :])
    values.append(edge_sums)

    total = (contact[...] + scatter(id_rows, values)) * (1.0 / 256.0)
    place = iota((64, 128), 0)
    electrode = (4 * ((place // 8) % 4) + 2 * (place // 32) + (place // 4) % 2) * 128 + iota((64, 128), 1)
    adds = jnp.logical_and(lax.axis_index("zx") == 0, lax.axis_index("elec") == 0)
    adds = jnp.logical_and(adds, lax.axis_index("core") == 0)
    for s in range(4):
        at = place % 4 == s
        amount = jnp.where(adds, amplitudes[0:1, s : s + 1], 0.0)
        total = total + jnp.where(at & (electrode == pairs[0:1, s : s + 1]), amount, 0.0)
        total = total - jnp.where(at & (electrode == pairs[1:2, s : s + 1]), amount, 0.0)
    first_half = lax.axis_index("core") == 0
    mine[...] = jnp.where(first_half, total[0:32], total[32:64])
    passed[:, 0:128] = jnp.where(first_half, total[32:48], total[0:16])
    passed[:, 128:256] = jnp.where(first_half, total[48:64], total[16:32])
    send(passed, face_near_out.at[pl.ds(512, 16)], sems.at[10])
    for copy in copies:
        copy.wait()


def outer(pairs, amplitudes, *args):
    outs = [
        stored(528, 256), stored(4, 128, 256), stored(32, 256), stored(32, 256),
        stored(4, 4, 128, 256), stored(8, 128, 256), stored(2, 128, 256), stored(16, 256), stored(128, 128),
        f32(32, 128),
    ]
    specs = [vmem()] * len(args)
    specs[2] = specs[3] = hbm()
    return pl.pallas_call(
        outer_kernel,
        in_specs=[vmem()] * 2 + specs,
        out_specs=[hbm()] * 9 + [vmem()],
        out_shape=outs,
        scratch_shapes=[
            pltpu.VMEM((8, 128), jnp.int32),
            pltpu.VMEM((4, 128, 256), F32),
            pltpu.VMEM((4, 128, 256), F32),
            pltpu.VMEM((32, 256), F32),
            pltpu.VMEM((32, 256), F32),
            pltpu.VMEM((4, 4, 128, 256), F32),
            pltpu.VMEM((2, 128, 256), F32),
            pltpu.VMEM((2, 128, 256), F32),
            pltpu.VMEM((16, 256), F32),
            pltpu.VMEM((2, 128, 256), F32),
            pltpu.VMEM((16, 256), F32),
            pltpu.SemaphoreType.DMA((13,)),
            pltpu.SemaphoreType.DMA((4,)),
            pltpu.SemaphoreType.DMA((4,)),
            pltpu.SemaphoreType.DMA((2,)),
        ],
        compiler_params=params(32),
        cost_estimate=pl.CostEstimate(flops=50_000_000, bytes_accessed=15_000_000, transcendentals=0),
        name="outer",
    )(pairs, amplitudes, *args)


def spread_kernel(mine, got_hbm, out, both, got, got_sem, sems):
    copy = pltpu.make_async_copy(got_hbm.at[pl.ds(512, 16)], got, got_sem)
    copy.start()
    copy.wait()
    both[0:16, :] = mine[0:16, :] + got[:, 0:128]
    both[16:32, :] = mine[16:32, :] + got[:, 128:256]
    copies = [pltpu.make_async_copy(both, out.at[n], sems.at[n]) for n in range(out.shape[0])]
    for copy in copies:
        copy.start()
    for copy in copies:
        copy.wait()


def spread(mine, got, count):
    return pl.pallas_call(
        spread_kernel,
        in_specs=[vmem(), pl.BlockSpec(memory_space=pl.ANY)],
        out_specs=hbm(),
        out_shape=stored(count, 32, 128),
        scratch_shapes=[
            pltpu.VMEM((32, 128), F32),
            pltpu.VMEM((16, 256), F32),
            pltpu.SemaphoreType.DMA,
            pltpu.SemaphoreType.DMA((count,)),
        ],
        compiler_params=params(2),
        name="spread",
    )(mine, got)


def gathered_kernel(parts_hbm, edge_lo, edge_hi, to_above, to_below, out, parts, sems, edge_sems):
    copies = [pltpu.make_async_copy(parts_hbm.at[n], parts.at[n], sems.at[n]) for n in range(parts.shape[0])]
    for n, (source, target) in enumerate(((edge_hi, to_above), (edge_lo, to_below))):
        copies.append(pltpu.make_async_copy(source, target.at[pl.ds(16, 32)], edge_sems.at[n]))
    for copy in copies:
        copy.start()
    for copy in copies:
        copy.wait()
    total = jnp.sum(parts[...], axis=0)
    for target in (out, to_above, to_below):
        target[0:16, 0:128] = total[0:16]
        target[0:16, 128:256] = total[16:32]


def gathered(parts, edge_lo, edge_hi):
    return pl.pallas_call(
        gathered_kernel,
        in_specs=[hbm()] * 3,
        out_specs=[vmem()] * 3,
        out_shape=[f32(48, 256), f32(48, 256), f32(16, 256)],
        scratch_shapes=[
            pltpu.VMEM(parts.shape, F32),
            pltpu.SemaphoreType.DMA((parts.shape[0],)),
            pltpu.SemaphoreType.DMA((2,)),
        ],
        compiler_params=params(4),
        name="gathered",
    )(parts, edge_lo, edge_hi)


def blocks_kernel(a0, a1, a2, a3, i0, i1, i2, i3, pull, out, charges):
    elec = lax.axis_index("elec")
    total = a0[0:16, :] + a1[0:16, :] + a2[...] + a3[0:16, :]
    for e in range(4):
        charges[e] = total[8 * (e % 2) : 8 * (e % 2) + 8, 128 * (e // 2) : 128 * (e // 2) + 128]
    upper = iota((8, 128), 0) < 4
    for turn, blocks in ((3, i0), (1, i1), (0, i2), (2, i3)):
        e = lax.rem(elec + turn, 4)
        charge = charges[e]
        start = blocks.shape[0] - 128
        both = blocks[start : start + 128, :]
        first = lax.dot_general(charge, both[:, 0:128], NT, precision=EXACT, preferred_element_type=F32)
        second = lax.dot_general(charge, both[:, 128:256], NT, precision=EXACT, preferred_element_type=F32)
        out[e] = jnp.where(upper, first, second)


def blocks(parts, impedances, pull):
    return pl.pallas_call(
        blocks_kernel,
        in_specs=[vmem()] * 8 + [pl.BlockSpec(memory_space=pl.ANY)],
        out_specs=vmem(),
        out_shape=f32(4, 8, 128),
        scratch_shapes=[pltpu.VMEM((4, 8, 128), F32)],
        compiler_params=params(4),
        name="blocks",
    )(*parts, *impedances, pull)


def ready_kernel(
    after, inner_hbm, outer_hbm, gain_hbm, wxf_hbm, misc_hbm, zeta_hbm, base, pull, sides_out, rows_out,
    gain, wxf, misc, zeta_t, sems, small_sems,
):
    order = (2, 3, 4, 5, 1, 6, 0, 7)
    rows = {x: inner_hbm.at[:, x - 2] for x in range(2, 6)}
    rows.update({x: outer_hbm.at[n] for n, x in enumerate((0, 1, 7, 6))})
    copies = {x: pltpu.make_async_copy(rows[x], base.at[:, x], sems.at[x]) for x in order}
    small = [
        pltpu.make_async_copy(source, target, small_sems.at[n])
        for n, (source, target) in enumerate(
            ((zeta_hbm, zeta_t), (misc_hbm, misc), (gain_hbm, gain), (wxf_hbm, wxf))
        )
    ]
    for copy in small:
        copy.start()
    for x in order:
        copies[x].start()
    for copy in small:
        copy.wait()
    for x in order:
        g = gain[x]
        part = (1.0 / OMEGA) * zeta_t[:, x : x + 1] * g
        pull[x] = part
        sides_out[x : x + 1, :] = (1.0 - part[0:1]) * g[0:1] * misc[x : x + 1, :]
        sides_out[8 + x : 9 + x, :] = (1.0 - part[127:128]) * g[127:128] * misc[8 + x : 9 + x, :]
        copies[x].wait()
        if x in (0, 7):
            n = jnp.where(sides()[0] == x // 7, 0, 1)
            rows_out[x // 7] = (1.0 - part) * g * wxf[n]
        for s in range(4):
            u = base[s, x]
            base[s, x] = u - part * u


def ready(*args):
    return pl.pallas_call(
        ready_kernel,
        in_specs=[pl.BlockSpec(memory_space=pl.ANY)] + [hbm()] * 6,
        out_specs=[vmem()] * 4,
        out_shape=[kept(4, 8, 128, 256), kept(8, 128, 256), kept(16, 256), kept(2, 128, 256)],
        scratch_shapes=[
            pltpu.VMEM((8, 128, 256), F32),
            pltpu.VMEM((2, 128, 256), F32),
            pltpu.VMEM((16, 256), F32),
            pltpu.VMEM((128, 128), F32),
            pltpu.SemaphoreType.DMA((8,)),
            pltpu.SemaphoreType.DMA((4,)),
        ],
        compiler_params=params(8),
        cost_estimate=pl.CostEstimate(flops=10_000_000, bytes_accessed=8_000_000, transcendentals=0),
        name="ready",
    )(*args)


def correct_kernel(
    cmap, own, got, base, pull, weight, row_weight, e_lo, e_hi, h_near, h_far, out_hbm, volts, table, buf, sems
):
    core = lax.axis_index("core")
    elec = lax.axis_index("elec")
    table[core] = own[...]
    table[1 - core] = got[...]
    for h in range(2):
        for j in range(2):
            volts[:, 128 * (2 * h + j) : 128 * (2 * h + j) + 128] = table[h, elec, 4 * j : 4 * j + 4, :]
    ids = cmap[...]
    block = lax.shift_right_logical(ids, 7)
    lane = lax.bitwise_and(ids, 127)
    touched = []
    for s in range(4):
        found = jnp.zeros((8, 128), F32)
        for b in range(16):
            e, h, j = b // 4, (b // 2) % 2, b % 2
            row = jnp.broadcast_to(table[h, e, 4 * j + s : 4 * j + s + 1, :], (8, 128))
            found = jnp.where(block == b, jnp.take_along_axis(row, lane, axis=1), found)
        touched.append(found)
    stacked = jnp.concatenate(touched + [jnp.zeros((96, 128), F32)], axis=0)
    volts_t = jnp.transpose(stacked)
    copies = []
    near_side = sides()[0]
    for x in (1, 2, 3, 4, 5, 6, 0, 7):
        for s in range(4):
            at = 8 * s + x
            new = base[s, x] + pull[x] * volts_t[:, at : at + 1]
            if x in (0, 7):
                halo = jnp.where(near_side == x // 7, h_near[128 * s : 128 * s + 128, :], h_far[s])
                new = new + row_weight[x // 7] * halo
            buf[s, x] = new
            low = weight[x : x + 1, :] * e_lo[16 + at : 17 + at, :]
            high = weight[8 + x : 9 + x, :] * e_hi[16 + at : 17 + at, :]
            buf[s, x, 0:1, :] = buf[s, x, 0:1, :] + low
            buf[s, x, 127:128, :] = buf[s, x, 127:128, :] + high
        copy = pltpu.make_async_copy(buf.at[:, x], out_hbm.at[:, x], sems.at[x])
        copy.start()
        copies.append(copy)
    for copy in copies:
        copy.wait()


def correct(*args):
    return pl.pallas_call(
        correct_kernel,
        in_specs=[vmem()] * 11,
        out_specs=[hbm(), vmem()],
        out_shape=[f32(4, 8, 128, 256), f32(4, 512)],
        scratch_shapes=[
            pltpu.VMEM((2, 4, 8, 128), F32),
            pltpu.VMEM((4, 8, 128, 256), F32),
            pltpu.SemaphoreType.DMA((8,)),
        ],
        compiler_params=params(8),
        name="correct",
    )(*args)


def per_device(u, f, c, cmap, admittance, impedance, pairs, amplitudes):
    tiles = lax.axis_size(TILE)
    groups = lax.axis_size("zx")
    elecs = lax.axis_size("elec")
    admittance = admittance.reshape(16, 128)
    u, f, c, impedance = in_hbm(u), in_hbm(f), in_hbm(c), in_hbm(impedance)

    def rotated(a, turn):
        return lax.ppermute(a, "elec", [(i, (i + turn) % elecs) for i in range(elecs)])

    def near(a):
        return lax.ppermute(a, "core", [(0, 1), (1, 0)])

    def far(a):
        pairs = [(i, i + 1) for i in range(1, tiles - 1, 2)]
        return lax.ppermute(a, TILE, pairs + [(j, i) for i, j in pairs])

    own_lo, own_hi, row_near, row_far, side = edges(u, c, impedance, in_hbm(cmap))
    y_lo = rotated(own_hi, 1)
    y_hi = rotated(own_lo, elecs - 1)
    x_far = far(row_far)
    x_near = near(row_near)
    opposite = rotated(side, 2)
    ends_near, ends_far = corners(y_lo, y_hi)
    ends_far = far(ends_far)
    ends_near = near(ends_near)

    u, f, wx, wy, wz, diag, zeta_t = weights(u, f, c, in_hbm(cmap), in_hbm(admittance))
    u2, u2_inner, gain, wyl, wyh, pulled1, keep1, pulled2, e_lo, e_hi, contact = inner(
        u, f, cmap, own_lo, own_hi, y_lo, y_hi, wx, wy, wz, diag
    )
    face_near, face_far, edge_lo, edge_hi, u2_outer, gain, wxf, misc, zeta_t, mine = outer(
        pairs.T, amplitudes.reshape(1, -1), cmap, admittance, in_hbm(row_near), in_hbm(row_far),
        y_lo, y_hi, x_near, x_far, ends_near, ends_far,
        wx, wy, wz, gain, wyl, wyh, u2, pulled1, keep1, pulled2, e_lo, e_hi, contact, zeta_t,
    )
    h_far = far(face_far)
    h_near = near(face_near)
    parts = spread(mine, h_near, groups)
    parts = lax.all_to_all(parts, "zx", 0, 0, tiled=True)
    to_above, to_below, summed = gathered(in_hbm(parts), in_hbm(edge_lo), in_hbm(edge_hi))
    base, pull, weight, row_weight = ready(
        summed, in_hbm(u2_inner), in_hbm(u2_outer), in_hbm(gain), in_hbm(wxf), in_hbm(misc), in_hbm(zeta_t)
    )
    e_lo = rotated(to_above, 1)
    e_hi = rotated(to_below, elecs - 1)
    own = blocks((e_lo, e_hi, summed, rotated(summed, 2)), (y_lo, y_hi, side, opposite), pull)
    got = near(own)
    out, volts = correct(cmap, own, got, base, pull, weight, row_weight, e_lo, e_hi, h_near, h_far)
    return out, volts


def solution(mesh):
    tile, src, elec = mesh.devices.shape
    cut = Mesh(mesh.devices.reshape(tile // 2, 2, src, elec), ("zx", "core", "src", "elec"))
    placed = (
        P("src", TILE, "elec", None),
        P("src", TILE, "elec", None),
        P(TILE, "elec", None),
        P(TILE, "elec"),
        P(),
        P("elec", None, None),
        P("src", None),
        P("src"),
    )
    return jax.shard_map(
        per_device,
        mesh=cut,
        in_specs=placed,
        out_specs=(P("src", TILE, "elec", None), P("src", "elec")),
        check_vma=False,
    )
```

```python
import jax
import jax.numpy as jnp
from jax import lax
from jax.experimental import pallas as pl
from jax.experimental.pallas import tpu as pltpu
from jax.sharding import Mesh
from jax.sharding import PartitionSpec as P

OMEGA = 0.8
KEEP = 1.0 - OMEGA
TINY = 1e-30
F32 = jnp.float32
EXACT = lax.Precision.HIGHEST
MIB = 1024 * 1024
TILE = ("zx", "core")

NT = (((1,), (1,)), ((), ()))


def params(mib):
    return pltpu.CompilerParams(vmem_limit_bytes=mib * MIB)


def vmem():
    return pl.BlockSpec(memory_space=pltpu.VMEM)


def hbm():
    return pl.BlockSpec(memory_space=pltpu.HBM)


def f32(*shape):
    return jax.ShapeDtypeStruct(shape, F32)


def kept(*shape):
    return pltpu.VMEM(shape, F32)


def stored(*shape):
    return pltpu.HBM(shape, F32)


def in_hbm(a):
    return pltpu.with_memory_space_constraint(a, pltpu.HBM)


def inverse(a):
    r = pl.reciprocal(a, approx=True)
    return r * (2.0 - a * r)


def face(a, b):
    return (2.0 * a * b) * inverse(a + b)


def outer_face(a, b):
    return (2.0 * a * b) * inverse(jnp.maximum(a + b, TINY))


def iota(shape, dim):
    return lax.broadcasted_iota(jnp.int32, shape, dim)


def shift_up(a, axis):
    return pltpu.roll(a, a.shape[axis] - 1, axis)


def shift_down(a, axis):
    return pltpu.roll(a, 1, axis)


def in_line(flux_weight, u, axis):
    return flux_weight * shift_up(u, axis) + shift_down(flux_weight * u, axis)


def line_weight(c, axis):
    w = face(c, shift_up(c, axis))
    return jnp.where(iota(c.shape, axis) < c.shape[axis] - 1, w, 0.0)


def both_sides(w, axis):
    return w + shift_down(w, axis)


def tile(k):
    return pl.ds(8 * k, 8)


def sweep(u_at, f_at, wy_at, wz_at, sides_at, emit):
    row = iota((8, 256), 0)
    here = [u_at(s, 0) for s in range(4)]
    rolled = [pltpu.roll(here[s], 7, 0) for s in range(4)]
    before = [None] * 4
    for k in range(16):
        wy = wy_at(k)
        wz = wz_at(k)
        weights_here = [weight(k) for weight, _ in sides_at]
        for s in range(4):
            u = here[s]
            up = rolled[s]
            if k < 15:
                here[s] = u_at(s, k + 1)
                rolled[s] = pltpu.roll(here[s], 7, 0)
                up = jnp.where(row == 7, rolled[s], up)
            down = pltpu.roll(wy * u, 1, 0)
            pulled = f_at(s, k) + wy * up
            pulled = pulled + jnp.where(row == 0, 0.0 if k == 0 else before[s], down)
            before[s] = down
            pulled = pulled + wz * shift_up(u, 1)
            pulled = pulled + shift_down(wz * u, 1)
            for weight, (_, neighbour) in zip(weights_here, sides_at):
                pulled = pulled + weight * neighbour(s, k)
            emit(s, k, u, pulled)


def fold(p):
    return p[:, :128] + p[:, 128:]


def row_sums(slabs):
    return folded_sums(jnp.concatenate([fold(p) for p in slabs], axis=0))


def folded_sums(folded):
    head = folded.astype(jnp.bfloat16)
    rest = (folded - head.astype(F32)).astype(jnp.bfloat16)
    ones = jnp.ones((8, 128), jnp.bfloat16)
    total = lax.dot_general(ones, head, NT, preferred_element_type=F32)
    total = total + lax.dot_general(ones, rest, NT, preferred_element_type=F32)
    return jnp.concatenate([total[0:1, 128 * s : 128 * s + 128] for s in range(4)], axis=0)


def to_lanes(column):
    mask = iota((8, 128), 0) == iota((8, 128), 1)
    return jnp.sum(jnp.where(mask, column, jnp.zeros_like(column)), axis=0, keepdims=True)


def gather_rows(ids, table):
    block = lax.shift_right_logical(ids, 7)
    lane = lax.bitwise_and(ids, 127)
    found = jnp.zeros(ids.shape, F32)
    for b in range(16):
        row = jnp.broadcast_to(table[b : b + 1], ids.shape)
        got = jnp.take_along_axis(row, lane, axis=1)
        found = jnp.where(block == b, got, found)
    return found


def scatter(id_rows, values):
    place = iota((64, 128), 0)
    block_of = 4 * ((place // 8) % 4) + 2 * (place // 32) + (place // 4) % 2
    total = jnp.zeros((192, 128), F32)
    for id_row, value in zip(id_rows, values):
        hit = lax.shift_right_logical(id_row, 7) == block_of
        spread = jnp.where(hit, jnp.concatenate([value] * 16, axis=0), 0.0)
        lane_hit = lax.bitwise_and(id_row, 127) == iota((128, 128), 0)
        onehot = jnp.where(lane_hit, 1.0, 0.0).astype(jnp.bfloat16)
        a = spread.astype(jnp.bfloat16)
        spread = spread - a.astype(F32)
        b = spread.astype(jnp.bfloat16)
        spread = spread - b.astype(F32)
        parts = jnp.concatenate([a, b, spread.astype(jnp.bfloat16)], axis=0)
        total = total + lax.dot_general(parts, onehot, NT, preferred_element_type=F32)
    return total[0:64] + total[64:128] + total[128:192]


ROW_C = 512
ROW_C2 = 640
ROW_MAP = 768
ROWS = 776


def sides():
    core = lax.axis_index("core")
    return 1 - core, core


def has_elecs():
    elec = lax.axis_index("elec")
    last = lax.axis_size("elec") - 1
    return jnp.where(elec > 0, 1.0, 0.0), jnp.where(elec < last, 1.0, 0.0)


def edges_kernel(
    u_hbm, c_hbm, imp_hbm, cmap_hbm, out_lo, out_hi, near_out, far_out, blocks, u, c, cmap, imp, side_by_side, sems, whole_sems
):
    core = lax.axis_index("core")
    copies = []
    for n, y in enumerate((0, 120)):
        copies.append(pltpu.make_async_copy(u_hbm.at[:, :, pl.ds(y, 8)], u.at[n], sems.at[2 * n]))
        copies.append(pltpu.make_async_copy(c_hbm.at[:, pl.ds(y, 8)], c.at[n], sems.at[2 * n + 1]))
    whole = []
    for n, (out, side) in enumerate(zip((near_out, far_out), sides())):
        for s in range(4):
            whole.append((u_hbm.at[s, 7 * side], out.at[pl.ds(128 * s, 128)], whole_sems.at[n, s]))
        whole.append((c_hbm.at[7 * side], out.at[pl.ds(ROW_C, 128)], whole_sems.at[n, 4]))
        whole.append((c_hbm.at[1 + 5 * side], out.at[pl.ds(ROW_C2, 128)], whole_sems.at[n, 5]))
    rows_of_blocks = [
        pltpu.make_async_copy(imp_hbm.at[2 * core + n], imp.at[n], whole_sems.at[n, 7]) for n in range(2)
    ]
    whole = [pltpu.make_async_copy(*copy) for copy in whole]
    copies.append(pltpu.make_async_copy(cmap_hbm, cmap, sems.at[4]))
    for copy in copies + rows_of_blocks + whole:
        copy.start()
    for copy in copies + rows_of_blocks:
        copy.wait()
    side_by_side[:, 0:128] = imp[0]
    side_by_side[:, 128:256] = imp[1]
    copy_blocks = pltpu.make_async_copy(side_by_side, blocks, sems.at[5])
    copy_blocks.start()
    for n, out, near, far, lane in ((0, out_lo, 0, 1, 0), (1, out_hi, 7, 6, 127)):
        out[56:184, 0:128] = imp[0]
        out[56:184, 128:256] = imp[1]
        for x in range(8):
            for s in range(4):
                out[8 * s + x : 8 * s + x + 1, :] = u[n, s, x, near : near + 1, :]
            out[32 + x : 33 + x, :] = c[n, x, near : near + 1, :]
            out[40 + x : 41 + x, :] = c[n, x, far : far + 1, :]
        out[48:56, :] = jnp.zeros((8, 256), F32)
        out[48:49, 0:128] = to_lanes(cmap[:, lane : lane + 1].astype(F32))
    for out, side in zip((near_out, far_out), sides()):
        out[ROW_MAP:ROWS, :] = jnp.zeros((8, 256), F32)
        out[ROW_MAP : ROW_MAP + 1, 0:128] = cmap[pl.ds(7 * side, 1), :].astype(F32)
    for copy in whole:
        copy.wait()
    copy_blocks.wait()


def edges(u, c, impedance, cmap):
    return pl.pallas_call(
        edges_kernel,
        in_specs=[hbm()] * 4,
        out_specs=[vmem()] * 4 + [hbm()],
        out_shape=[f32(184, 256), f32(184, 256), f32(ROWS, 256), f32(ROWS, 256), stored(128, 256)],
        scratch_shapes=[
            pltpu.VMEM((2, 4, 8, 8, 256), F32),
            pltpu.VMEM((2, 8, 8, 256), F32),
            pltpu.VMEM((8, 128), jnp.int32),
            pltpu.VMEM((2, 128, 128), F32),
            pltpu.VMEM((128, 256), F32),
            pltpu.SemaphoreType.DMA((6,)),
            pltpu.SemaphoreType.DMA((2, 8)),
        ],
        compiler_params=params(4),
        name="edges",
    )(u, c, impedance, cmap)


def corners_kernel(y_lo, y_hi, near_out, far_out):
    below, above = has_elecs()
    for out, side in zip((near_out, far_out), sides()):
        out[...] = jnp.zeros((8, 256), F32)
        out[0:1, :] = below * y_lo[pl.ds(32 + 7 * side, 1), :]
        out[1:2, :] = above * y_hi[pl.ds(32 + 7 * side, 1), :]


def corners(y_lo, y_hi):
    return pl.pallas_call(
        corners_kernel,
        in_specs=[vmem()] * 2,
        out_specs=[vmem()] * 2,
        out_shape=[f32(8, 256)] * 2,
        compiler_params=params(2),
        name="corners",
    )(y_lo, y_hi)


def weights_kernel(
    u_hbm, c_hbm, cmap_hbm, admittance_hbm, u, wx, wy, wz, diag, zeta_t, rim, c, cmap, admittance, sems, u_sems
):
    small = [
        pltpu.make_async_copy(cmap_hbm, cmap, sems.at[8]),
        pltpu.make_async_copy(admittance_hbm, admittance, sems.at[9]),
    ]
    rows = [pltpu.make_async_copy(c_hbm.at[x], c.at[x], sems.at[x]) for x in range(8)]
    later = [pltpu.make_async_copy(u_hbm.at[s], u.at[s], u_sems.at[s]) for s in range(4)]
    for copy in small + rows + later:
        copy.start()
    for copy in small:
        copy.wait()
    zeta = gather_rows(cmap[...], admittance[...])
    zeta_t[...] = jnp.transpose(jnp.concatenate([zeta, jnp.zeros((120, 128), F32)], axis=0))
    row = iota((8, 256), 0)
    last_lane = iota((8, 256), 1) == 255
    rows[0].wait()
    for x in range(8):
        if x < 7:
            rows[x + 1].wait()
        here = c[x, tile(0), :]
        rolled = pltpu.roll(here, 7, 0)
        before = None
        for k in range(16):
            up = rolled
            now = here
            if k < 15:
                here = c[x, tile(k + 1), :]
                rolled = pltpu.roll(here, 7, 0)
                up = jnp.where(row == 7, rolled, up)
            along_y = face(now, up)
            if k == 15:
                along_y = jnp.where(row == 7, 0.0, along_y)
            down = pltpu.roll(along_y, 1, 0)
            along_z = jnp.where(last_lane, 0.0, face(now, shift_up(now, 1)))
            total = along_y + jnp.where(row == 0, 0.0 if k == 0 else before, down)
            before = down
            total = total + along_z + shift_down(along_z, 1)
            total = total + zeta_t[tile(k), x : x + 1]
            if x < 7:
                along_x = face(now, c[x + 1, tile(k), :])
                wx[x, tile(k), :] = along_x
                total = total + along_x
            if x > 0:
                total = total + wx[x - 1, tile(k), :]
            wy[x, tile(k), :] = along_y
            wz[x, tile(k), :] = along_z
            diag[x, tile(k), :] = total
    rim[0] = c[0]
    rim[1] = c[7]
    for copy in later:
        copy.wait()


def weights(u, c, cmap, admittance):
    outs = [
        kept(4, 8, 128, 256),
        kept(7, 128, 256), kept(8, 128, 256), kept(8, 128, 256), kept(8, 128, 256), kept(128, 128),
        kept(2, 128, 256),
    ]
    return pl.pallas_call(
        weights_kernel,
        in_specs=[hbm()] * 4,
        out_specs=[vmem()] * len(outs),
        out_shape=outs,
        scratch_shapes=[
            pltpu.VMEM((8, 128, 256), F32),
            pltpu.VMEM((8, 128), jnp.int32),
            pltpu.VMEM((16, 128), F32),
            pltpu.SemaphoreType.DMA((10,)),
            pltpu.SemaphoreType.DMA((4,)),
        ],
        compiler_params=params(4),
        cost_estimate=pl.CostEstimate(flops=20_000_000, bytes_accessed=6_000_000, transcendentals=0),
        name="weights",
    )(u, c, cmap, admittance)


def inner_kernel(
    u, f_hbm, cmap, own_lo, own_hi, y_lo, y_hi, wx, wy, wz, diag,
    u2, u2_out, gain, wyl, wyh, pulled1, keep1, pulled2, edge_lo, edge_hi, contact,
    f, u1, sums, folded, middle, sems, f_sems,
):
    def row_of_f(x):
        return pltpu.make_async_copy(f_hbm.at[:, x], f.at[:, x], f_sems.at[x])

    for x in (1, 2, 3, 4, 5, 6, 0, 7):
        row_of_f(x).start()

    below, above = has_elecs()
    wyl[...] = outer_face(own_lo[32:40, :], below * y_lo[32:40, :])
    wyh[...] = outer_face(own_hi[32:40, :], above * y_hi[32:40, :])
    row = iota((8, 256), 0)
    for x in range(8):
        for k in range(16):
            total = diag[x, tile(k), :]
            if k == 0:
                total = total + jnp.where(row == 0, wyl[x : x + 1, :], 0.0)
            if k == 15:
                total = total + jnp.where(row == 7, wyh[x : x + 1, :], 0.0)
            gain[x, tile(k), :] = total if x in (0, 7) else OMEGA * inverse(total)

    def with_halos(pulled, s, k, x):
        at = 8 * s + x
        if k == 0:
            pulled = pulled + jnp.where(row == 0, wyl[pl.ds(x, 1), :] * y_lo[pl.ds(at, 1), :], 0.0)
        if k == 15:
            pulled = pulled + jnp.where(row == 7, wyh[pl.ds(x, 1), :] * y_hi[pl.ds(at, 1), :], 0.0)
        return pulled

    def first(x, carry):
        row_of_f(x).wait()

        def emit(s, k, here, pulled):
            new = KEEP * here + gain[x, tile(k), :] * with_halos(pulled, s, k, x)
            u1[s, x, tile(k), :] = new
            if k == 0:
                edge_lo[pl.ds(8 * s + x, 1), :] = new[0:1]
            if k == 15:
                edge_hi[pl.ds(8 * s + x, 1), :] = new[7:8]

        sweep(
            lambda s, k: u[s, x, tile(k), :],
            lambda s, k: f[s, x, tile(k), :],
            lambda k: wy[x, tile(k), :],
            lambda k: wz[x, tile(k), :],
            [
                (lambda k: wx[x - 1, tile(k), :], lambda s, k: u[s, x - 1, tile(k), :]),
                (lambda k: wx[x, tile(k), :], lambda s, k: u[s, x + 1, tile(k), :]),
            ],
            emit,
        )
        return carry

    lax.fori_loop(1, 7, first, 0)
    row_of_f(0).wait()
    row_of_f(7).wait()

    def rim(n, carry):
        x = 7 * n
        inside = 1 + 5 * n

        def emit(s, k, here, pulled):
            pulled1[n, s, tile(k), :] = with_halos(pulled, s, k, x)
            keep1[n, s, tile(k), :] = KEEP * here
            pulled2[n, s, tile(k), :] = f[s, x, tile(k), :] + wx[6 * n, tile(k), :] * u1[s, inside, tile(k), :]

        sweep(
            lambda s, k: u[s, x, tile(k), :],
            lambda s, k: f[s, x, tile(k), :],
            lambda k: wy[x, tile(k), :],
            lambda k: wz[x, tile(k), :],
            [(lambda k: wx[6 * n, tile(k), :], lambda s, k: u[s, inside, tile(k), :])],
            emit,
        )
        return carry

    lax.fori_loop(0, 2, rim, 0)

    def second(x, sides_at, target):
        def emit(s, k, here, pulled):
            new = KEEP * here + gain[x, tile(k), :] * pulled
            target[s, tile(k), :] = new
            folded[pl.ds(128 * s + 8 * k, 8), :] = fold(new)

        sweep(
            lambda s, k: u1[s, x, tile(k), :],
            lambda s, k: f[s, x, tile(k), :],
            lambda k: wy[x, tile(k), :],
            lambda k: wz[x, tile(k), :],
            sides_at,
            emit,
        )

    def below_at(x):
        return (lambda k: wx[x - 1, tile(k), :], lambda s, k: u1[s, x - 1, tile(k), :])

    def above_at(x):
        return (lambda k: wx[x, tile(k), :], lambda s, k: u1[s, x + 1, tile(k), :])

    def second_middle(x, carry):
        sums[x - 1] = folded_sums(folded[...])
        second(x, [below_at(x), above_at(x)], middle.at[x - 2])
        pltpu.make_async_copy(middle.at[x - 2], u2_out.at[:, x - 2], sems.at[x - 2]).start()
        return carry

    second(1, [above_at(1)], u2.at[0])
    lax.fori_loop(2, 6, second_middle, 0)
    sums[5] = folded_sums(folded[...])
    second(6, [below_at(6)], u2.at[1])
    sums[6] = folded_sums(folded[...])
    contact[...] = scatter([cmap[x : x + 1, :] for x in range(1, 7)], [sums[x] for x in range(1, 7)])
    for n in range(4):
        pltpu.make_async_copy(middle.at[n], u2_out.at[:, n], sems.at[n]).wait()


def inner(u, f, cmap, own_lo, own_hi, y_lo, y_hi, wx, wy, wz, diag):
    outs = [
        kept(2, 4, 128, 256), stored(4, 4, 128, 256), kept(8, 128, 256), kept(8, 256), kept(8, 256),
        kept(2, 4, 128, 256), kept(2, 4, 128, 256), kept(2, 4, 128, 256),
        kept(32, 256), kept(32, 256), kept(64, 128),
    ]
    return pl.pallas_call(
        inner_kernel,
        in_specs=[vmem(), hbm()] + [vmem()] * 9,
        out_specs=[vmem(), hbm()] + [vmem()] * (len(outs) - 2),
        out_shape=outs,
        scratch_shapes=[
            pltpu.VMEM((4, 8, 128, 256), F32),
            pltpu.VMEM((4, 8, 128, 256), F32),
            pltpu.VMEM((8, 4, 128), F32),
            pltpu.VMEM((512, 128), F32),
            pltpu.VMEM((4, 4, 128, 256), F32),
            pltpu.SemaphoreType.DMA((4,)),
            pltpu.SemaphoreType.DMA((8,)),
        ],
        compiler_params=params(16),
        cost_estimate=pl.CostEstimate(flops=100_000_000, bytes_accessed=25_000_000, transcendentals=0),
        name="inner",
    )(u, f, cmap, own_lo, own_hi, y_lo, y_hi, wx, wy, wz, diag)


def outer_kernel(
    pairs, amplitudes, cmap, admittance, rim, y_lo, y_hi, x_near, x_far, ends_near, ends_far,
    wx, wy, wz, gain, wyl, wyh, u2, pulled1, keep1, pulled2, e_lo, e_hi, contact, zeta_in,
    face_near_out, face_far_out, edge_lo_out, edge_hi_out, u2_out, gain_out, wxf_out, misc_out, zeta_out, mine, other,
    ids, face_near, face_far, edge_lo, edge_hi, u2b, gain_b, wxf, misc, folded, sems, u2_sems, edge_sems,
):
    copies = []

    def send(source, target, sem):
        copy = pltpu.make_async_copy(source, target, sem)
        copy.start()
        copies.append(copy)

    send(gain.at[pl.ds(1, 6)], gain_out.at[pl.ds(1, 6)], sems.at[0])
    send(zeta_in, zeta_out, sems.at[1])
    misc[0:8, :] = wyl[...]
    misc[8:16, :] = wyh[...]
    send(misc, misc_out, sems.at[3])
    ids[0:8, :] = jnp.full((8, 128), 2048, jnp.int32)
    ids[0:1, :] = x_near[ROW_MAP : ROW_MAP + 1, 0:128].astype(jnp.int32)
    ids[1:2, :] = x_far[ROW_MAP : ROW_MAP + 1, 0:128].astype(jnp.int32)
    lanes = iota((1, 128), 1)
    low_ids = y_lo[48:49, 0:128].astype(jnp.int32)
    high_ids = pltpu.roll(y_hi[48:49, 0:128], 8, 1).astype(jnp.int32)
    ids[2:3, :] = jnp.where(lanes < 8, low_ids, jnp.where(lanes < 16, high_ids, 2048))
    zeta = gather_rows(ids[...], admittance[...])
    zeta_t = jnp.transpose(jnp.concatenate([zeta, jnp.zeros((120, 128), F32)], axis=0))
    row = iota((128, 256), 0)

    id_rows = []
    values = []
    for n, (side, msg, ends, out, sent) in enumerate(
        zip(sides(), (x_near, x_far), (ends_near, ends_far), (face_near, face_far), (face_near_out, face_far_out))
    ):
        x = 7 * side
        there = msg[ROW_C : ROW_C + 128, :]
        outside = outer_face(rim[side], there)
        wxf[n] = outside
        g = OMEGA * inverse(gain[x] + outside)
        gain_b[n] = g
        for s in range(4):
            out[s] = keep1[side, s] + g * (pulled1[side, s] + outside * msg[128 * s : 128 * s + 128, :])
        send(out, sent, sems.at[4 + n])
        send(gain_b.at[n], gain_out.at[x], sems.at[6 + n])
        spare = jnp.maximum(there, TINY)
        diag = both_sides(line_weight(spare, 0), 0) + both_sides(line_weight(spare, 1), 1) + zeta_t[:, n : n + 1]
        diag = diag + outside + outer_face(there, msg[ROW_C2 : ROW_C2 + 128, :])
        diag = diag + jnp.where(row == 0, outer_face(there[0:1], ends[0:1, :]), 0.0)
        diag = diag + jnp.where(row == 127, outer_face(there[127:128], ends[1:2, :]), 0.0)
        factor = OMEGA * outside * inverse(jnp.maximum(diag, TINY))
        id_rows.append(ids[n : n + 1, :])
        values.append(row_sums([factor * out[s] for s in range(4)]))
        inside = 1 + 5 * side
        factor = gain[inside] * wx[6 * side]
        slabs = []
        for s in range(4):
            new = factor * out[s]
            u2b[2 * n + 1, s] = u2[side, s] + new
            slabs.append(new)
        send(u2b.at[2 * n + 1], u2_out.at[2 * side + 1], u2_sems.at[2 * n + 1])
        id_rows.append(cmap[pl.ds(inside, 1), :])
        values.append(row_sums(slabs))
        def emit(s, k, here, pulled, n=n):
            new = KEEP * here + gain_b[n, tile(k), :] * pulled
            u2b[2 * n, s, tile(k), :] = new
            folded[pl.ds(128 * s + 8 * k, 8), :] = fold(new)

        sweep(
            lambda s, k, out=out: out[s, tile(k), :],
            lambda s, k, side=side: pulled2[side, s, tile(k), :],
            lambda k, x=x: wy[x, tile(k), :],
            lambda k, x=x: wz[x, tile(k), :],
            [],
            emit,
        )
        send(u2b.at[2 * n], u2_out.at[2 * side], u2_sems.at[2 * n])
        id_rows.append(cmap[pl.ds(x, 1), :])
        values.append(folded_sums(folded[...]))

    send(wxf, wxf_out, sems.at[8])

    edge_sums = jnp.zeros((4, 128), F32)
    for n, (msg, own, inside, edge, y, sent) in enumerate(
        ((y_lo, wyl, e_lo, edge_lo, 0, edge_lo_out), (y_hi, wyh, e_hi, edge_hi, 127, edge_hi_out))
    ):
        edge[0:32, :] = inside[...]
        for s in range(4):
            for side, out in zip(sides(), (face_near, face_far)):
                edge[pl.ds(8 * s + 7 * side, 1), :] = out[s, y : y + 1, :]
        send(edge, sent, edge_sems.at[n])
        there = msg[32:40, :]
        x_rows = iota((8, 256), 0)
        spare = jnp.maximum(there, TINY)
        diag = both_sides(line_weight(spare, 0), 0) + both_sides(line_weight(spare, 1), 1) + own[...]
        diag = diag + outer_face(there, msg[40:48, :])
        for side, ends in zip(sides(), (ends_near, ends_far)):
            diag = diag + jnp.where(x_rows == 7 * side, outer_face(there, ends[n : n + 1, :]), 0.0)
        diag = diag + zeta_t[8 * n : 8 * n + 8, 2:3]
        factor = OMEGA * own[...] * inverse(jnp.maximum(diag, TINY))
        lined = []
        for s in range(4):
            line = to_lanes(jnp.sum(factor * edge[8 * s : 8 * s + 8, :], axis=1, keepdims=True))
            lined.append(pltpu.roll(line, 8 * n, 1) if n else line)
        edge_sums = edge_sums + jnp.concatenate(lined, axis=0)
    id_rows.append(ids[2:3, :])
    values.append(edge_sums)

    total = (contact[...] + scatter(id_rows, values)) * (1.0 / 256.0)
    place = iota((64, 128), 0)
    electrode = (4 * ((place // 8) % 4) + 2 * (place // 32) + (place // 4) % 2) * 128 + iota((64, 128), 1)
    adds = jnp.logical_and(lax.axis_index("zx") == 0, lax.axis_index("elec") == 0)
    adds = jnp.logical_and(adds, lax.axis_index("core") == 0)
    for s in range(4):
        at = place % 4 == s
        amount = jnp.where(adds, amplitudes[0:1, s : s + 1], 0.0)
        total = total + jnp.where(at & (electrode == pairs[0:1, s : s + 1]), amount, 0.0)
        total = total - jnp.where(at & (electrode == pairs[1:2, s : s + 1]), amount, 0.0)
    first_half = lax.axis_index("core") == 0
    mine[...] = jnp.where(first_half, total[0:32], total[32:64])
    other[...] = jnp.where(first_half, total[32:64], total[0:32])
    for copy in copies:
        copy.wait()


def outer(pairs, amplitudes, *args):
    outs = [
        stored(4, 128, 256), stored(4, 128, 256), stored(32, 256), stored(32, 256),
        stored(4, 4, 128, 256), stored(8, 128, 256), stored(2, 128, 256), stored(16, 256), stored(128, 128),
        f32(32, 128), f32(32, 128),
    ]
    return pl.pallas_call(
        outer_kernel,
        in_specs=[vmem()] * (2 + len(args)),
        out_specs=[hbm()] * 9 + [vmem()] * 2,
        out_shape=outs,
        scratch_shapes=[
            pltpu.VMEM((8, 128), jnp.int32),
            pltpu.VMEM((4, 128, 256), F32),
            pltpu.VMEM((4, 128, 256), F32),
            pltpu.VMEM((32, 256), F32),
            pltpu.VMEM((32, 256), F32),
            pltpu.VMEM((4, 4, 128, 256), F32),
            pltpu.VMEM((2, 128, 256), F32),
            pltpu.VMEM((2, 128, 256), F32),
            pltpu.VMEM((16, 256), F32),
            pltpu.VMEM((512, 128), F32),
            pltpu.SemaphoreType.DMA((9,)),
            pltpu.SemaphoreType.DMA((4,)),
            pltpu.SemaphoreType.DMA((2,)),
        ],
        compiler_params=params(32),
        cost_estimate=pl.CostEstimate(flops=50_000_000, bytes_accessed=15_000_000, transcendentals=0),
        name="outer",
    )(pairs, amplitudes, *args)


def spread_kernel(mine, got, out, both, sems):
    both[...] = mine[...] + got[...]
    copies = [pltpu.make_async_copy(both, out.at[n], sems.at[n]) for n in range(out.shape[0])]
    for copy in copies:
        copy.start()
    for copy in copies:
        copy.wait()


def spread(mine, got, count):
    return pl.pallas_call(
        spread_kernel,
        in_specs=[vmem()] * 2,
        out_specs=hbm(),
        out_shape=stored(count, 32, 128),
        scratch_shapes=[pltpu.VMEM((32, 128), F32), pltpu.SemaphoreType.DMA((count,))],
        compiler_params=params(2),
        name="spread",
    )(mine, got)


def gathered_kernel(parts_hbm, edge_lo, edge_hi, to_above, to_below, out, parts, sems, edge_sems):
    copies = [pltpu.make_async_copy(parts_hbm.at[n], parts.at[n], sems.at[n]) for n in range(parts.shape[0])]
    for n, (source, target) in enumerate(((edge_hi, to_above), (edge_lo, to_below))):
        copies.append(pltpu.make_async_copy(source, target.at[pl.ds(16, 32)], edge_sems.at[n]))
    for copy in copies:
        copy.start()
    for copy in copies:
        copy.wait()
    total = jnp.sum(parts[...], axis=0)
    for target in (out, to_above, to_below):
        target[0:16, 0:128] = total[0:16]
        target[0:16, 128:256] = total[16:32]


def gathered(parts, edge_lo, edge_hi):
    return pl.pallas_call(
        gathered_kernel,
        in_specs=[pl.BlockSpec(memory_space=pl.ANY)] + [hbm()] * 2,
        out_specs=[vmem()] * 3,
        out_shape=[f32(48, 256), f32(48, 256), f32(16, 256)],
        scratch_shapes=[
            pltpu.VMEM(parts.shape, F32),
            pltpu.SemaphoreType.DMA((parts.shape[0],)),
            pltpu.SemaphoreType.DMA((2,)),
        ],
        compiler_params=params(4),
        name="gathered",
    )(parts, edge_lo, edge_hi)


def blocks_kernel(a0, a1, a2, a3, i0, i1, i2, i3, pull, out, charges):
    elec = lax.axis_index("elec")
    total = a0[0:16, :] + a1[0:16, :] + a2[...] + a3[0:16, :]
    for e in range(4):
        charges[e] = total[8 * (e % 2) : 8 * (e % 2) + 8, 128 * (e // 2) : 128 * (e // 2) + 128]
    upper = iota((8, 128), 0) < 4
    for turn, blocks in ((3, i0), (1, i1), (0, i2), (2, i3)):
        e = lax.rem(elec + turn, 4)
        charge = charges[e]
        start = blocks.shape[0] - 128
        both = blocks[start : start + 128, :]
        first = lax.dot_general(charge, both[:, 0:128], NT, precision=EXACT, preferred_element_type=F32)
        second = lax.dot_general(charge, both[:, 128:256], NT, precision=EXACT, preferred_element_type=F32)
        out[e] = jnp.where(upper, first, second)


def blocks(parts, impedances, pull):
    return pl.pallas_call(
        blocks_kernel,
        in_specs=[vmem()] * 8 + [pl.BlockSpec(memory_space=pl.ANY)],
        out_specs=vmem(),
        out_shape=f32(4, 8, 128),
        scratch_shapes=[pltpu.VMEM((4, 8, 128), F32)],
        compiler_params=params(4),
        name="blocks",
    )(*parts, *impedances, pull)


def ready_kernel(
    after, inner_hbm, outer_hbm, gain_hbm, wxf_hbm, misc_hbm, zeta_hbm, base, pull, sides_out, rows_out,
    gain, wxf, misc, zeta_t, sems, small_sems,
):
    order = (2, 3, 4, 5, 1, 6, 0, 7)
    rows = {x: inner_hbm.at[:, x - 2] for x in range(2, 6)}
    rows.update({x: outer_hbm.at[n] for n, x in enumerate((0, 1, 7, 6))})
    copies = {x: pltpu.make_async_copy(rows[x], base.at[:, x], sems.at[x]) for x in order}
    small = [
        pltpu.make_async_copy(source, target, small_sems.at[n])
        for n, (source, target) in enumerate(
            ((zeta_hbm, zeta_t), (misc_hbm, misc), (gain_hbm, gain), (wxf_hbm, wxf))
        )
    ]
    for copy in small:
        copy.start()
    for x in order:
        copies[x].start()
    for copy in small:
        copy.wait()
    for x in order:
        g = gain[x]
        part = (1.0 / OMEGA) * zeta_t[:, x : x + 1] * g
        pull[x] = part
        sides_out[x : x + 1, :] = (1.0 - part[0:1]) * g[0:1] * misc[x : x + 1, :]
        sides_out[8 + x : 9 + x, :] = (1.0 - part[127:128]) * g[127:128] * misc[8 + x : 9 + x, :]
        copies[x].wait()
        if x in (0, 7):
            n = jnp.where(sides()[0] == x // 7, 0, 1)
            rows_out[x // 7] = (1.0 - part) * g * wxf[n]
        for s in range(4):
            u = base[s, x]
            base[s, x] = u - part * u


def ready(*args):
    return pl.pallas_call(
        ready_kernel,
        in_specs=[pl.BlockSpec(memory_space=pl.ANY)] + [hbm()] * 6,
        out_specs=[vmem()] * 4,
        out_shape=[kept(4, 8, 128, 256), kept(8, 128, 256), kept(16, 256), kept(2, 128, 256)],
        scratch_shapes=[
            pltpu.VMEM((8, 128, 256), F32),
            pltpu.VMEM((2, 128, 256), F32),
            pltpu.VMEM((16, 256), F32),
            pltpu.VMEM((128, 128), F32),
            pltpu.SemaphoreType.DMA((8,)),
            pltpu.SemaphoreType.DMA((4,)),
        ],
        compiler_params=params(8),
        cost_estimate=pl.CostEstimate(flops=10_000_000, bytes_accessed=8_000_000, transcendentals=0),
        name="ready",
    )(*args)


def correct_kernel(
    cmap, own, got, base, pull, weight, row_weight, e_lo, e_hi, h_near, h_far, out_hbm, volts, table, buf, sems
):
    core = lax.axis_index("core")
    elec = lax.axis_index("elec")
    table[core] = own[...]
    table[1 - core] = got[...]
    for h in range(2):
        for j in range(2):
            volts[:, 128 * (2 * h + j) : 128 * (2 * h + j) + 128] = table[h, elec, 4 * j : 4 * j + 4, :]
    ids = cmap[...]
    block = lax.shift_right_logical(ids, 7)
    lane = lax.bitwise_and(ids, 127)
    touched = []
    for s in range(4):
        found = jnp.zeros((8, 128), F32)
        for b in range(16):
            e, h, j = b // 4, (b // 2) % 2, b % 2
            row = jnp.broadcast_to(table[h, e, 4 * j + s : 4 * j + s + 1, :], (8, 128))
            found = jnp.where(block == b, jnp.take_along_axis(row, lane, axis=1), found)
        touched.append(found)
    stacked = jnp.concatenate(touched + [jnp.zeros((96, 128), F32)], axis=0)
    volts_t = jnp.transpose(stacked)
    copies = []
    near_side = sides()[0]
    for x in (1, 2, 3, 4, 5, 6, 0, 7):
        for s in range(4):
            at = 8 * s + x
            new = base[s, x] + pull[x] * volts_t[:, at : at + 1]
            if x in (0, 7):
                halo = jnp.where(near_side == x // 7, h_near[s], h_far[s])
                new = new + row_weight[x // 7] * halo
            buf[s, x] = new
            low = weight[x : x + 1, :] * e_lo[16 + at : 17 + at, :]
            high = weight[8 + x : 9 + x, :] * e_hi[16 + at : 17 + at, :]
            buf[s, x, 0:1, :] = buf[s, x, 0:1, :] + low
            buf[s, x, 127:128, :] = buf[s, x, 127:128, :] + high
        copy = pltpu.make_async_copy(buf.at[:, x], out_hbm.at[:, x], sems.at[x])
        copy.start()
        copies.append(copy)
    for copy in copies:
        copy.wait()


def correct(*args):
    return pl.pallas_call(
        correct_kernel,
        in_specs=[vmem()] * 11,
        out_specs=[hbm(), vmem()],
        out_shape=[f32(4, 8, 128, 256), f32(4, 512)],
        scratch_shapes=[
            pltpu.VMEM((2, 4, 8, 128), F32),
            pltpu.VMEM((4, 8, 128, 256), F32),
            pltpu.SemaphoreType.DMA((8,)),
        ],
        compiler_params=params(8),
        name="correct",
    )(*args)


def per_device(u, f, c, cmap, admittance, impedance, pairs, amplitudes):
    tiles = lax.axis_size(TILE)
    groups = lax.axis_size("zx")
    elecs = lax.axis_size("elec")
    admittance = admittance.reshape(16, 128)
    u, f, c, impedance = in_hbm(u), in_hbm(f), in_hbm(c), in_hbm(impedance)

    def rotated(a, turn):
        return lax.ppermute(a, "elec", [(i, (i + turn) % elecs) for i in range(elecs)])

    def near(a):
        return lax.ppermute(a, "core", [(0, 1), (1, 0)])

    def far(a):
        pairs = [(i, i + 1) for i in range(1, tiles - 1, 2)]
        return lax.ppermute(a, TILE, pairs + [(j, i) for i, j in pairs])

    own_lo, own_hi, row_near, row_far, side = edges(u, c, impedance, in_hbm(cmap))
    y_lo = rotated(own_hi, 1)
    y_hi = rotated(own_lo, elecs - 1)
    x_far = far(row_far)
    x_near = near(row_near)
    opposite = rotated(side, 2)
    ends_near, ends_far = corners(y_lo, y_hi)
    ends_far = far(ends_far)
    ends_near = near(ends_near)

    u, wx, wy, wz, diag, zeta_t, rim = weights(u, c, in_hbm(cmap), in_hbm(admittance))
    u2, u2_inner, gain, wyl, wyh, pulled1, keep1, pulled2, e_lo, e_hi, contact = inner(
        u, f, cmap, own_lo, own_hi, y_lo, y_hi, wx, wy, wz, diag
    )
    face_near, face_far, edge_lo, edge_hi, u2_outer, gain, wxf, misc, zeta_t, mine, other = outer(
        pairs.T, amplitudes.reshape(1, -1), cmap, admittance, rim, y_lo, y_hi, x_near, x_far, ends_near, ends_far,
        wx, wy, wz, gain, wyl, wyh, u2, pulled1, keep1, pulled2, e_lo, e_hi, contact, zeta_t,
    )
    h_far = far(face_far)
    h_near = near(face_near)
    parts = spread(mine, near(other), groups)
    parts = lax.all_to_all(parts, "zx", 0, 0, tiled=True)
    to_above, to_below, summed = gathered(parts, in_hbm(edge_lo), in_hbm(edge_hi))
    base, pull, weight, row_weight = ready(
        summed, in_hbm(u2_inner), in_hbm(u2_outer), in_hbm(gain), in_hbm(wxf), in_hbm(misc), in_hbm(zeta_t)
    )
    e_lo = rotated(to_above, 1)
    e_hi = rotated(to_below, elecs - 1)
    own = blocks((e_lo, e_hi, summed, rotated(summed, 2)), (y_lo, y_hi, side, opposite), pull)
    got = near(own)
    out, volts = correct(cmap, own, got, base, pull, weight, row_weight, e_lo, e_hi, h_near, h_far)
    return out, volts


def solution(mesh):
    tile, src, elec = mesh.devices.shape
    cut = Mesh(mesh.devices.reshape(tile // 2, 2, src, elec), ("zx", "core", "src", "elec"))
    placed = (
        P("src", TILE, "elec", None),
        P("src", TILE, "elec", None),
        P(TILE, "elec", None),
        P(TILE, "elec"),
        P(),
        P("elec", None, None),
        P("src", None),
        P("src"),
    )
    return jax.shard_map(
        per_device,
        mesh=cut,
        in_specs=placed,
        out_specs=(P("src", TILE, "elec", None), P("src", "elec")),
        check_vma=False,
    )
```

```python
import jax
import jax.numpy as jnp
from jax import lax
from jax.experimental import pallas as pl
from jax.experimental.pallas import tpu as pltpu
from jax.sharding import Mesh
from jax.sharding import PartitionSpec as P

OMEGA = 0.8
KEEP = 1.0 - OMEGA
TINY = 1e-30
F32 = jnp.float32
EXACT = lax.Precision.HIGHEST
MIB = 1024 * 1024
TILE = ("zx", "core")

NT = (((1,), (1,)), ((), ()))


def params(mib):
    return pltpu.CompilerParams(vmem_limit_bytes=mib * MIB)


def vmem():
    return pl.BlockSpec(memory_space=pltpu.VMEM)


def hbm():
    return pl.BlockSpec(memory_space=pltpu.HBM)


def f32(*shape):
    return jax.ShapeDtypeStruct(shape, F32)


def kept(*shape):
    return pltpu.VMEM(shape, F32)


def stored(*shape):
    return pltpu.HBM(shape, F32)


def in_hbm(a):
    return pltpu.with_memory_space_constraint(a, pltpu.HBM)


def inverse(a):
    r = pl.reciprocal(a, approx=True)
    return r * (2.0 - a * r)


def face(a, b):
    return (2.0 * a * b) * inverse(a + b)


def outer_face(a, b):
    return (2.0 * a * b) * inverse(jnp.maximum(a + b, TINY))


def iota(shape, dim):
    return lax.broadcasted_iota(jnp.int32, shape, dim)


def shift_up(a, axis):
    return pltpu.roll(a, a.shape[axis] - 1, axis)


def shift_down(a, axis):
    return pltpu.roll(a, 1, axis)


def in_line(flux_weight, u, axis):
    return flux_weight * shift_up(u, axis) + shift_down(flux_weight * u, axis)


def line_weight(c, axis):
    w = face(c, shift_up(c, axis))
    return jnp.where(iota(c.shape, axis) < c.shape[axis] - 1, w, 0.0)


def both_sides(w, axis):
    return w + shift_down(w, axis)


def tile(k):
    return pl.ds(8 * k, 8)


def sweep(u_at, f_at, wy_at, wz_at, sides_at, emit):
    row = iota((8, 256), 0)
    here = [u_at(s, 0) for s in range(4)]
    rolled = [pltpu.roll(here[s], 7, 0) for s in range(4)]
    before = [None] * 4
    for k in range(16):
        wy = wy_at(k)
        wz = wz_at(k)
        weights_here = [weight(k) for weight, _ in sides_at]
        for s in range(4):
            u = here[s]
            up = rolled[s]
            if k < 15:
                here[s] = u_at(s, k + 1)
                rolled[s] = pltpu.roll(here[s], 7, 0)
                up = jnp.where(row == 7, rolled[s], up)
            down = pltpu.roll(wy * u, 1, 0)
            pulled = f_at(s, k) + wy * up
            pulled = pulled + jnp.where(row == 0, 0.0 if k == 0 else before[s], down)
            before[s] = down
            pulled = pulled + wz * shift_up(u, 1)
            pulled = pulled + shift_down(wz * u, 1)
            for weight, (_, neighbour) in zip(weights_here, sides_at):
                pulled = pulled + weight * neighbour(s, k)
            emit(s, k, u, pulled)


def fold(p):
    return p[:, :128] + p[:, 128:]


def row_sums(slabs):
    return folded_sums(jnp.concatenate([fold(p) for p in slabs], axis=0))


def folded_sums(folded):
    head = folded.astype(jnp.bfloat16)
    rest = (folded - head.astype(F32)).astype(jnp.bfloat16)
    ones = jnp.ones((8, 128), jnp.bfloat16)
    total = lax.dot_general(ones, head, NT, preferred_element_type=F32)
    total = total + lax.dot_general(ones, rest, NT, preferred_element_type=F32)
    return jnp.concatenate([total[0:1, 128 * s : 128 * s + 128] for s in range(4)], axis=0)


def to_lanes(column):
    mask = iota((8, 128), 0) == iota((8, 128), 1)
    return jnp.sum(jnp.where(mask, column, jnp.zeros_like(column)), axis=0, keepdims=True)


def gather_rows(ids, table):
    block = lax.shift_right_logical(ids, 7)
    lane = lax.bitwise_and(ids, 127)
    found = jnp.zeros(ids.shape, F32)
    for b in range(16):
        row = jnp.broadcast_to(table[b : b + 1], ids.shape)
        got = jnp.take_along_axis(row, lane, axis=1)
        found = jnp.where(block == b, got, found)
    return found


def scatter(id_rows, values):
    place = iota((64, 128), 0)
    block_of = 4 * ((place // 8) % 4) + 2 * (place // 32) + (place // 4) % 2
    total = jnp.zeros((128, 128), F32)
    for id_row, value in zip(id_rows, values):
        hit = lax.shift_right_logical(id_row, 7) == block_of
        spread = jnp.where(hit, jnp.concatenate([value] * 16, axis=0), 0.0)
        lane_hit = lax.bitwise_and(id_row, 127) == iota((128, 128), 0)
        onehot = jnp.where(lane_hit, 1.0, 0.0).astype(jnp.bfloat16)
        a = spread.astype(jnp.bfloat16)
        b = (spread - a.astype(F32)).astype(jnp.bfloat16)
        parts = jnp.concatenate([a, b], axis=0)
        total = total + lax.dot_general(parts, onehot, NT, preferred_element_type=F32)
    return total[0:64] + total[64:128]


ROW_C = 512
ROW_C2 = 640
ROW_MAP = 768
ROWS = 776


def sides():
    core = lax.axis_index("core")
    return 1 - core, core


def has_elecs():
    elec = lax.axis_index("elec")
    last = lax.axis_size("elec") - 1
    return jnp.where(elec > 0, 1.0, 0.0), jnp.where(elec < last, 1.0, 0.0)


def edges_kernel(
    u_hbm, c_hbm, imp_hbm, cmap_hbm, out_lo, out_hi, near_out, far_out, blocks, u, c, cmap, imp, side_by_side, sems, whole_sems
):
    core = lax.axis_index("core")
    copies = []
    for n, y in enumerate((0, 120)):
        copies.append(pltpu.make_async_copy(u_hbm.at[:, :, pl.ds(y, 8)], u.at[n], sems.at[2 * n]))
        copies.append(pltpu.make_async_copy(c_hbm.at[:, pl.ds(y, 8)], c.at[n], sems.at[2 * n + 1]))
    whole = []
    for n, (out, side) in enumerate(zip((near_out, far_out), sides())):
        for s in range(4):
            whole.append((u_hbm.at[s, 7 * side], out.at[pl.ds(128 * s, 128)], whole_sems.at[n, s]))
        whole.append((c_hbm.at[7 * side], out.at[pl.ds(ROW_C, 128)], whole_sems.at[n, 4]))
        whole.append((c_hbm.at[1 + 5 * side], out.at[pl.ds(ROW_C2, 128)], whole_sems.at[n, 5]))
    rows_of_blocks = [
        pltpu.make_async_copy(imp_hbm.at[2 * core + n], imp.at[n], whole_sems.at[n, 7]) for n in range(2)
    ]
    whole = [pltpu.make_async_copy(*copy) for copy in whole]
    copies.append(pltpu.make_async_copy(cmap_hbm, cmap, sems.at[4]))
    for copy in copies + rows_of_blocks + whole:
        copy.start()
    for copy in copies + rows_of_blocks:
        copy.wait()
    side_by_side[:, 0:128] = imp[0]
    side_by_side[:, 128:256] = imp[1]
    copy_blocks = pltpu.make_async_copy(side_by_side, blocks, sems.at[5])
    copy_blocks.start()
    for n, out, near, far, lane in ((0, out_lo, 0, 1, 0), (1, out_hi, 7, 6, 127)):
        out[56:184, 0:128] = imp[0]
        out[56:184, 128:256] = imp[1]
        for x in range(8):
            for s in range(4):
                out[8 * s + x : 8 * s + x + 1, :] = u[n, s, x, near : near + 1, :]
            out[32 + x : 33 + x, :] = c[n, x, near : near + 1, :]
            out[40 + x : 41 + x, :] = c[n, x, far : far + 1, :]
        out[48:56, :] = jnp.zeros((8, 256), F32)
        out[48:49, 0:128] = to_lanes(cmap[:, lane : lane + 1].astype(F32))
    for out, side in zip((near_out, far_out), sides()):
        out[ROW_MAP:ROWS, :] = jnp.zeros((8, 256), F32)
        out[ROW_MAP : ROW_MAP + 1, 0:128] = cmap[pl.ds(7 * side, 1), :].astype(F32)
    for copy in whole:
        copy.wait()
    copy_blocks.wait()


def edges(u, c, impedance, cmap):
    return pl.pallas_call(
        edges_kernel,
        in_specs=[hbm()] * 4,
        out_specs=[vmem()] * 4 + [hbm()],
        out_shape=[f32(184, 256), f32(184, 256), f32(ROWS, 256), f32(ROWS, 256), stored(128, 256)],
        scratch_shapes=[
            pltpu.VMEM((2, 4, 8, 8, 256), F32),
            pltpu.VMEM((2, 8, 8, 256), F32),
            pltpu.VMEM((8, 128), jnp.int32),
            pltpu.VMEM((2, 128, 128), F32),
            pltpu.VMEM((128, 256), F32),
            pltpu.SemaphoreType.DMA((6,)),
            pltpu.SemaphoreType.DMA((2, 8)),
        ],
        compiler_params=params(4),
        name="edges",
    )(u, c, impedance, cmap)


def corners_kernel(y_lo, y_hi, near_out, far_out):
    below, above = has_elecs()
    for out, side in zip((near_out, far_out), sides()):
        out[...] = jnp.zeros((8, 256), F32)
        out[0:1, :] = below * y_lo[pl.ds(32 + 7 * side, 1), :]
        out[1:2, :] = above * y_hi[pl.ds(32 + 7 * side, 1), :]


def corners(y_lo, y_hi):
    return pl.pallas_call(
        corners_kernel,
        in_specs=[vmem()] * 2,
        out_specs=[vmem()] * 2,
        out_shape=[f32(8, 256)] * 2,
        compiler_params=params(2),
        name="corners",
    )(y_lo, y_hi)


def weights_kernel(
    u_hbm, f, c_hbm, cmap_hbm, admittance_hbm, u, wx, wy, wz, diag, zeta_t, rim, pulled1, keep1,
    c, cmap, admittance, sems, u_sems,
):
    small = [
        pltpu.make_async_copy(cmap_hbm, cmap, sems.at[8]),
        pltpu.make_async_copy(admittance_hbm, admittance, sems.at[9]),
    ]
    rows = [pltpu.make_async_copy(c_hbm.at[x], c.at[x], sems.at[x]) for x in range(8)]
    later = [pltpu.make_async_copy(u_hbm.at[s], u.at[s], u_sems.at[s]) for s in range(4)]
    for copy in small + rows + later:
        copy.start()
    for copy in small:
        copy.wait()
    zeta = gather_rows(cmap[...], admittance[...])
    zeta_t[...] = jnp.transpose(jnp.concatenate([zeta, jnp.zeros((120, 128), F32)], axis=0))
    row = iota((8, 256), 0)
    last_lane = iota((8, 256), 1) == 255
    rows[0].wait()
    for x in range(8):
        if x < 7:
            rows[x + 1].wait()
        here = c[x, tile(0), :]
        rolled = pltpu.roll(here, 7, 0)
        before = None
        for k in range(16):
            up = rolled
            now = here
            if k < 15:
                here = c[x, tile(k + 1), :]
                rolled = pltpu.roll(here, 7, 0)
                up = jnp.where(row == 7, rolled, up)
            along_y = face(now, up)
            if k == 15:
                along_y = jnp.where(row == 7, 0.0, along_y)
            down = pltpu.roll(along_y, 1, 0)
            along_z = jnp.where(last_lane, 0.0, face(now, shift_up(now, 1)))
            total = along_y + jnp.where(row == 0, 0.0 if k == 0 else before, down)
            before = down
            total = total + along_z + shift_down(along_z, 1)
            total = total + zeta_t[tile(k), x : x + 1]
            if x < 7:
                along_x = face(now, c[x + 1, tile(k), :])
                wx[x, tile(k), :] = along_x
                total = total + along_x
            if x > 0:
                total = total + wx[x - 1, tile(k), :]
            wy[x, tile(k), :] = along_y
            wz[x, tile(k), :] = along_z
            diag[x, tile(k), :] = total if x in (0, 7) or k in (0, 15) else OMEGA * inverse(total)
    rim[0] = c[0]
    rim[1] = c[7]
    for copy in later:
        copy.wait()

    def rim_row(n, carry):
        x = 7 * n
        inside = 1 + 5 * n

        def emit(s, k, here, pulled):
            pulled1[n, s, tile(k), :] = pulled
            keep1[n, s, tile(k), :] = KEEP * here

        sweep(
            lambda s, k: u[s, x, tile(k), :],
            lambda s, k: f[s, x, tile(k), :],
            lambda k: wy[x, tile(k), :],
            lambda k: wz[x, tile(k), :],
            [(lambda k: wx[6 * n, tile(k), :], lambda s, k: u[s, inside, tile(k), :])],
            emit,
        )
        return carry

    lax.fori_loop(0, 2, rim_row, 0)


def weights(u, f, c, cmap, admittance):
    outs = [
        kept(4, 8, 128, 256),
        kept(7, 128, 256), kept(8, 128, 256), kept(8, 128, 256), kept(8, 128, 256), kept(128, 128),
        kept(2, 128, 256), kept(2, 4, 128, 256), kept(2, 4, 128, 256),
    ]
    return pl.pallas_call(
        weights_kernel,
        in_specs=[hbm(), vmem()] + [hbm()] * 3,
        out_specs=[vmem()] * len(outs),
        out_shape=outs,
        scratch_shapes=[
            pltpu.VMEM((8, 128, 256), F32),
            pltpu.VMEM((8, 128), jnp.int32),
            pltpu.VMEM((16, 128), F32),
            pltpu.SemaphoreType.DMA((10,)),
            pltpu.SemaphoreType.DMA((4,)),
        ],
        compiler_params=params(4),
        cost_estimate=pl.CostEstimate(flops=20_000_000, bytes_accessed=6_000_000, transcendentals=0),
        name="weights",
    )(u, f, c, cmap, admittance)


def inner_kernel(
    u, f, cmap, own_lo, own_hi, y_lo, y_hi, wx, wy, wz, diag,
    u2, u2_out, gain, wyl, wyh, pulled2, edge_lo, edge_hi, contact,
    u1, sums, folded, middle, sems,
):

    below, above = has_elecs()
    wyl[...] = outer_face(own_lo[32:40, :], below * y_lo[32:40, :])
    wyh[...] = outer_face(own_hi[32:40, :], above * y_hi[32:40, :])
    row = iota((8, 256), 0)
    for x in range(8):
        for k in range(16):
            total = diag[x, tile(k), :]
            if k == 0:
                total = total + jnp.where(row == 0, wyl[x : x + 1, :], 0.0)
            if k == 15:
                total = total + jnp.where(row == 7, wyh[x : x + 1, :], 0.0)
            gain[x, tile(k), :] = OMEGA * inverse(total) if 0 < x < 7 and k in (0, 15) else total

    def with_halos(pulled, s, k, x):
        at = 8 * s + x
        if k == 0:
            pulled = pulled + jnp.where(row == 0, wyl[pl.ds(x, 1), :] * y_lo[pl.ds(at, 1), :], 0.0)
        if k == 15:
            pulled = pulled + jnp.where(row == 7, wyh[pl.ds(x, 1), :] * y_hi[pl.ds(at, 1), :], 0.0)
        return pulled

    def first(x, carry):

        def emit(s, k, here, pulled):
            new = KEEP * here + gain[x, tile(k), :] * with_halos(pulled, s, k, x)
            u1[s, x, tile(k), :] = new
            if k == 0:
                edge_lo[pl.ds(8 * s + x, 1), :] = new[0:1]
            if k == 15:
                edge_hi[pl.ds(8 * s + x, 1), :] = new[7:8]

        sweep(
            lambda s, k: u[s, x, tile(k), :],
            lambda s, k: f[s, x, tile(k), :],
            lambda k: wy[x, tile(k), :],
            lambda k: wz[x, tile(k), :],
            [
                (lambda k: wx[x - 1, tile(k), :], lambda s, k: u[s, x - 1, tile(k), :]),
                (lambda k: wx[x, tile(k), :], lambda s, k: u[s, x + 1, tile(k), :]),
            ],
            emit,
        )
        return carry

    lax.fori_loop(1, 7, first, 0)

    for n in range(2):
        for k in range(16):
            weight = wx[6 * n, tile(k), :]
            for s in range(4):
                pulled2[n, s, tile(k), :] = f[s, 7 * n, tile(k), :] + weight * u1[s, 1 + 5 * n, tile(k), :]

    def second(x, sides_at, target):
        def emit(s, k, here, pulled):
            new = KEEP * here + gain[x, tile(k), :] * pulled
            target[s, tile(k), :] = new
            folded[pl.ds(128 * s + 8 * k, 8), :] = fold(new)

        sweep(
            lambda s, k: u1[s, x, tile(k), :],
            lambda s, k: f[s, x, tile(k), :],
            lambda k: wy[x, tile(k), :],
            lambda k: wz[x, tile(k), :],
            sides_at,
            emit,
        )

    def below_at(x):
        return (lambda k: wx[x - 1, tile(k), :], lambda s, k: u1[s, x - 1, tile(k), :])

    def above_at(x):
        return (lambda k: wx[x, tile(k), :], lambda s, k: u1[s, x + 1, tile(k), :])

    def second_middle(x, carry):
        sums[x - 1] = folded_sums(folded[...])
        second(x, [below_at(x), above_at(x)], middle.at[x - 2])
        pltpu.make_async_copy(middle.at[x - 2], u2_out.at[:, x - 2], sems.at[x - 2]).start()
        return carry

    second(1, [above_at(1)], u2.at[0])
    lax.fori_loop(2, 6, second_middle, 0)
    sums[5] = folded_sums(folded[...])
    second(6, [below_at(6)], u2.at[1])
    sums[6] = folded_sums(folded[...])
    contact[...] = scatter([cmap[x : x + 1, :] for x in range(1, 7)], [sums[x] for x in range(1, 7)])
    for n in range(4):
        pltpu.make_async_copy(middle.at[n], u2_out.at[:, n], sems.at[n]).wait()


def inner(u, f, cmap, own_lo, own_hi, y_lo, y_hi, wx, wy, wz, diag):
    outs = [
        kept(2, 4, 128, 256), stored(4, 4, 128, 256), kept(8, 128, 256), kept(8, 256), kept(8, 256),
        kept(2, 4, 128, 256),
        kept(32, 256), kept(32, 256), kept(64, 128),
    ]
    return pl.pallas_call(
        inner_kernel,
        in_specs=[vmem()] * 11,
        out_specs=[vmem(), hbm()] + [vmem()] * (len(outs) - 2),
        out_shape=outs,
        scratch_shapes=[
            pltpu.VMEM((4, 8, 128, 256), F32),
            pltpu.VMEM((8, 4, 128), F32),
            pltpu.VMEM((512, 128), F32),
            pltpu.VMEM((4, 4, 128, 256), F32),
            pltpu.SemaphoreType.DMA((4,)),
        ],
        compiler_params=params(12),
        cost_estimate=pl.CostEstimate(flops=100_000_000, bytes_accessed=25_000_000, transcendentals=0),
        name="inner",
    )(u, f, cmap, own_lo, own_hi, y_lo, y_hi, wx, wy, wz, diag)


def one_side(
    side, msg, ends, neighbour_ids, cmap, admittance, rim, y_lo, y_hi, wx, wy, wz, gain, wyl, wyh, u2, pulled1, keep1,
    pulled2, out, g_ref, outside_ref, u2_row, u2_inside, folded, faces_done, inside_done, row_done,
):
    x = 7 * side
    zeta = gather_rows(jnp.broadcast_to(neighbour_ids, (8, 128)), admittance[...])
    zeta_t = jnp.transpose(jnp.concatenate([zeta, jnp.zeros((120, 128), F32)], axis=0))
    row = iota((128, 256), 0)
    there = msg[ROW_C : ROW_C + 128, :]
    outside = outer_face(rim[side], there)
    outside_ref[...] = outside
    g = OMEGA * inverse(gain[x] + outside)
    g_ref[...] = g
    for s in range(4):
        out[s] = keep1[side, s] + g * (pulled1[side, s] + outside * msg[128 * s : 128 * s + 128, :])
        at = 8 * s + x
        low = g[0:1] * wyl[pl.ds(x, 1), :] * y_lo[pl.ds(at, 1), :]
        high = g[127:128] * wyh[pl.ds(x, 1), :] * y_hi[pl.ds(at, 1), :]
        out[s, 0:1, :] = out[s, 0:1, :] + low
        out[s, 127:128, :] = out[s, 127:128, :] + high
    faces_done()
    spare = jnp.maximum(there, TINY)
    diag = both_sides(line_weight(spare, 0), 0) + both_sides(line_weight(spare, 1), 1) + zeta_t[:, 0:1]
    diag = diag + outside + outer_face(there, msg[ROW_C2 : ROW_C2 + 128, :])
    diag = diag + jnp.where(row == 0, outer_face(there[0:1], ends[0:1, :]), 0.0)
    diag = diag + jnp.where(row == 127, outer_face(there[127:128], ends[1:2, :]), 0.0)
    factor = OMEGA * outside * inverse(jnp.maximum(diag, TINY))
    beyond = row_sums([factor * out[s] for s in range(4)])
    inside = 1 + 5 * side
    factor = gain[inside] * wx[6 * side]
    slabs = []
    for s in range(4):
        new = factor * out[s]
        u2_inside[s] = u2[side, s] + new
        slabs.append(new)
    inside_done()
    within = row_sums(slabs)

    def emit(s, k, here, pulled):
        new = KEEP * here + g_ref[tile(k), :] * pulled
        u2_row[s, tile(k), :] = new
        folded[pl.ds(128 * s + 8 * k, 8), :] = fold(new)

    sweep(
        lambda s, k: out[s, tile(k), :],
        lambda s, k: pulled2[side, s, tile(k), :],
        lambda k: wy[x, tile(k), :],
        lambda k: wz[x, tile(k), :],
        [],
        emit,
    )
    row_done()
    ids = [neighbour_ids, cmap[pl.ds(inside, 1), :], cmap[pl.ds(x, 1), :]]
    return ids, [beyond, within, folded_sums(folded[...])]


def sender():
    copies = []

    def send(source, target, sem):
        copy = pltpu.make_async_copy(source, target, sem)
        copy.start()
        copies.append(copy)

    return send, copies


def near_kernel(
    cmap, admittance, rim, y_lo, y_hi, msg, ends,
    wx, wy, wz, gain, wyl, wyh, u2, pulled1, keep1, pulled2, contact_in,
    face_out, u2_out, face_near, gain_near, outside_near, contact,
    u2b, folded, sems,
):
    send, copies = sender()
    ids, values = one_side(
        sides()[0], msg, ends, msg[ROW_MAP : ROW_MAP + 1, 0:128].astype(jnp.int32), cmap, admittance, rim, y_lo, y_hi,
        wx, wy, wz, gain, wyl, wyh, u2, pulled1, keep1, pulled2, face_near, gain_near, outside_near,
        u2b.at[0], u2b.at[1], folded,
        lambda: send(face_near, face_out, sems.at[0]),
        lambda: send(u2b.at[1], u2_out.at[1], sems.at[1]),
        lambda: send(u2b.at[0], u2_out.at[0], sems.at[2]),
    )
    contact[...] = contact_in[...] + scatter(ids, values)
    for copy in copies:
        copy.wait()


def near_side(*args):
    outs = [
        stored(4, 128, 256), stored(2, 4, 128, 256),
        kept(4, 128, 256), kept(128, 256), kept(128, 256), kept(64, 128),
    ]
    return pl.pallas_call(
        near_kernel,
        in_specs=[vmem()] * len(args),
        out_specs=[hbm()] * 2 + [vmem()] * 4,
        out_shape=outs,
        scratch_shapes=[
            pltpu.VMEM((2, 4, 128, 256), F32),
            pltpu.VMEM((512, 128), F32),
            pltpu.SemaphoreType.DMA((3,)),
        ],
        compiler_params=params(12),
        cost_estimate=pl.CostEstimate(flops=25_000_000, bytes_accessed=8_000_000, transcendentals=0),
        name="near_side",
    )(*args)


def far_kernel(
    pairs, amplitudes, face_near, gain_near, outside_near, ends_near, e_lo, e_hi, zeta_in,
    cmap, admittance, rim, y_lo, y_hi, msg, ends,
    wx, wy, wz, gain, wyl, wyh, u2, pulled1, keep1, pulled2, contact_in,
    face_out, edge_lo_out, edge_hi_out, u2_out, gain_out, wxf_out, misc_out, zeta_out, mine, other,
    face_far, edge_lo, edge_hi, u2b, gain_far, outside_far, misc, folded, sems,
):
    near, far = sides()
    send, copies = sender()
    send(gain.at[pl.ds(1, 6)], gain_out.at[pl.ds(1, 6)], sems.at[0])
    send(gain_near, gain_out.at[7 * near], sems.at[1])
    send(outside_near, wxf_out.at[0], sems.at[2])
    send(zeta_in, zeta_out, sems.at[3])
    misc[0:8, :] = wyl[...]
    misc[8:16, :] = wyh[...]
    send(misc, misc_out, sems.at[4])
    id_rows, values = one_side(
        far, msg, ends, msg[ROW_MAP : ROW_MAP + 1, 0:128].astype(jnp.int32), cmap, admittance, rim, y_lo, y_hi,
        wx, wy, wz, gain, wyl, wyh, u2, pulled1, keep1, pulled2, face_far, gain_far, outside_far,
        u2b.at[0], u2b.at[1], folded,
        lambda: send(face_far, face_out, sems.at[5]),
        lambda: send(u2b.at[1], u2_out.at[1], sems.at[6]),
        lambda: send(u2b.at[0], u2_out.at[0], sems.at[7]),
    )
    send(gain_far, gain_out.at[7 * far], sems.at[8])
    send(outside_far, wxf_out.at[1], sems.at[9])

    lanes = iota((1, 128), 1)
    low_ids = y_lo[48:49, 0:128].astype(jnp.int32)
    high_ids = pltpu.roll(y_hi[48:49, 0:128], 8, 1).astype(jnp.int32)
    edge_ids = jnp.where(lanes < 8, low_ids, jnp.where(lanes < 16, high_ids, 2048))
    zeta = gather_rows(jnp.broadcast_to(edge_ids, (8, 128)), admittance[...])
    zeta_t = jnp.transpose(jnp.concatenate([zeta, jnp.zeros((120, 128), F32)], axis=0))
    edge_sums = jnp.zeros((4, 128), F32)
    for n, (edge_msg, own, inside, edge, y, sent) in enumerate(
        ((y_lo, wyl, e_lo, edge_lo, 0, edge_lo_out), (y_hi, wyh, e_hi, edge_hi, 127, edge_hi_out))
    ):
        edge[0:32, :] = inside[...]
        for s in range(4):
            for side, out in zip(sides(), (face_near, face_far)):
                edge[pl.ds(8 * s + 7 * side, 1), :] = out[s, y : y + 1, :]
        send(edge, sent, sems.at[10 + n])
        there = edge_msg[32:40, :]
        x_rows = iota((8, 256), 0)
        spare = jnp.maximum(there, TINY)
        diag = both_sides(line_weight(spare, 0), 0) + both_sides(line_weight(spare, 1), 1) + own[...]
        diag = diag + outer_face(there, edge_msg[40:48, :])
        for side, corner in zip(sides(), (ends_near, ends)):
            diag = diag + jnp.where(x_rows == 7 * side, outer_face(there, corner[n : n + 1, :]), 0.0)
        diag = diag + zeta_t[8 * n : 8 * n + 8, 0:1]
        factor = OMEGA * own[...] * inverse(jnp.maximum(diag, TINY))
        lined = []
        for s in range(4):
            line = to_lanes(jnp.sum(factor * edge[8 * s : 8 * s + 8, :], axis=1, keepdims=True))
            lined.append(pltpu.roll(line, 8 * n, 1) if n else line)
        edge_sums = edge_sums + jnp.concatenate(lined, axis=0)
    id_rows.append(edge_ids)
    values.append(edge_sums)

    total = (contact_in[...] + scatter(id_rows, values)) * (1.0 / 256.0)
    place = iota((64, 128), 0)
    electrode = (4 * ((place // 8) % 4) + 2 * (place // 32) + (place // 4) % 2) * 128 + iota((64, 128), 1)
    adds = jnp.logical_and(lax.axis_index("zx") == 0, lax.axis_index("elec") == 0)
    adds = jnp.logical_and(adds, lax.axis_index("core") == 0)
    for s in range(4):
        at = place % 4 == s
        amount = jnp.where(adds, amplitudes[0:1, s : s + 1], 0.0)
        total = total + jnp.where(at & (electrode == pairs[0:1, s : s + 1]), amount, 0.0)
        total = total - jnp.where(at & (electrode == pairs[1:2, s : s + 1]), amount, 0.0)
    first_half = lax.axis_index("core") == 0
    mine[...] = jnp.where(first_half, total[0:32], total[32:64])
    other[...] = jnp.where(first_half, total[32:64], total[0:32])
    for copy in copies:
        copy.wait()


def far_side(*args):
    outs = [
        stored(4, 128, 256), stored(32, 256), stored(32, 256),
        stored(2, 4, 128, 256), stored(8, 128, 256), stored(2, 128, 256), stored(16, 256), stored(128, 128),
        f32(32, 128), f32(32, 128),
    ]
    return pl.pallas_call(
        far_kernel,
        in_specs=[vmem()] * len(args),
        out_specs=[hbm()] * 8 + [vmem()] * 2,
        out_shape=outs,
        scratch_shapes=[
            pltpu.VMEM((4, 128, 256), F32),
            pltpu.VMEM((32, 256), F32),
            pltpu.VMEM((32, 256), F32),
            pltpu.VMEM((2, 4, 128, 256), F32),
            pltpu.VMEM((128, 256), F32),
            pltpu.VMEM((128, 256), F32),
            pltpu.VMEM((16, 256), F32),
            pltpu.VMEM((512, 128), F32),
            pltpu.SemaphoreType.DMA((12,)),
        ],
        compiler_params=params(12),
        cost_estimate=pl.CostEstimate(flops=25_000_000, bytes_accessed=8_000_000, transcendentals=0),
        name="far_side",
    )(*args)


def spread_kernel(mine, got, out, copies, sem):
    both = mine[...] + got[...]
    for n in range(out.shape[0]):
        copies[n] = both
    copy = pltpu.make_async_copy(copies, out, sem)
    copy.start()
    copy.wait()


def spread(mine, got, count):
    return pl.pallas_call(
        spread_kernel,
        in_specs=[vmem()] * 2,
        out_specs=hbm(),
        out_shape=stored(count, 32, 128),
        scratch_shapes=[pltpu.VMEM((count, 32, 128), F32), pltpu.SemaphoreType.DMA],
        compiler_params=params(2),
        name="spread",
    )(mine, got)


def gathered_kernel(parts_hbm, edge_lo, edge_hi, to_above, to_below, out, parts, sems, edge_sems):
    copies = [pltpu.make_async_copy(parts_hbm, parts, sems.at[0])]
    for n, (source, target) in enumerate(((edge_hi, to_above), (edge_lo, to_below))):
        copies.append(pltpu.make_async_copy(source, target.at[pl.ds(16, 32)], edge_sems.at[n]))
    for copy in copies:
        copy.start()
    for copy in copies:
        copy.wait()
    total = jnp.sum(parts[...], axis=0)
    for target in (out, to_above, to_below):
        target[0:16, 0:128] = total[0:16]
        target[0:16, 128:256] = total[16:32]


def gathered(parts, edge_lo, edge_hi):
    return pl.pallas_call(
        gathered_kernel,
        in_specs=[pl.BlockSpec(memory_space=pl.ANY)] + [hbm()] * 2,
        out_specs=[vmem()] * 3,
        out_shape=[f32(48, 256), f32(48, 256), f32(16, 256)],
        scratch_shapes=[
            pltpu.VMEM(parts.shape, F32),
            pltpu.SemaphoreType.DMA((1,)),
            pltpu.SemaphoreType.DMA((2,)),
        ],
        compiler_params=params(4),
        name="gathered",
    )(parts, edge_lo, edge_hi)


def blocks_kernel(a0, a1, a2, a3, i0, i1, i2, i3, pull, out, charges):
    elec = lax.axis_index("elec")
    total = a0[0:16, :] + a1[0:16, :] + a2[...] + a3[0:16, :]
    for e in range(4):
        charges[e] = total[8 * (e % 2) : 8 * (e % 2) + 8, 128 * (e // 2) : 128 * (e // 2) + 128]
    upper = iota((8, 128), 0) < 4
    for turn, blocks in ((3, i0), (1, i1), (0, i2), (2, i3)):
        e = lax.rem(elec + turn, 4)
        charge = charges[e]
        start = blocks.shape[0] - 128
        both = blocks[start : start + 128, :]
        first = lax.dot_general(charge, both[:, 0:128], NT, precision=EXACT, preferred_element_type=F32)
        second = lax.dot_general(charge, both[:, 128:256], NT, precision=EXACT, preferred_element_type=F32)
        out[e] = jnp.where(upper, first, second)


def blocks(parts, impedances, pull):
    return pl.pallas_call(
        blocks_kernel,
        in_specs=[vmem()] * 8 + [pl.BlockSpec(memory_space=pl.ANY)],
        out_specs=vmem(),
        out_shape=f32(4, 8, 128),
        scratch_shapes=[pltpu.VMEM((4, 8, 128), F32)],
        compiler_params=params(4),
        name="blocks",
    )(*parts, *impedances, pull)


def ready_kernel(
    after, inner_hbm, near_hbm, far_hbm, gain_hbm, wxf_hbm, misc_hbm, zeta_hbm, base, pull, sides_out, rows_out,
    gain, wxf, misc, zeta_t, sems, small_sems,
):
    order = (2, 3, 4, 5, 1, 6, 0, 7)
    middle = [pltpu.make_async_copy(inner_hbm, base.at[:, pl.ds(2, 4)], sems.at[0])]
    rest = []
    for n, (side, source) in enumerate(zip(sides(), (near_hbm, far_hbm))):
        for inside in range(2):
            x = 7 * side + inside * (1 - 2 * side)
            rest.append(pltpu.make_async_copy(source.at[inside], base.at[:, x], sems.at[1 + 2 * n + inside]))
    small = [
        pltpu.make_async_copy(source, target, small_sems.at[n])
        for n, (source, target) in enumerate(
            ((zeta_hbm, zeta_t), (misc_hbm, misc), (gain_hbm, gain), (wxf_hbm, wxf))
        )
    ]
    for copy in small:
        copy.start()
    for copy in middle + rest:
        copy.start()
    for copy in small:
        copy.wait()
    for x in order:
        g = gain[x]
        part = (1.0 / OMEGA) * zeta_t[:, x : x + 1] * g
        pull[x] = part
        sides_out[x : x + 1, :] = (1.0 - part[0:1]) * g[0:1] * misc[x : x + 1, :]
        sides_out[8 + x : 9 + x, :] = (1.0 - part[127:128]) * g[127:128] * misc[8 + x : 9 + x, :]
        for copy in {2: middle, 1: rest}.get(x, ()):
            copy.wait()
        if x in (0, 7):
            n = jnp.where(sides()[0] == x // 7, 0, 1)
            rows_out[x // 7] = (1.0 - part) * g * wxf[n]
        for s in range(4):
            u = base[s, x]
            base[s, x] = u - part * u


def ready(*args):
    return pl.pallas_call(
        ready_kernel,
        in_specs=[pl.BlockSpec(memory_space=pl.ANY)] + [hbm()] * 7,
        out_specs=[vmem()] * 4,
        out_shape=[kept(4, 8, 128, 256), kept(8, 128, 256), kept(16, 256), kept(2, 128, 256)],
        scratch_shapes=[
            pltpu.VMEM((8, 128, 256), F32),
            pltpu.VMEM((2, 128, 256), F32),
            pltpu.VMEM((16, 256), F32),
            pltpu.VMEM((128, 128), F32),
            pltpu.SemaphoreType.DMA((8,)),
            pltpu.SemaphoreType.DMA((4,)),
        ],
        compiler_params=params(8),
        cost_estimate=pl.CostEstimate(flops=10_000_000, bytes_accessed=8_000_000, transcendentals=0),
        name="ready",
    )(*args)


def correct_kernel(
    cmap, own, got, base, pull, weight, row_weight, e_lo, e_hi, h_near, h_far, out_hbm, volts, table, buf, sems
):
    core = lax.axis_index("core")
    elec = lax.axis_index("elec")
    table[core] = own[...]
    table[1 - core] = got[...]
    for h in range(2):
        for j in range(2):
            volts[:, 128 * (2 * h + j) : 128 * (2 * h + j) + 128] = table[h, elec, 4 * j : 4 * j + 4, :]
    ids = cmap[...]
    block = lax.shift_right_logical(ids, 7)
    lane = lax.bitwise_and(ids, 127)
    touched = []
    for s in range(4):
        found = jnp.zeros((8, 128), F32)
        for b in range(16):
            e, h, j = b // 4, (b // 2) % 2, b % 2
            row = jnp.broadcast_to(table[h, e, 4 * j + s : 4 * j + s + 1, :], (8, 128))
            found = jnp.where(block == b, jnp.take_along_axis(row, lane, axis=1), found)
        touched.append(found)
    stacked = jnp.concatenate(touched + [jnp.zeros((96, 128), F32)], axis=0)
    volts_t = jnp.transpose(stacked)
    copies = []
    near_side = sides()[0]
    for x in (1, 2, 3, 4, 5, 6, 0, 7):
        for s in range(4):
            at = 8 * s + x
            new = base[s, x] + pull[x] * volts_t[:, at : at + 1]
            if x in (0, 7):
                halo = jnp.where(near_side == x // 7, h_near[s], h_far[s])
                new = new + row_weight[x // 7] * halo
            buf[s, x] = new
            low = weight[x : x + 1, :] * e_lo[16 + at : 17 + at, :]
            high = weight[8 + x : 9 + x, :] * e_hi[16 + at : 17 + at, :]
            buf[s, x, 0:1, :] = buf[s, x, 0:1, :] + low
            buf[s, x, 127:128, :] = buf[s, x, 127:128, :] + high
        copy = pltpu.make_async_copy(buf.at[:, x], out_hbm.at[:, x], sems.at[x])
        copy.start()
        copies.append(copy)
    for copy in copies:
        copy.wait()


def correct(*args):
    return pl.pallas_call(
        correct_kernel,
        in_specs=[vmem()] * 11,
        out_specs=[hbm(), vmem()],
        out_shape=[f32(4, 8, 128, 256), f32(4, 512)],
        scratch_shapes=[
            pltpu.VMEM((2, 4, 8, 128), F32),
            pltpu.VMEM((4, 8, 128, 256), F32),
            pltpu.SemaphoreType.DMA((8,)),
        ],
        compiler_params=params(8),
        name="correct",
    )(*args)


def per_device(u, f, c, cmap, admittance, impedance, pairs, amplitudes):
    tiles = lax.axis_size(TILE)
    groups = lax.axis_size("zx")
    elecs = lax.axis_size("elec")
    admittance = admittance.reshape(16, 128)
    u_hbm, c, impedance = in_hbm(u), in_hbm(c), in_hbm(impedance)

    def rotated(a, turn):
        return lax.ppermute(a, "elec", [(i, (i + turn) % elecs) for i in range(elecs)])

    def near(a):
        return lax.ppermute(a, "core", [(0, 1), (1, 0)])

    def far(a):
        pairs = [(i, i + 1) for i in range(1, tiles - 1, 2)]
        return lax.ppermute(a, TILE, pairs + [(j, i) for i, j in pairs])

    own_lo, own_hi, row_near, row_far, side = edges(u_hbm, c, impedance, in_hbm(cmap))
    y_lo = rotated(own_hi, 1)
    y_hi = rotated(own_lo, elecs - 1)
    x_far = far(row_far)
    x_near = near(row_near)
    opposite = rotated(side, 2)
    ends_near, ends_far = corners(y_lo, y_hi)
    ends_far = far(ends_far)
    ends_near = near(ends_near)

    u, wx, wy, wz, diag, zeta_t, rim, pulled1, keep1 = weights(u_hbm, f, c, in_hbm(cmap), in_hbm(admittance))
    u2, u2_inner, gain, wyl, wyh, pulled2, e_lo, e_hi, contact = inner(
        u, f, cmap, own_lo, own_hi, y_lo, y_hi, wx, wy, wz, diag
    )
    shared = (wx, wy, wz, gain, wyl, wyh, u2, pulled1, keep1, pulled2)
    face_near, u2_near, own_near, gain_near, outside_near, contact = near_side(
        cmap, admittance, rim, y_lo, y_hi, x_near, ends_near, *shared, contact
    )
    face_far, edge_lo, edge_hi, u2_far, gain, wxf, misc, zeta_t, mine, other = far_side(
        pairs.T, amplitudes.reshape(1, -1), own_near, gain_near, outside_near, ends_near, e_lo, e_hi, zeta_t,
        cmap, admittance, rim, y_lo, y_hi, x_far, ends_far, *shared, contact,
    )
    h_far = far(face_far)
    h_near = near(face_near)
    parts = spread(mine, near(other), groups)
    parts = lax.all_to_all(parts, "zx", 0, 0, tiled=True)
    to_above, to_below, summed = gathered(parts, in_hbm(edge_lo), in_hbm(edge_hi))
    base, pull, weight, row_weight = ready(
        summed, in_hbm(u2_inner), in_hbm(u2_near), in_hbm(u2_far), in_hbm(gain), in_hbm(wxf), in_hbm(misc), in_hbm(zeta_t)
    )
    e_lo = rotated(to_above, 1)
    e_hi = rotated(to_below, elecs - 1)
    own = blocks((e_lo, e_hi, summed, rotated(summed, 2)), (y_lo, y_hi, side, opposite), pull)
    got = near(own)
    out, volts = correct(cmap, own, got, base, pull, weight, row_weight, e_lo, e_hi, h_near, h_far)
    return out, volts


def solution(mesh):
    tile, src, elec = mesh.devices.shape
    cut = Mesh(mesh.devices.reshape(tile // 2, 2, src, elec), ("zx", "core", "src", "elec"))
    placed = (
        P("src", TILE, "elec", None),
        P("src", TILE, "elec", None),
        P(TILE, "elec", None),
        P(TILE, "elec"),
        P(),
        P("elec", None, None),
        P("src", None),
        P("src"),
    )
    return jax.shard_map(
        per_device,
        mesh=cut,
        in_specs=placed,
        out_specs=(P("src", TILE, "elec", None), P("src", "elec")),
        check_vma=False,
    )
```

```python
import jax
import jax.numpy as jnp
from jax import lax
from jax.experimental import pallas as pl
from jax.experimental.pallas import tpu as pltpu
from jax.sharding import Mesh
from jax.sharding import PartitionSpec as P

OMEGA = 0.8
KEEP = 1.0 - OMEGA
TINY = 1e-30
F32 = jnp.float32
MIB = 1024 * 1024
TILE = ("zx", "core")

NT = (((1,), (1,)), ((), ()))


def params(mib):
    return pltpu.CompilerParams(vmem_limit_bytes=mib * MIB)


def vmem():
    return pl.BlockSpec(memory_space=pltpu.VMEM)


def hbm():
    return pl.BlockSpec(memory_space=pltpu.HBM)


def f32(*shape):
    return jax.ShapeDtypeStruct(shape, F32)


def kept(*shape):
    return pltpu.VMEM(shape, F32)


def stored(*shape):
    return pltpu.HBM(shape, F32)


def in_hbm(a):
    return pltpu.with_memory_space_constraint(a, pltpu.HBM)


def inverse(a):
    r = pl.reciprocal(a, approx=True)
    return r * (2.0 - a * r)


def face(a, b):
    return (2.0 * a * b) * inverse(a + b)


def outer_face(a, b):
    return (2.0 * a * b) * inverse(jnp.maximum(a + b, TINY))


def iota(shape, dim):
    return lax.broadcasted_iota(jnp.int32, shape, dim)


def shift_up(a, axis):
    return pltpu.roll(a, a.shape[axis] - 1, axis)


def shift_down(a, axis):
    return pltpu.roll(a, 1, axis)


def in_line(flux_weight, u, axis):
    return flux_weight * shift_up(u, axis) + shift_down(flux_weight * u, axis)


def line_weight(c, axis):
    w = face(c, shift_up(c, axis))
    return jnp.where(iota(c.shape, axis) < c.shape[axis] - 1, w, 0.0)


def both_sides(w, axis):
    return w + shift_down(w, axis)


def tile(k):
    return pl.ds(8 * k, 8)


def sweep(u_at, f_at, wy_at, wz_at, sides_at, emit):
    row = iota((8, 256), 0)
    here = [u_at(s, 0) for s in range(4)]
    rolled = [pltpu.roll(here[s], 7, 0) for s in range(4)]
    before = [None] * 4
    for k in range(16):
        wy = wy_at(k)
        wz = wz_at(k)
        weights_here = [weight(k) for weight, _ in sides_at]
        for s in range(4):
            u = here[s]
            up = rolled[s]
            if k < 15:
                here[s] = u_at(s, k + 1)
                rolled[s] = pltpu.roll(here[s], 7, 0)
                up = jnp.where(row == 7, rolled[s], up)
            down = pltpu.roll(wy * u, 1, 0)
            pulled = f_at(s, k) + wy * up
            pulled = pulled + jnp.where(row == 0, 0.0 if k == 0 else before[s], down)
            before[s] = down
            pulled = pulled + wz * shift_up(u, 1)
            pulled = pulled + shift_down(wz * u, 1)
            for weight, (_, neighbour) in zip(weights_here, sides_at):
                pulled = pulled + weight * neighbour(s, k)
            emit(s, k, u, pulled)


def fold(p):
    return p[:, :128] + p[:, 128:]


def row_sums(slabs):
    return folded_sums(jnp.concatenate([fold(p) for p in slabs], axis=0))


def folded_sums(folded):
    head = folded.astype(jnp.bfloat16)
    rest = (folded - head.astype(F32)).astype(jnp.bfloat16)
    ones = jnp.ones((8, 128), jnp.bfloat16)
    total = lax.dot_general(ones, head, NT, preferred_element_type=F32)
    total = total + lax.dot_general(ones, rest, NT, preferred_element_type=F32)
    return jnp.concatenate([total[0:1, 128 * s : 128 * s + 128] for s in range(4)], axis=0)


def to_lanes(column):
    mask = iota((8, 128), 0) == iota((8, 128), 1)
    return jnp.sum(jnp.where(mask, column, jnp.zeros_like(column)), axis=0, keepdims=True)


def gather_rows(ids, table):
    block = lax.shift_right_logical(ids, 7)
    lane = lax.bitwise_and(ids, 127)
    found = jnp.zeros(ids.shape, F32)
    for b in range(16):
        row = jnp.broadcast_to(table[b : b + 1], ids.shape)
        got = jnp.take_along_axis(row, lane, axis=1)
        found = jnp.where(block == b, got, found)
    return found


def scatter(id_rows, values):
    place = iota((64, 128), 0)
    block_of = 4 * ((place // 8) % 4) + 2 * (place // 32) + (place // 4) % 2
    total = jnp.zeros((128, 128), F32)
    for id_row, value in zip(id_rows, values):
        hit = lax.shift_right_logical(id_row, 7) == block_of
        spread = jnp.where(hit, jnp.concatenate([value] * 16, axis=0), 0.0)
        lane_hit = lax.bitwise_and(id_row, 127) == iota((128, 128), 0)
        onehot = jnp.where(lane_hit, 1.0, 0.0).astype(jnp.bfloat16)
        a = spread.astype(jnp.bfloat16)
        b = (spread - a.astype(F32)).astype(jnp.bfloat16)
        parts = jnp.concatenate([a, b], axis=0)
        total = total + lax.dot_general(parts, onehot, NT, preferred_element_type=F32)
    return total[0:64] + total[64:128]


ROW_C = 512
ROW_C2 = 640
ROW_MAP = 768
ROWS = 776


def sides():
    core = lax.axis_index("core")
    return 1 - core, core


def has_elecs():
    elec = lax.axis_index("elec")
    last = lax.axis_size("elec") - 1
    return jnp.where(elec > 0, 1.0, 0.0), jnp.where(elec < last, 1.0, 0.0)


def edges_kernel(
    u_hbm, c_hbm, imp_hbm, cmap_hbm, out_lo, out_hi, near_out, far_out, blocks, u, c, cmap, imp, side_by_side, sems, whole_sems
):
    core = lax.axis_index("core")
    copies = []
    for n, y in enumerate((0, 120)):
        copies.append(pltpu.make_async_copy(u_hbm.at[:, :, pl.ds(y, 8)], u.at[n], sems.at[2 * n]))
        copies.append(pltpu.make_async_copy(c_hbm.at[:, pl.ds(y, 8)], c.at[n], sems.at[2 * n + 1]))
    whole = []
    for n, (out, side) in enumerate(zip((near_out, far_out), sides())):
        for s in range(4):
            whole.append((u_hbm.at[s, 7 * side], out.at[pl.ds(128 * s, 128)], whole_sems.at[n, s]))
        whole.append((c_hbm.at[7 * side], out.at[pl.ds(ROW_C, 128)], whole_sems.at[n, 4]))
        whole.append((c_hbm.at[1 + 5 * side], out.at[pl.ds(ROW_C2, 128)], whole_sems.at[n, 5]))
    rows_of_blocks = [
        pltpu.make_async_copy(imp_hbm.at[2 * core + n], imp.at[n], whole_sems.at[n, 7]) for n in range(2)
    ]
    whole = [pltpu.make_async_copy(*copy) for copy in whole]
    copies.append(pltpu.make_async_copy(cmap_hbm, cmap, sems.at[4]))
    for copy in copies + rows_of_blocks + whole:
        copy.start()
    for copy in copies + rows_of_blocks:
        copy.wait()
    side_by_side[:, 0:128] = imp[0]
    side_by_side[:, 128:256] = imp[1]
    copy_blocks = pltpu.make_async_copy(side_by_side, blocks, sems.at[5])
    copy_blocks.start()
    for n, out, near, far, lane in ((0, out_lo, 0, 1, 0), (1, out_hi, 7, 6, 127)):
        out[56:184, 0:128] = imp[0]
        out[56:184, 128:256] = imp[1]
        for x in range(8):
            for s in range(4):
                out[8 * s + x : 8 * s + x + 1, :] = u[n, s, x, near : near + 1, :]
            out[32 + x : 33 + x, :] = c[n, x, near : near + 1, :]
            out[40 + x : 41 + x, :] = c[n, x, far : far + 1, :]
        out[48:56, :] = jnp.zeros((8, 256), F32)
        out[48:49, 0:128] = to_lanes(cmap[:, lane : lane + 1].astype(F32))
    for out, side in zip((near_out, far_out), sides()):
        out[ROW_MAP:ROWS, :] = jnp.zeros((8, 256), F32)
        out[ROW_MAP : ROW_MAP + 1, 0:128] = cmap[pl.ds(7 * side, 1), :].astype(F32)
    for copy in whole:
        copy.wait()
    copy_blocks.wait()


def edges(u, c, impedance, cmap):
    return pl.pallas_call(
        edges_kernel,
        in_specs=[hbm()] * 4,
        out_specs=[vmem()] * 4 + [hbm()],
        out_shape=[f32(184, 256), f32(184, 256), f32(ROWS, 256), f32(ROWS, 256), stored(128, 256)],
        scratch_shapes=[
            pltpu.VMEM((2, 4, 8, 8, 256), F32),
            pltpu.VMEM((2, 8, 8, 256), F32),
            pltpu.VMEM((8, 128), jnp.int32),
            pltpu.VMEM((2, 128, 128), F32),
            pltpu.VMEM((128, 256), F32),
            pltpu.SemaphoreType.DMA((6,)),
            pltpu.SemaphoreType.DMA((2, 8)),
        ],
        compiler_params=params(4),
        name="edges",
    )(u, c, impedance, cmap)


def corners_kernel(y_lo, y_hi, near_out, far_out):
    below, above = has_elecs()
    for out, side in zip((near_out, far_out), sides()):
        out[...] = jnp.zeros((8, 256), F32)
        out[0:1, :] = below * y_lo[pl.ds(32 + 7 * side, 1), :]
        out[1:2, :] = above * y_hi[pl.ds(32 + 7 * side, 1), :]


def corners(y_lo, y_hi):
    return pl.pallas_call(
        corners_kernel,
        in_specs=[vmem()] * 2,
        out_specs=[vmem()] * 2,
        out_shape=[f32(8, 256)] * 2,
        compiler_params=params(2),
        name="corners",
    )(y_lo, y_hi)


def weights_kernel(
    u_hbm, f, c_hbm, cmap_hbm, admittance_hbm, u, wx, wy, wz, diag, zeta_t, rim, pulled1, keep1,
    c, cmap, admittance, sems, u_sems,
):
    small = [
        pltpu.make_async_copy(cmap_hbm, cmap, sems.at[8]),
        pltpu.make_async_copy(admittance_hbm, admittance, sems.at[9]),
    ]
    rows = [pltpu.make_async_copy(c_hbm.at[x], c.at[x], sems.at[x]) for x in range(8)]
    later = [pltpu.make_async_copy(u_hbm.at[s], u.at[s], u_sems.at[s]) for s in range(4)]
    for copy in small + rows + later:
        copy.start()
    for copy in small:
        copy.wait()
    zeta = gather_rows(cmap[...], admittance[...])
    zeta_t[...] = jnp.transpose(jnp.concatenate([zeta, jnp.zeros((120, 128), F32)], axis=0))
    row = iota((8, 256), 0)
    last_lane = iota((8, 256), 1) == 255
    rows[0].wait()
    for x in range(8):
        if x < 7:
            rows[x + 1].wait()
        here = c[x, tile(0), :]
        rolled = pltpu.roll(here, 7, 0)
        before = None
        for k in range(16):
            up = rolled
            now = here
            if k < 15:
                here = c[x, tile(k + 1), :]
                rolled = pltpu.roll(here, 7, 0)
                up = jnp.where(row == 7, rolled, up)
            along_y = face(now, up)
            if k == 15:
                along_y = jnp.where(row == 7, 0.0, along_y)
            down = pltpu.roll(along_y, 1, 0)
            along_z = jnp.where(last_lane, 0.0, face(now, shift_up(now, 1)))
            total = along_y + jnp.where(row == 0, 0.0 if k == 0 else before, down)
            before = down
            total = total + along_z + shift_down(along_z, 1)
            total = total + zeta_t[tile(k), x : x + 1]
            if x < 7:
                along_x = face(now, c[x + 1, tile(k), :])
                wx[x, tile(k), :] = along_x
                total = total + along_x
            if x > 0:
                total = total + wx[x - 1, tile(k), :]
            wy[x, tile(k), :] = along_y
            wz[x, tile(k), :] = along_z
            diag[x, tile(k), :] = total if x in (0, 7) or k in (0, 15) else OMEGA * inverse(total)
    rim[0] = c[0]
    rim[1] = c[7]
    for copy in later:
        copy.wait()

    def rim_row(n, carry):
        x = 7 * n
        inside = 1 + 5 * n

        def emit(s, k, here, pulled):
            pulled1[n, s, tile(k), :] = pulled
            keep1[n, s, tile(k), :] = KEEP * here

        sweep(
            lambda s, k: u[s, x, tile(k), :],
            lambda s, k: f[s, x, tile(k), :],
            lambda k: wy[x, tile(k), :],
            lambda k: wz[x, tile(k), :],
            [(lambda k: wx[6 * n, tile(k), :], lambda s, k: u[s, inside, tile(k), :])],
            emit,
        )
        return carry

    lax.fori_loop(0, 2, rim_row, 0)


def weights(u, f, c, cmap, admittance):
    outs = [
        kept(4, 8, 128, 256),
        kept(7, 128, 256), kept(8, 128, 256), kept(8, 128, 256), kept(8, 128, 256), kept(128, 128),
        kept(2, 128, 256), kept(2, 4, 128, 256), kept(2, 4, 128, 256),
    ]
    return pl.pallas_call(
        weights_kernel,
        in_specs=[hbm(), vmem()] + [hbm()] * 3,
        out_specs=[vmem()] * len(outs),
        out_shape=outs,
        scratch_shapes=[
            pltpu.VMEM((8, 128, 256), F32),
            pltpu.VMEM((8, 128), jnp.int32),
            pltpu.VMEM((16, 128), F32),
            pltpu.SemaphoreType.DMA((10,)),
            pltpu.SemaphoreType.DMA((4,)),
        ],
        compiler_params=params(4),
        cost_estimate=pl.CostEstimate(flops=20_000_000, bytes_accessed=6_000_000, transcendentals=0),
        name="weights",
    )(u, f, c, cmap, admittance)


def inner_kernel(
    u, f, cmap, own_lo, own_hi, y_lo, y_hi, wx, wy, wz, diag,
    u2, u2_out, gain, wyl, wyh, pulled2, edge_lo, edge_hi, contact,
    u1, sums, folded, middle, sems,
):

    below, above = has_elecs()
    wyl[...] = outer_face(own_lo[32:40, :], below * y_lo[32:40, :])
    wyh[...] = outer_face(own_hi[32:40, :], above * y_hi[32:40, :])
    row = iota((8, 256), 0)
    for x in range(8):
        for k in range(16):
            total = diag[x, tile(k), :]
            if k == 0:
                total = total + jnp.where(row == 0, wyl[x : x + 1, :], 0.0)
            if k == 15:
                total = total + jnp.where(row == 7, wyh[x : x + 1, :], 0.0)
            gain[x, tile(k), :] = OMEGA * inverse(total) if 0 < x < 7 and k in (0, 15) else total

    def with_halos(pulled, s, k, x):
        at = 8 * s + x
        if k == 0:
            pulled = pulled + jnp.where(row == 0, wyl[pl.ds(x, 1), :] * y_lo[pl.ds(at, 1), :], 0.0)
        if k == 15:
            pulled = pulled + jnp.where(row == 7, wyh[pl.ds(x, 1), :] * y_hi[pl.ds(at, 1), :], 0.0)
        return pulled

    def first(x, carry):

        def emit(s, k, here, pulled):
            new = KEEP * here + gain[x, tile(k), :] * with_halos(pulled, s, k, x)
            u1[s, x, tile(k), :] = new
            if k == 0:
                edge_lo[pl.ds(8 * s + x, 1), :] = new[0:1]
            if k == 15:
                edge_hi[pl.ds(8 * s + x, 1), :] = new[7:8]

        sweep(
            lambda s, k: u[s, x, tile(k), :],
            lambda s, k: f[s, x, tile(k), :],
            lambda k: wy[x, tile(k), :],
            lambda k: wz[x, tile(k), :],
            [
                (lambda k: wx[x - 1, tile(k), :], lambda s, k: u[s, x - 1, tile(k), :]),
                (lambda k: wx[x, tile(k), :], lambda s, k: u[s, x + 1, tile(k), :]),
            ],
            emit,
        )
        return carry

    lax.fori_loop(1, 7, first, 0)

    for n in range(2):
        for k in range(16):
            weight = wx[6 * n, tile(k), :]
            for s in range(4):
                pulled2[n, s, tile(k), :] = f[s, 7 * n, tile(k), :] + weight * u1[s, 1 + 5 * n, tile(k), :]

    def second(x, sides_at, target):
        def emit(s, k, here, pulled):
            new = KEEP * here + gain[x, tile(k), :] * pulled
            target[s, tile(k), :] = new
            folded[pl.ds(128 * s + 8 * k, 8), :] = fold(new)

        sweep(
            lambda s, k: u1[s, x, tile(k), :],
            lambda s, k: f[s, x, tile(k), :],
            lambda k: wy[x, tile(k), :],
            lambda k: wz[x, tile(k), :],
            sides_at,
            emit,
        )

    def below_at(x):
        return (lambda k: wx[x - 1, tile(k), :], lambda s, k: u1[s, x - 1, tile(k), :])

    def above_at(x):
        return (lambda k: wx[x, tile(k), :], lambda s, k: u1[s, x + 1, tile(k), :])

    def second_middle(x, carry):
        sums[x - 1] = folded_sums(folded[...])
        second(x, [below_at(x), above_at(x)], middle.at[x - 2])
        pltpu.make_async_copy(middle.at[x - 2], u2_out.at[:, x - 2], sems.at[x - 2]).start()
        return carry

    second(1, [above_at(1)], u2.at[0])
    lax.fori_loop(2, 6, second_middle, 0)
    sums[5] = folded_sums(folded[...])
    second(6, [below_at(6)], u2.at[1])
    sums[6] = folded_sums(folded[...])
    contact[...] = scatter([cmap[x : x + 1, :] for x in range(1, 7)], [sums[x] for x in range(1, 7)])
    for n in range(4):
        pltpu.make_async_copy(middle.at[n], u2_out.at[:, n], sems.at[n]).wait()


def inner(u, f, cmap, own_lo, own_hi, y_lo, y_hi, wx, wy, wz, diag):
    outs = [
        kept(2, 4, 128, 256), stored(4, 4, 128, 256), kept(8, 128, 256), kept(8, 256), kept(8, 256),
        kept(2, 4, 128, 256),
        kept(32, 256), kept(32, 256), kept(64, 128),
    ]
    return pl.pallas_call(
        inner_kernel,
        in_specs=[vmem()] * 11,
        out_specs=[vmem(), hbm()] + [vmem()] * (len(outs) - 2),
        out_shape=outs,
        scratch_shapes=[
            pltpu.VMEM((4, 8, 128, 256), F32),
            pltpu.VMEM((8, 4, 128), F32),
            pltpu.VMEM((512, 128), F32),
            pltpu.VMEM((4, 4, 128, 256), F32),
            pltpu.SemaphoreType.DMA((4,)),
        ],
        compiler_params=params(12),
        cost_estimate=pl.CostEstimate(flops=100_000_000, bytes_accessed=25_000_000, transcendentals=0),
        name="inner",
    )(u, f, cmap, own_lo, own_hi, y_lo, y_hi, wx, wy, wz, diag)


def one_side(
    side, msg, ends, neighbour_ids, cmap, admittance, rim, y_lo, y_hi, wx, wy, wz, gain, wyl, wyh, u2, pulled1, keep1,
    pulled2, out, g_ref, outside_ref, u2_row, u2_inside, folded, faces_done, inside_done, row_done,
):
    x = 7 * side
    zeta = gather_rows(jnp.broadcast_to(neighbour_ids, (8, 128)), admittance[...])
    zeta_t = jnp.transpose(jnp.concatenate([zeta, jnp.zeros((120, 128), F32)], axis=0))
    row = iota((128, 256), 0)
    there = msg[ROW_C : ROW_C + 128, :]
    outside = outer_face(rim[side], there)
    outside_ref[...] = outside
    g = OMEGA * inverse(gain[x] + outside)
    g_ref[...] = g
    for s in range(4):
        out[s] = keep1[side, s] + g * (pulled1[side, s] + outside * msg[128 * s : 128 * s + 128, :])
        at = 8 * s + x
        low = g[0:1] * wyl[pl.ds(x, 1), :] * y_lo[pl.ds(at, 1), :]
        high = g[127:128] * wyh[pl.ds(x, 1), :] * y_hi[pl.ds(at, 1), :]
        out[s, 0:1, :] = out[s, 0:1, :] + low
        out[s, 127:128, :] = out[s, 127:128, :] + high
    faces_done()
    spare = jnp.maximum(there, TINY)
    diag = both_sides(line_weight(spare, 0), 0) + both_sides(line_weight(spare, 1), 1) + zeta_t[:, 0:1]
    diag = diag + outside + outer_face(there, msg[ROW_C2 : ROW_C2 + 128, :])
    diag = diag + jnp.where(row == 0, outer_face(there[0:1], ends[0:1, :]), 0.0)
    diag = diag + jnp.where(row == 127, outer_face(there[127:128], ends[1:2, :]), 0.0)
    factor = OMEGA * outside * inverse(jnp.maximum(diag, TINY))
    beyond = row_sums([factor * out[s] for s in range(4)])
    inside = 1 + 5 * side
    factor = gain[inside] * wx[6 * side]
    slabs = []
    for s in range(4):
        new = factor * out[s]
        u2_inside[s] = u2[side, s] + new
        slabs.append(new)
    inside_done()
    within = row_sums(slabs)

    def emit(s, k, here, pulled):
        new = KEEP * here + g_ref[tile(k), :] * pulled
        u2_row[s, tile(k), :] = new
        folded[pl.ds(128 * s + 8 * k, 8), :] = fold(new)

    sweep(
        lambda s, k: out[s, tile(k), :],
        lambda s, k: pulled2[side, s, tile(k), :],
        lambda k: wy[x, tile(k), :],
        lambda k: wz[x, tile(k), :],
        [],
        emit,
    )
    row_done()
    ids = [neighbour_ids, cmap[pl.ds(inside, 1), :], cmap[pl.ds(x, 1), :]]
    return ids, [beyond, within, folded_sums(folded[...])]


def sender():
    copies = []

    def send(source, target, sem):
        copy = pltpu.make_async_copy(source, target, sem)
        copy.start()
        copies.append(copy)

    return send, copies


def near_kernel(
    cmap, admittance, rim, y_lo, y_hi, msg, ends,
    wx, wy, wz, gain, wyl, wyh, u2, pulled1, keep1, pulled2, contact_in,
    face_out, u2_out, face_near, gain_near, outside_near, contact,
    u2b, folded, sems,
):
    send, copies = sender()
    ids, values = one_side(
        sides()[0], msg, ends, msg[ROW_MAP : ROW_MAP + 1, 0:128].astype(jnp.int32), cmap, admittance, rim, y_lo, y_hi,
        wx, wy, wz, gain, wyl, wyh, u2, pulled1, keep1, pulled2, face_near, gain_near, outside_near,
        u2b.at[0], u2b.at[1], folded,
        lambda: send(face_near, face_out, sems.at[0]),
        lambda: send(u2b.at[1], u2_out.at[1], sems.at[1]),
        lambda: send(u2b.at[0], u2_out.at[0], sems.at[2]),
    )
    contact[...] = contact_in[...] + scatter(ids, values)
    for copy in copies:
        copy.wait()


def near_side(*args):
    outs = [
        stored(4, 128, 256), stored(2, 4, 128, 256),
        kept(4, 128, 256), kept(128, 256), kept(128, 256), kept(64, 128),
    ]
    return pl.pallas_call(
        near_kernel,
        in_specs=[vmem()] * len(args),
        out_specs=[hbm()] * 2 + [vmem()] * 4,
        out_shape=outs,
        scratch_shapes=[
            pltpu.VMEM((2, 4, 128, 256), F32),
            pltpu.VMEM((512, 128), F32),
            pltpu.SemaphoreType.DMA((3,)),
        ],
        compiler_params=params(12),
        cost_estimate=pl.CostEstimate(flops=25_000_000, bytes_accessed=8_000_000, transcendentals=0),
        name="near_side",
    )(*args)


def far_kernel(
    pairs, amplitudes, face_near, gain_near, outside_near, ends_near, e_lo, e_hi, zeta_in,
    cmap, admittance, rim, y_lo, y_hi, msg, ends,
    wx, wy, wz, gain, wyl, wyh, u2, pulled1, keep1, pulled2, contact_in,
    face_out, edge_lo_out, edge_hi_out, u2_out, gain_out, wxf_out, misc_out, zeta_out, mine, other,
    face_far, edge_lo, edge_hi, u2b, gain_far, outside_far, misc, folded, sems,
):
    near, far = sides()
    send, copies = sender()
    send(gain.at[pl.ds(1, 6)], gain_out.at[pl.ds(1, 6)], sems.at[0])
    send(gain_near, gain_out.at[7 * near], sems.at[1])
    send(outside_near, wxf_out.at[0], sems.at[2])
    send(zeta_in, zeta_out, sems.at[3])
    misc[0:8, :] = wyl[...]
    misc[8:16, :] = wyh[...]
    send(misc, misc_out, sems.at[4])
    id_rows, values = one_side(
        far, msg, ends, msg[ROW_MAP : ROW_MAP + 1, 0:128].astype(jnp.int32), cmap, admittance, rim, y_lo, y_hi,
        wx, wy, wz, gain, wyl, wyh, u2, pulled1, keep1, pulled2, face_far, gain_far, outside_far,
        u2b.at[0], u2b.at[1], folded,
        lambda: send(face_far, face_out, sems.at[5]),
        lambda: send(u2b.at[1], u2_out.at[1], sems.at[6]),
        lambda: send(u2b.at[0], u2_out.at[0], sems.at[7]),
    )
    send(gain_far, gain_out.at[7 * far], sems.at[8])
    send(outside_far, wxf_out.at[1], sems.at[9])

    lanes = iota((1, 128), 1)
    low_ids = y_lo[48:49, 0:128].astype(jnp.int32)
    high_ids = pltpu.roll(y_hi[48:49, 0:128], 8, 1).astype(jnp.int32)
    edge_ids = jnp.where(lanes < 8, low_ids, jnp.where(lanes < 16, high_ids, 2048))
    zeta = gather_rows(jnp.broadcast_to(edge_ids, (8, 128)), admittance[...])
    zeta_t = jnp.transpose(jnp.concatenate([zeta, jnp.zeros((120, 128), F32)], axis=0))
    edge_sums = jnp.zeros((4, 128), F32)
    for n, (edge_msg, own, inside, edge, y, sent) in enumerate(
        ((y_lo, wyl, e_lo, edge_lo, 0, edge_lo_out), (y_hi, wyh, e_hi, edge_hi, 127, edge_hi_out))
    ):
        edge[0:32, :] = inside[...]
        for s in range(4):
            for side, out in zip(sides(), (face_near, face_far)):
                edge[pl.ds(8 * s + 7 * side, 1), :] = out[s, y : y + 1, :]
        send(edge, sent, sems.at[10 + n])
        there = edge_msg[32:40, :]
        x_rows = iota((8, 256), 0)
        spare = jnp.maximum(there, TINY)
        diag = both_sides(line_weight(spare, 0), 0) + both_sides(line_weight(spare, 1), 1) + own[...]
        diag = diag + outer_face(there, edge_msg[40:48, :])
        for side, corner in zip(sides(), (ends_near, ends)):
            diag = diag + jnp.where(x_rows == 7 * side, outer_face(there, corner[n : n + 1, :]), 0.0)
        diag = diag + zeta_t[8 * n : 8 * n + 8, 0:1]
        factor = OMEGA * own[...] * inverse(jnp.maximum(diag, TINY))
        lined = []
        for s in range(4):
            line = to_lanes(jnp.sum(factor * edge[8 * s : 8 * s + 8, :], axis=1, keepdims=True))
            lined.append(pltpu.roll(line, 8 * n, 1) if n else line)
        edge_sums = edge_sums + jnp.concatenate(lined, axis=0)
    id_rows.append(edge_ids)
    values.append(edge_sums)

    total = (contact_in[...] + scatter(id_rows, values)) * (1.0 / 256.0)
    place = iota((64, 128), 0)
    electrode = (4 * ((place // 8) % 4) + 2 * (place // 32) + (place // 4) % 2) * 128 + iota((64, 128), 1)
    adds = jnp.logical_and(lax.axis_index("zx") == 0, lax.axis_index("elec") == 0)
    adds = jnp.logical_and(adds, lax.axis_index("core") == 0)
    for s in range(4):
        at = place % 4 == s
        amount = jnp.where(adds, amplitudes[0:1, s : s + 1], 0.0)
        total = total + jnp.where(at & (electrode == pairs[0:1, s : s + 1]), amount, 0.0)
        total = total - jnp.where(at & (electrode == pairs[1:2, s : s + 1]), amount, 0.0)
    first_half = lax.axis_index("core") == 0
    mine[...] = jnp.where(first_half, total[0:32], total[32:64])
    other[...] = jnp.where(first_half, total[32:64], total[0:32])
    for copy in copies:
        copy.wait()


def far_side(*args):
    outs = [
        stored(4, 128, 256), stored(32, 256), stored(32, 256),
        stored(2, 4, 128, 256), stored(8, 128, 256), stored(2, 128, 256), stored(16, 256), stored(128, 128),
        f32(32, 128), f32(32, 128),
    ]
    return pl.pallas_call(
        far_kernel,
        in_specs=[vmem()] * len(args),
        out_specs=[hbm()] * 8 + [vmem()] * 2,
        out_shape=outs,
        scratch_shapes=[
            pltpu.VMEM((4, 128, 256), F32),
            pltpu.VMEM((32, 256), F32),
            pltpu.VMEM((32, 256), F32),
            pltpu.VMEM((2, 4, 128, 256), F32),
            pltpu.VMEM((128, 256), F32),
            pltpu.VMEM((128, 256), F32),
            pltpu.VMEM((16, 256), F32),
            pltpu.VMEM((512, 128), F32),
            pltpu.SemaphoreType.DMA((12,)),
        ],
        compiler_params=params(12),
        cost_estimate=pl.CostEstimate(flops=25_000_000, bytes_accessed=8_000_000, transcendentals=0),
        name="far_side",
    )(*args)


def spread_kernel(mine, got, out, copies, sem):
    both = mine[...] + got[...]
    for n in range(out.shape[0]):
        copies[n] = both
    copy = pltpu.make_async_copy(copies, out, sem)
    copy.start()
    copy.wait()


def spread(mine, got, count):
    return pl.pallas_call(
        spread_kernel,
        in_specs=[vmem()] * 2,
        out_specs=hbm(),
        out_shape=stored(count, 32, 128),
        scratch_shapes=[pltpu.VMEM((count, 32, 128), F32), pltpu.SemaphoreType.DMA],
        compiler_params=params(2),
        name="spread",
    )(mine, got)


def gathered_kernel(parts_hbm, edge_lo, edge_hi, to_above, to_below, out, parts, sems, edge_sems):
    copies = [pltpu.make_async_copy(parts_hbm, parts, sems.at[0])]
    for n, (source, target) in enumerate(((edge_hi, to_above), (edge_lo, to_below))):
        copies.append(pltpu.make_async_copy(source, target.at[pl.ds(16, 32)], edge_sems.at[n]))
    for copy in copies:
        copy.start()
    for copy in copies:
        copy.wait()
    total = jnp.sum(parts[...], axis=0)
    for target in (out, to_above, to_below):
        target[0:16, 0:128] = total[0:16]
        target[0:16, 128:256] = total[16:32]


def gathered(parts, edge_lo, edge_hi):
    return pl.pallas_call(
        gathered_kernel,
        in_specs=[pl.BlockSpec(memory_space=pl.ANY)] + [hbm()] * 2,
        out_specs=[vmem()] * 3,
        out_shape=[f32(48, 256), f32(48, 256), f32(16, 256)],
        scratch_shapes=[
            pltpu.VMEM(parts.shape, F32),
            pltpu.SemaphoreType.DMA((1,)),
            pltpu.SemaphoreType.DMA((2,)),
        ],
        compiler_params=params(4),
        name="gathered",
    )(parts, edge_lo, edge_hi)


def blocks_kernel(a0, a1, a2, a3, i0, i1, i2, i3, pull, out, charges):
    elec = lax.axis_index("elec")
    total = a0[0:16, :] + a1[0:16, :] + a2[...] + a3[0:16, :]
    for e in range(4):
        charges[e] = total[8 * (e % 2) : 8 * (e % 2) + 8, 128 * (e // 2) : 128 * (e // 2) + 128]
    upper = iota((8, 128), 0) < 4

    def split(a):
        head = a.astype(jnp.bfloat16)
        return head, (a - head.astype(F32)).astype(jnp.bfloat16)

    def product(charge, block):
        head, rest = split(charge)
        block_head, block_rest = split(block)
        total = lax.dot_general(head, block_head, NT, preferred_element_type=F32)
        total = total + lax.dot_general(rest, block_head, NT, preferred_element_type=F32)
        return total + lax.dot_general(head, block_rest, NT, preferred_element_type=F32)

    for turn, blocks in ((3, i0), (1, i1), (0, i2), (2, i3)):
        e = lax.rem(elec + turn, 4)
        charge = charges[e]
        start = blocks.shape[0] - 128
        both = blocks[start : start + 128, :]
        first = product(charge, both[:, 0:128])
        second = product(charge, both[:, 128:256])
        out[e] = jnp.where(upper, first, second)


def blocks(parts, impedances, pull):
    return pl.pallas_call(
        blocks_kernel,
        in_specs=[vmem()] * 8 + [pl.BlockSpec(memory_space=pl.ANY)],
        out_specs=vmem(),
        out_shape=f32(4, 8, 128),
        scratch_shapes=[pltpu.VMEM((4, 8, 128), F32)],
        compiler_params=params(4),
        name="blocks",
    )(*parts, *impedances, pull)


def ready_kernel(
    after, inner_hbm, near_hbm, far_hbm, gain_hbm, wxf_hbm, misc_hbm, zeta_hbm, base, pull, sides_out, rows_out,
    gain, wxf, misc, zeta_t, sems, small_sems,
):
    order = (2, 3, 4, 5, 1, 6, 0, 7)
    middle = [pltpu.make_async_copy(inner_hbm, base.at[:, pl.ds(2, 4)], sems.at[0])]
    rest = []
    for n, (side, source) in enumerate(zip(sides(), (near_hbm, far_hbm))):
        for inside in range(2):
            x = 7 * side + inside * (1 - 2 * side)
            rest.append(pltpu.make_async_copy(source.at[inside], base.at[:, x], sems.at[1 + 2 * n + inside]))
    small = [
        pltpu.make_async_copy(source, target, small_sems.at[n])
        for n, (source, target) in enumerate(
            ((zeta_hbm, zeta_t), (misc_hbm, misc), (gain_hbm, gain), (wxf_hbm, wxf))
        )
    ]
    for copy in small:
        copy.start()
    for copy in middle + rest:
        copy.start()
    for copy in small:
        copy.wait()
    for x in order:
        g = gain[x]
        part = (1.0 / OMEGA) * zeta_t[:, x : x + 1] * g
        pull[x] = part
        sides_out[x : x + 1, :] = (1.0 - part[0:1]) * g[0:1] * misc[x : x + 1, :]
        sides_out[8 + x : 9 + x, :] = (1.0 - part[127:128]) * g[127:128] * misc[8 + x : 9 + x, :]
        for copy in {2: middle, 1: rest}.get(x, ()):
            copy.wait()
        if x in (0, 7):
            n = jnp.where(sides()[0] == x // 7, 0, 1)
            rows_out[x // 7] = (1.0 - part) * g * wxf[n]
        for s in range(4):
            u = base[s, x]
            base[s, x] = u - part * u


def ready(*args):
    return pl.pallas_call(
        ready_kernel,
        in_specs=[pl.BlockSpec(memory_space=pl.ANY)] + [hbm()] * 7,
        out_specs=[vmem()] * 4,
        out_shape=[kept(4, 8, 128, 256), kept(8, 128, 256), kept(16, 256), kept(2, 128, 256)],
        scratch_shapes=[
            pltpu.VMEM((8, 128, 256), F32),
            pltpu.VMEM((2, 128, 256), F32),
            pltpu.VMEM((16, 256), F32),
            pltpu.VMEM((128, 128), F32),
            pltpu.SemaphoreType.DMA((8,)),
            pltpu.SemaphoreType.DMA((4,)),
        ],
        compiler_params=params(8),
        cost_estimate=pl.CostEstimate(flops=10_000_000, bytes_accessed=8_000_000, transcendentals=0),
        name="ready",
    )(*args)


def look_up(ids, half, volts):
    block = lax.shift_right_logical(ids, 7)
    lane = lax.bitwise_and(ids, 127)
    touched = []
    for s in range(4):
        found = jnp.zeros((8, 128), F32)
        for e in range(4):
            for j in range(2):
                row = jnp.broadcast_to(volts[e, 4 * j + s : 4 * j + s + 1, :], (8, 128))
                there = jnp.take_along_axis(row, lane, axis=1)
                found = jnp.where(block == 4 * e + 2 * half + j, there, found)
        touched.append(found)
    return touched


def own_half_kernel(cmap, own, out):
    found = look_up(cmap[...], lax.axis_index("core"), own)
    for s in range(4):
        out[8 * s : 8 * s + 8, :] = found[s]


def own_half(cmap, own):
    return pl.pallas_call(
        own_half_kernel,
        in_specs=[vmem()] * 2,
        out_specs=vmem(),
        out_shape=f32(32, 128),
        compiler_params=params(2),
        name="own_half",
    )(cmap, own)


def correct_kernel(
    cmap, half, own, got, base, pull, weight, row_weight, e_lo, e_hi, h_near, h_far, out_hbm, volts, table, buf, sems
):
    core = lax.axis_index("core")
    elec = lax.axis_index("elec")
    table[core] = own[...]
    table[1 - core] = got[...]
    for h in range(2):
        for j in range(2):
            volts[:, 128 * (2 * h + j) : 128 * (2 * h + j) + 128] = table[h, elec, 4 * j : 4 * j + 4, :]
    found = look_up(cmap[...], 1 - core, got)
    touched = [found[s] + half[8 * s : 8 * s + 8, :] for s in range(4)]
    stacked = jnp.concatenate(touched + [jnp.zeros((96, 128), F32)], axis=0)
    volts_t = jnp.transpose(stacked)
    copies = []
    near_side = sides()[0]
    for x in (1, 2, 3, 4, 5, 6, 0, 7):
        for s in range(4):
            at = 8 * s + x
            new = base[s, x] + pull[x] * volts_t[:, at : at + 1]
            if x in (0, 7):
                halo = jnp.where(near_side == x // 7, h_near[s], h_far[s])
                new = new + row_weight[x // 7] * halo
            buf[s, x] = new
            low = weight[x : x + 1, :] * e_lo[16 + at : 17 + at, :]
            high = weight[8 + x : 9 + x, :] * e_hi[16 + at : 17 + at, :]
            buf[s, x, 0:1, :] = buf[s, x, 0:1, :] + low
            buf[s, x, 127:128, :] = buf[s, x, 127:128, :] + high
        copy = pltpu.make_async_copy(buf.at[:, x], out_hbm.at[:, x], sems.at[x])
        copy.start()
        copies.append(copy)
    for copy in copies:
        copy.wait()


def correct(*args):
    return pl.pallas_call(
        correct_kernel,
        in_specs=[vmem()] * 12,
        out_specs=[hbm(), vmem()],
        out_shape=[f32(4, 8, 128, 256), f32(4, 512)],
        scratch_shapes=[
            pltpu.VMEM((2, 4, 8, 128), F32),
            pltpu.VMEM((4, 8, 128, 256), F32),
            pltpu.SemaphoreType.DMA((8,)),
        ],
        compiler_params=params(8),
        name="correct",
    )(*args)


def per_device(u, f, c, cmap, admittance, impedance, pairs, amplitudes):
    tiles = lax.axis_size(TILE)
    groups = lax.axis_size("zx")
    elecs = lax.axis_size("elec")
    admittance = admittance.reshape(16, 128)
    u_hbm, c, impedance = in_hbm(u), in_hbm(c), in_hbm(impedance)

    def rotated(a, turn):
        return lax.ppermute(a, "elec", [(i, (i + turn) % elecs) for i in range(elecs)])

    def near(a):
        return lax.ppermute(a, "core", [(0, 1), (1, 0)])

    def far(a):
        pairs = [(i, i + 1) for i in range(1, tiles - 1, 2)]
        return lax.ppermute(a, TILE, pairs + [(j, i) for i, j in pairs])

    own_lo, own_hi, row_near, row_far, side = edges(u_hbm, c, impedance, in_hbm(cmap))
    y_lo = rotated(own_hi, 1)
    y_hi = rotated(own_lo, elecs - 1)
    x_far = far(row_far)
    x_near = near(row_near)
    opposite = rotated(side, 2)
    ends_near, ends_far = corners(y_lo, y_hi)
    ends_far = far(ends_far)
    ends_near = near(ends_near)

    u, wx, wy, wz, diag, zeta_t, rim, pulled1, keep1 = weights(u_hbm, f, c, in_hbm(cmap), in_hbm(admittance))
    u2, u2_inner, gain, wyl, wyh, pulled2, e_lo, e_hi, contact = inner(
        u, f, cmap, own_lo, own_hi, y_lo, y_hi, wx, wy, wz, diag
    )
    shared = (wx, wy, wz, gain, wyl, wyh, u2, pulled1, keep1, pulled2)
    face_near, u2_near, own_near, gain_near, outside_near, contact = near_side(
        cmap, admittance, rim, y_lo, y_hi, x_near, ends_near, *shared, contact
    )
    face_far, edge_lo, edge_hi, u2_far, gain, wxf, misc, zeta_t, mine, other = far_side(
        pairs.T, amplitudes.reshape(1, -1), own_near, gain_near, outside_near, ends_near, e_lo, e_hi, zeta_t,
        cmap, admittance, rim, y_lo, y_hi, x_far, ends_far, *shared, contact,
    )
    h_far = far(face_far)
    h_near = near(face_near)
    parts = spread(mine, near(other), groups)
    parts = lax.all_to_all(parts, "zx", 0, 0, tiled=True)
    to_above, to_below, summed = gathered(parts, in_hbm(edge_lo), in_hbm(edge_hi))
    base, pull, weight, row_weight = ready(
        summed, in_hbm(u2_inner), in_hbm(u2_near), in_hbm(u2_far), in_hbm(gain), in_hbm(wxf), in_hbm(misc), in_hbm(zeta_t)
    )
    e_lo = rotated(to_above, 1)
    e_hi = rotated(to_below, elecs - 1)
    own = blocks((e_lo, e_hi, summed, rotated(summed, 2)), (y_lo, y_hi, side, opposite), pull)
    got = near(own)
    out, volts = correct(cmap, own_half(cmap, own), own, got, base, pull, weight, row_weight, e_lo, e_hi, h_near, h_far)
    return out, volts


def solution(mesh):
    tile, src, elec = mesh.devices.shape
    cut = Mesh(mesh.devices.reshape(tile // 2, 2, src, elec), ("zx", "core", "src", "elec"))
    placed = (
        P("src", TILE, "elec", None),
        P("src", TILE, "elec", None),
        P(TILE, "elec", None),
        P(TILE, "elec"),
        P(),
        P("elec", None, None),
        P("src", None),
        P("src"),
    )
    return jax.shard_map(
        per_device,
        mesh=cut,
        in_specs=placed,
        out_specs=(P("src", TILE, "elec", None), P("src", "elec")),
        check_vma=False,
    )
```

```python
import jax
import jax.numpy as jnp
from jax import lax
from jax.experimental import pallas as pl
from jax.experimental.pallas import tpu as pltpu
from jax.sharding import Mesh
from jax.sharding import PartitionSpec as P

OMEGA = 0.8
KEEP = 1.0 - OMEGA
TINY = 1e-30
F32 = jnp.float32
MIB = 1024 * 1024
TILE = ("zx", "core")

NT = (((1,), (1,)), ((), ()))


def params(mib):
    return pltpu.CompilerParams(vmem_limit_bytes=mib * MIB)


def vmem():
    return pl.BlockSpec(memory_space=pltpu.VMEM)


def hbm():
    return pl.BlockSpec(memory_space=pltpu.HBM)


def f32(*shape):
    return jax.ShapeDtypeStruct(shape, F32)


def kept(*shape):
    return pltpu.VMEM(shape, F32)


def stored(*shape):
    return pltpu.HBM(shape, F32)


def in_hbm(a):
    return pltpu.with_memory_space_constraint(a, pltpu.HBM)


def inverse(a):
    r = pl.reciprocal(a, approx=True)
    return r * (2.0 - a * r)


def face(a, b):
    return (2.0 * a * b) * inverse(a + b)


def outer_face(a, b):
    return (2.0 * a * b) * inverse(jnp.maximum(a + b, TINY))


def iota(shape, dim):
    return lax.broadcasted_iota(jnp.int32, shape, dim)


def shift_up(a, axis):
    return pltpu.roll(a, a.shape[axis] - 1, axis)


def shift_down(a, axis):
    return pltpu.roll(a, 1, axis)


def in_line(flux_weight, u, axis):
    return flux_weight * shift_up(u, axis) + shift_down(flux_weight * u, axis)


def line_weight(c, axis):
    w = face(c, shift_up(c, axis))
    return jnp.where(iota(c.shape, axis) < c.shape[axis] - 1, w, 0.0)


def both_sides(w, axis):
    return w + shift_down(w, axis)


def tile(k):
    return pl.ds(8 * k, 8)


def sweep(u_at, f_at, wy_at, wz_at, sides_at, emit):
    row = iota((8, 256), 0)
    here = [u_at(s, 0) for s in range(4)]
    rolled = [pltpu.roll(here[s], 7, 0) for s in range(4)]
    before = [None] * 4
    for k in range(16):
        wy = wy_at(k)
        wz = wz_at(k)
        weights_here = [weight(k) for weight, _ in sides_at]
        for s in range(4):
            u = here[s]
            up = rolled[s]
            if k < 15:
                here[s] = u_at(s, k + 1)
                rolled[s] = pltpu.roll(here[s], 7, 0)
                up = jnp.where(row == 7, rolled[s], up)
            down = pltpu.roll(wy * u, 1, 0)
            pulled = f_at(s, k) + wy * up
            pulled = pulled + jnp.where(row == 0, 0.0 if k == 0 else before[s], down)
            before[s] = down
            pulled = pulled + wz * shift_up(u, 1)
            pulled = pulled + shift_down(wz * u, 1)
            for weight, (_, neighbour) in zip(weights_here, sides_at):
                pulled = pulled + weight * neighbour(s, k)
            emit(s, k, u, pulled)


def fold(p):
    return p[:, :128] + p[:, 128:]


def row_sums(slabs):
    return folded_sums(jnp.concatenate([fold(p) for p in slabs], axis=0))


def folded_sums(folded):
    head = folded.astype(jnp.bfloat16)
    rest = (folded - head.astype(F32)).astype(jnp.bfloat16)
    ones = jnp.ones((8, 128), jnp.bfloat16)
    total = lax.dot_general(ones, head, NT, preferred_element_type=F32)
    total = total + lax.dot_general(ones, rest, NT, preferred_element_type=F32)
    return jnp.concatenate([total[0:1, 128 * s : 128 * s + 128] for s in range(4)], axis=0)


def to_lanes(column):
    mask = iota((8, 128), 0) == iota((8, 128), 1)
    return jnp.sum(jnp.where(mask, column, jnp.zeros_like(column)), axis=0, keepdims=True)


def gather_rows(ids, table):
    block = lax.shift_right_logical(ids, 7)
    lane = lax.bitwise_and(ids, 127)
    found = jnp.zeros(ids.shape, F32)
    for b in range(16):
        row = jnp.broadcast_to(table[b : b + 1], ids.shape)
        got = jnp.take_along_axis(row, lane, axis=1)
        found = jnp.where(block == b, got, found)
    return found


def scatter(id_rows, values):
    place = iota((64, 128), 0)
    block_of = 4 * ((place // 8) % 4) + 2 * (place // 32) + (place // 4) % 2
    total = jnp.zeros((128, 128), F32)
    for id_row, value in zip(id_rows, values):
        hit = lax.shift_right_logical(id_row, 7) == block_of
        spread = jnp.where(hit, jnp.concatenate([value] * 16, axis=0), 0.0)
        lane_hit = lax.bitwise_and(id_row, 127) == iota((128, 128), 0)
        onehot = jnp.where(lane_hit, 1.0, 0.0).astype(jnp.bfloat16)
        a = spread.astype(jnp.bfloat16)
        b = (spread - a.astype(F32)).astype(jnp.bfloat16)
        parts = jnp.concatenate([a, b], axis=0)
        total = total + lax.dot_general(parts, onehot, NT, preferred_element_type=F32)
    return total[0:64] + total[64:128]


ROW_C = 512
ROW_C2 = 640
ROW_MAP = 768
ROWS = 776


def sides():
    core = lax.axis_index("core")
    return 1 - core, core


def has_elecs():
    elec = lax.axis_index("elec")
    last = lax.axis_size("elec") - 1
    return jnp.where(elec > 0, 1.0, 0.0), jnp.where(elec < last, 1.0, 0.0)


def edges_kernel(
    u_hbm, c_hbm, imp_hbm, cmap_hbm, out_lo, out_hi, near_out, far_out, blocks, u, c, cmap, imp, side_by_side, sems, whole_sems
):
    core = lax.axis_index("core")
    copies = []
    for n, y in enumerate((0, 120)):
        copies.append(pltpu.make_async_copy(u_hbm.at[:, :, pl.ds(y, 8)], u.at[n], sems.at[2 * n]))
        copies.append(pltpu.make_async_copy(c_hbm.at[:, pl.ds(y, 8)], c.at[n], sems.at[2 * n + 1]))
    whole = []
    for n, (out, side) in enumerate(zip((near_out, far_out), sides())):
        for s in range(4):
            whole.append((u_hbm.at[s, 7 * side], out.at[pl.ds(128 * s, 128)], whole_sems.at[n, s]))
        whole.append((c_hbm.at[7 * side], out.at[pl.ds(ROW_C, 128)], whole_sems.at[n, 4]))
        whole.append((c_hbm.at[1 + 5 * side], out.at[pl.ds(ROW_C2, 128)], whole_sems.at[n, 5]))
    rows_of_blocks = [
        pltpu.make_async_copy(imp_hbm.at[2 * core + n], imp.at[n], whole_sems.at[n, 7]) for n in range(2)
    ]
    whole = [pltpu.make_async_copy(*copy) for copy in whole]
    copies.append(pltpu.make_async_copy(cmap_hbm, cmap, sems.at[4]))
    for copy in copies + rows_of_blocks + whole:
        copy.start()
    for copy in copies + rows_of_blocks:
        copy.wait()
    side_by_side[:, 0:128] = imp[0]
    side_by_side[:, 128:256] = imp[1]
    copy_blocks = pltpu.make_async_copy(side_by_side, blocks, sems.at[5])
    copy_blocks.start()
    for n, out, near, far, lane in ((0, out_lo, 0, 1, 0), (1, out_hi, 7, 6, 127)):
        out[56:184, 0:128] = imp[0]
        out[56:184, 128:256] = imp[1]
        for x in range(8):
            for s in range(4):
                out[8 * s + x : 8 * s + x + 1, :] = u[n, s, x, near : near + 1, :]
            out[32 + x : 33 + x, :] = c[n, x, near : near + 1, :]
            out[40 + x : 41 + x, :] = c[n, x, far : far + 1, :]
        out[48:56, :] = jnp.zeros((8, 256), F32)
        out[48:49, 0:128] = to_lanes(cmap[:, lane : lane + 1].astype(F32))
    for out, side in zip((near_out, far_out), sides()):
        out[ROW_MAP:ROWS, :] = jnp.zeros((8, 256), F32)
        out[ROW_MAP : ROW_MAP + 1, 0:128] = cmap[pl.ds(7 * side, 1), :].astype(F32)
    for copy in whole:
        copy.wait()
    copy_blocks.wait()


def edges(u, c, impedance, cmap):
    return pl.pallas_call(
        edges_kernel,
        in_specs=[hbm()] * 4,
        out_specs=[vmem()] * 4 + [hbm()],
        out_shape=[f32(184, 256), f32(184, 256), f32(ROWS, 256), f32(ROWS, 256), stored(128, 256)],
        scratch_shapes=[
            pltpu.VMEM((2, 4, 8, 8, 256), F32),
            pltpu.VMEM((2, 8, 8, 256), F32),
            pltpu.VMEM((8, 128), jnp.int32),
            pltpu.VMEM((2, 128, 128), F32),
            pltpu.VMEM((128, 256), F32),
            pltpu.SemaphoreType.DMA((6,)),
            pltpu.SemaphoreType.DMA((2, 8)),
        ],
        compiler_params=params(4),
        name="edges",
    )(u, c, impedance, cmap)


def corners_kernel(y_lo, y_hi, near_out, far_out):
    below, above = has_elecs()
    for out, side in zip((near_out, far_out), sides()):
        out[...] = jnp.zeros((8, 256), F32)
        out[0:1, :] = below * y_lo[pl.ds(32 + 7 * side, 1), :]
        out[1:2, :] = above * y_hi[pl.ds(32 + 7 * side, 1), :]


def corners(y_lo, y_hi):
    return pl.pallas_call(
        corners_kernel,
        in_specs=[vmem()] * 2,
        out_specs=[vmem()] * 2,
        out_shape=[f32(8, 256)] * 2,
        compiler_params=params(2),
        name="corners",
    )(y_lo, y_hi)


def weights_kernel(
    u_hbm, f, c_hbm, cmap_hbm, admittance_hbm, u, wx, wy, wz, diag, zeta_t, rim, pulled1, keep1,
    c, cmap, admittance, sems, u_sems,
):
    small = [
        pltpu.make_async_copy(cmap_hbm, cmap, sems.at[8]),
        pltpu.make_async_copy(admittance_hbm, admittance, sems.at[9]),
    ]
    rows = [pltpu.make_async_copy(c_hbm.at[x], c.at[x], sems.at[x]) for x in range(8)]
    later = [pltpu.make_async_copy(u_hbm.at[s], u.at[s], u_sems.at[s]) for s in range(4)]
    for copy in small + rows + later:
        copy.start()
    for copy in small:
        copy.wait()
    zeta = gather_rows(cmap[...], admittance[...])
    zeta_t[...] = jnp.transpose(jnp.concatenate([zeta, jnp.zeros((120, 128), F32)], axis=0))
    row = iota((8, 256), 0)
    last_lane = iota((8, 256), 1) == 255
    rows[0].wait()
    for x in range(8):
        if x < 7:
            rows[x + 1].wait()
        here = c[x, tile(0), :]
        rolled = pltpu.roll(here, 7, 0)
        before = None
        for k in range(16):
            up = rolled
            now = here
            if k < 15:
                here = c[x, tile(k + 1), :]
                rolled = pltpu.roll(here, 7, 0)
                up = jnp.where(row == 7, rolled, up)
            along_y = face(now, up)
            if k == 15:
                along_y = jnp.where(row == 7, 0.0, along_y)
            down = pltpu.roll(along_y, 1, 0)
            along_z = jnp.where(last_lane, 0.0, face(now, shift_up(now, 1)))
            total = along_y + jnp.where(row == 0, 0.0 if k == 0 else before, down)
            before = down
            total = total + along_z + shift_down(along_z, 1)
            total = total + zeta_t[tile(k), x : x + 1]
            if x < 7:
                along_x = face(now, c[x + 1, tile(k), :])
                wx[x, tile(k), :] = along_x
                total = total + along_x
            if x > 0:
                total = total + wx[x - 1, tile(k), :]
            wy[x, tile(k), :] = along_y
            wz[x, tile(k), :] = along_z
            diag[x, tile(k), :] = total if x in (0, 7) or k in (0, 15) else OMEGA * inverse(total)
    rim[0] = c[0]
    rim[1] = c[7]
    for copy in later:
        copy.wait()

    def rim_row(n, carry):
        x = 7 * n
        inside = 1 + 5 * n

        def emit(s, k, here, pulled):
            pulled1[n, s, tile(k), :] = pulled
            keep1[n, s, tile(k), :] = KEEP * here

        sweep(
            lambda s, k: u[s, x, tile(k), :],
            lambda s, k: f[s, x, tile(k), :],
            lambda k: wy[x, tile(k), :],
            lambda k: wz[x, tile(k), :],
            [(lambda k: wx[6 * n, tile(k), :], lambda s, k: u[s, inside, tile(k), :])],
            emit,
        )
        return carry

    lax.fori_loop(0, 2, rim_row, 0)


def weights(u, f, c, cmap, admittance):
    outs = [
        kept(4, 8, 128, 256),
        kept(7, 128, 256), kept(8, 128, 256), kept(8, 128, 256), kept(8, 128, 256), kept(128, 128),
        kept(2, 128, 256), kept(2, 4, 128, 256), kept(2, 4, 128, 256),
    ]
    return pl.pallas_call(
        weights_kernel,
        in_specs=[hbm(), vmem()] + [hbm()] * 3,
        out_specs=[vmem()] * len(outs),
        out_shape=outs,
        scratch_shapes=[
            pltpu.VMEM((8, 128, 256), F32),
            pltpu.VMEM((8, 128), jnp.int32),
            pltpu.VMEM((16, 128), F32),
            pltpu.SemaphoreType.DMA((10,)),
            pltpu.SemaphoreType.DMA((4,)),
        ],
        compiler_params=params(4),
        cost_estimate=pl.CostEstimate(flops=20_000_000, bytes_accessed=6_000_000, transcendentals=0),
        name="weights",
    )(u, f, c, cmap, admittance)


def inner_kernel(
    u, f, cmap, own_lo, own_hi, y_lo, y_hi, wx, wy, wz, diag,
    u2, u2_out, gain, wyl, wyh, pulled2, edge_lo, edge_hi, contact,
    u1, sums, folded, middle, sems,
):

    below, above = has_elecs()
    wyl[...] = outer_face(own_lo[32:40, :], below * y_lo[32:40, :])
    wyh[...] = outer_face(own_hi[32:40, :], above * y_hi[32:40, :])
    row = iota((8, 256), 0)
    for x in range(8):
        for k in range(16):
            total = diag[x, tile(k), :]
            if k == 0:
                total = total + jnp.where(row == 0, wyl[x : x + 1, :], 0.0)
            if k == 15:
                total = total + jnp.where(row == 7, wyh[x : x + 1, :], 0.0)
            gain[x, tile(k), :] = OMEGA * inverse(total) if 0 < x < 7 and k in (0, 15) else total

    def with_halos(pulled, s, k, x):
        at = 8 * s + x
        if k == 0:
            pulled = pulled + jnp.where(row == 0, wyl[pl.ds(x, 1), :] * y_lo[pl.ds(at, 1), :], 0.0)
        if k == 15:
            pulled = pulled + jnp.where(row == 7, wyh[pl.ds(x, 1), :] * y_hi[pl.ds(at, 1), :], 0.0)
        return pulled

    def first(x, carry):

        def emit(s, k, here, pulled):
            new = KEEP * here + gain[x, tile(k), :] * with_halos(pulled, s, k, x)
            u1[s, x, tile(k), :] = new
            if k == 0:
                edge_lo[pl.ds(8 * s + x, 1), :] = new[0:1]
            if k == 15:
                edge_hi[pl.ds(8 * s + x, 1), :] = new[7:8]

        sweep(
            lambda s, k: u[s, x, tile(k), :],
            lambda s, k: f[s, x, tile(k), :],
            lambda k: wy[x, tile(k), :],
            lambda k: wz[x, tile(k), :],
            [
                (lambda k: wx[x - 1, tile(k), :], lambda s, k: u[s, x - 1, tile(k), :]),
                (lambda k: wx[x, tile(k), :], lambda s, k: u[s, x + 1, tile(k), :]),
            ],
            emit,
        )
        return carry

    lax.fori_loop(1, 7, first, 0)

    for n in range(2):
        for k in range(16):
            weight = wx[6 * n, tile(k), :]
            for s in range(4):
                pulled2[n, s, tile(k), :] = f[s, 7 * n, tile(k), :] + weight * u1[s, 1 + 5 * n, tile(k), :]

    def second(x, sides_at, target):
        def emit(s, k, here, pulled):
            new = KEEP * here + gain[x, tile(k), :] * pulled
            target[s, tile(k), :] = new
            folded[pl.ds(128 * s + 8 * k, 8), :] = fold(new)

        sweep(
            lambda s, k: u1[s, x, tile(k), :],
            lambda s, k: f[s, x, tile(k), :],
            lambda k: wy[x, tile(k), :],
            lambda k: wz[x, tile(k), :],
            sides_at,
            emit,
        )

    def below_at(x):
        return (lambda k: wx[x - 1, tile(k), :], lambda s, k: u1[s, x - 1, tile(k), :])

    def above_at(x):
        return (lambda k: wx[x, tile(k), :], lambda s, k: u1[s, x + 1, tile(k), :])

    def second_middle(x, carry):
        sums[x - 1] = folded_sums(folded[...])
        second(x, [below_at(x), above_at(x)], middle.at[x - 2])
        pltpu.make_async_copy(middle.at[x - 2], u2_out.at[:, x - 2], sems.at[x - 2]).start()
        return carry

    second(1, [above_at(1)], u2.at[0])
    lax.fori_loop(2, 6, second_middle, 0)
    sums[5] = folded_sums(folded[...])
    second(6, [below_at(6)], u2.at[1])
    sums[6] = folded_sums(folded[...])
    contact[...] = scatter([cmap[x : x + 1, :] for x in range(1, 7)], [sums[x] for x in range(1, 7)])
    for n in range(4):
        pltpu.make_async_copy(middle.at[n], u2_out.at[:, n], sems.at[n]).wait()


def inner(u, f, cmap, own_lo, own_hi, y_lo, y_hi, wx, wy, wz, diag):
    outs = [
        kept(2, 4, 128, 256), stored(4, 4, 128, 256), kept(8, 128, 256), kept(8, 256), kept(8, 256),
        kept(2, 4, 128, 256),
        kept(32, 256), kept(32, 256), kept(64, 128),
    ]
    return pl.pallas_call(
        inner_kernel,
        in_specs=[vmem()] * 11,
        out_specs=[vmem(), hbm()] + [vmem()] * (len(outs) - 2),
        out_shape=outs,
        scratch_shapes=[
            pltpu.VMEM((4, 8, 128, 256), F32),
            pltpu.VMEM((8, 4, 128), F32),
            pltpu.VMEM((512, 128), F32),
            pltpu.VMEM((4, 4, 128, 256), F32),
            pltpu.SemaphoreType.DMA((4,)),
        ],
        compiler_params=params(12),
        cost_estimate=pl.CostEstimate(flops=100_000_000, bytes_accessed=25_000_000, transcendentals=0),
        name="inner",
    )(u, f, cmap, own_lo, own_hi, y_lo, y_hi, wx, wy, wz, diag)


def one_side(
    side, msg, ends, neighbour_ids, cmap, admittance, rim, y_lo, y_hi, wx, wy, wz, gain, wyl, wyh, u2, pulled1, keep1,
    pulled2, out, g_ref, outside_ref, u2_row, u2_inside, folded, faces_done, inside_done, row_done,
):
    x = 7 * side
    zeta = gather_rows(jnp.broadcast_to(neighbour_ids, (8, 128)), admittance[...])
    zeta_t = jnp.transpose(jnp.concatenate([zeta, jnp.zeros((120, 128), F32)], axis=0))
    row = iota((128, 256), 0)
    there = msg[ROW_C : ROW_C + 128, :]
    outside = outer_face(rim[side], there)
    outside_ref[...] = outside
    g = OMEGA * inverse(gain[x] + outside)
    g_ref[...] = g
    spare = jnp.maximum(there, TINY)
    diag = both_sides(line_weight(spare, 0), 0) + both_sides(line_weight(spare, 1), 1) + zeta_t[:, 0:1]
    diag = diag + outside + outer_face(there, msg[ROW_C2 : ROW_C2 + 128, :])
    diag = diag + jnp.where(row == 0, outer_face(there[0:1], ends[0:1, :]), 0.0)
    diag = diag + jnp.where(row == 127, outer_face(there[127:128], ends[1:2, :]), 0.0)
    factor = OMEGA * outside * inverse(jnp.maximum(diag, TINY))
    for s in range(4):
        out[s] = keep1[side, s] + g * (pulled1[side, s] + outside * msg[128 * s : 128 * s + 128, :])
        at = 8 * s + x
        low = g[0:1] * wyl[pl.ds(x, 1), :] * y_lo[pl.ds(at, 1), :]
        high = g[127:128] * wyh[pl.ds(x, 1), :] * y_hi[pl.ds(at, 1), :]
        out[s, 0:1, :] = out[s, 0:1, :] + low
        out[s, 127:128, :] = out[s, 127:128, :] + high
    faces_done()
    beyond = row_sums([factor * out[s] for s in range(4)])
    inside = 1 + 5 * side
    factor = gain[inside] * wx[6 * side]
    slabs = []
    for s in range(4):
        new = factor * out[s]
        u2_inside[s] = u2[side, s] + new
        slabs.append(new)
    inside_done()
    within = row_sums(slabs)

    def emit(s, k, here, pulled):
        new = KEEP * here + g_ref[tile(k), :] * pulled
        u2_row[s, tile(k), :] = new
        folded[pl.ds(128 * s + 8 * k, 8), :] = fold(new)

    sweep(
        lambda s, k: out[s, tile(k), :],
        lambda s, k: pulled2[side, s, tile(k), :],
        lambda k: wy[x, tile(k), :],
        lambda k: wz[x, tile(k), :],
        [],
        emit,
    )
    row_done()
    ids = [neighbour_ids, cmap[pl.ds(inside, 1), :], cmap[pl.ds(x, 1), :]]
    return ids, [beyond, within, folded_sums(folded[...])]


def sender():
    copies = []

    def send(source, target, sem):
        copy = pltpu.make_async_copy(source, target, sem)
        copy.start()
        copies.append(copy)

    return send, copies


def near_kernel(
    cmap, admittance, rim, y_lo, y_hi, msg, ends,
    wx, wy, wz, gain, wyl, wyh, u2, pulled1, keep1, pulled2, contact_in,
    face_out, u2_out, face_near, gain_near, outside_near, contact,
    u2b, folded, sems,
):
    send, copies = sender()
    ids, values = one_side(
        sides()[0], msg, ends, msg[ROW_MAP : ROW_MAP + 1, 0:128].astype(jnp.int32), cmap, admittance, rim, y_lo, y_hi,
        wx, wy, wz, gain, wyl, wyh, u2, pulled1, keep1, pulled2, face_near, gain_near, outside_near,
        u2b.at[0], u2b.at[1], folded,
        lambda: send(face_near, face_out, sems.at[0]),
        lambda: send(u2b.at[1], u2_out.at[1], sems.at[1]),
        lambda: send(u2b.at[0], u2_out.at[0], sems.at[2]),
    )
    contact[...] = contact_in[...] + scatter(ids, values)
    for copy in copies:
        copy.wait()


def near_side(*args):
    outs = [
        stored(4, 128, 256), stored(2, 4, 128, 256),
        kept(4, 128, 256), kept(128, 256), kept(128, 256), kept(64, 128),
    ]
    return pl.pallas_call(
        near_kernel,
        in_specs=[vmem()] * len(args),
        out_specs=[hbm()] * 2 + [vmem()] * 4,
        out_shape=outs,
        scratch_shapes=[
            pltpu.VMEM((2, 4, 128, 256), F32),
            pltpu.VMEM((512, 128), F32),
            pltpu.SemaphoreType.DMA((3,)),
        ],
        compiler_params=params(12),
        cost_estimate=pl.CostEstimate(flops=25_000_000, bytes_accessed=8_000_000, transcendentals=0),
        name="near_side",
    )(*args)


def far_kernel(
    pairs, amplitudes, face_near, gain_near, outside_near, ends_near, e_lo, e_hi, zeta_in,
    cmap, admittance, rim, y_lo, y_hi, msg, ends,
    wx, wy, wz, gain, wyl, wyh, u2, pulled1, keep1, pulled2, contact_in,
    face_out, edge_lo_out, edge_hi_out, u2_out, gain_out, wxf_out, misc_out, zeta_out, mine, other,
    face_far, edge_lo, edge_hi, u2b, gain_far, outside_far, misc, folded, sems,
):
    near, far = sides()
    send, copies = sender()
    lanes = iota((1, 128), 1)
    low_ids = y_lo[48:49, 0:128].astype(jnp.int32)
    high_ids = pltpu.roll(y_hi[48:49, 0:128], 8, 1).astype(jnp.int32)
    edge_ids = jnp.where(lanes < 8, low_ids, jnp.where(lanes < 16, high_ids, 2048))
    zeta = gather_rows(jnp.broadcast_to(edge_ids, (8, 128)), admittance[...])
    zeta_t = jnp.transpose(jnp.concatenate([zeta, jnp.zeros((120, 128), F32)], axis=0))
    edge_factors = []
    for n, (edge_msg, own) in enumerate(((y_lo, wyl), (y_hi, wyh))):
        there = edge_msg[32:40, :]
        x_rows = iota((8, 256), 0)
        spare = jnp.maximum(there, TINY)
        diag = both_sides(line_weight(spare, 0), 0) + both_sides(line_weight(spare, 1), 1) + own[...]
        diag = diag + outer_face(there, edge_msg[40:48, :])
        for side, corner in zip(sides(), (ends_near, ends)):
            diag = diag + jnp.where(x_rows == 7 * side, outer_face(there, corner[n : n + 1, :]), 0.0)
        diag = diag + zeta_t[8 * n : 8 * n + 8, 0:1]
        edge_factors.append(OMEGA * own[...] * inverse(jnp.maximum(diag, TINY)))
    send(gain.at[pl.ds(1, 6)], gain_out.at[pl.ds(1, 6)], sems.at[0])
    send(gain_near, gain_out.at[7 * near], sems.at[1])
    send(outside_near, wxf_out.at[0], sems.at[2])
    send(zeta_in, zeta_out, sems.at[3])
    misc[0:8, :] = wyl[...]
    misc[8:16, :] = wyh[...]
    send(misc, misc_out, sems.at[4])
    id_rows, values = one_side(
        far, msg, ends, msg[ROW_MAP : ROW_MAP + 1, 0:128].astype(jnp.int32), cmap, admittance, rim, y_lo, y_hi,
        wx, wy, wz, gain, wyl, wyh, u2, pulled1, keep1, pulled2, face_far, gain_far, outside_far,
        u2b.at[0], u2b.at[1], folded,
        lambda: send(face_far, face_out, sems.at[5]),
        lambda: send(u2b.at[1], u2_out.at[1], sems.at[6]),
        lambda: send(u2b.at[0], u2_out.at[0], sems.at[7]),
    )
    send(gain_far, gain_out.at[7 * far], sems.at[8])
    send(outside_far, wxf_out.at[1], sems.at[9])

    edge_sums = jnp.zeros((4, 128), F32)
    for n, (inside, edge, y, sent) in enumerate(
        ((e_lo, edge_lo, 0, edge_lo_out), (e_hi, edge_hi, 127, edge_hi_out))
    ):
        edge[0:32, :] = inside[...]
        for s in range(4):
            for side, out in zip(sides(), (face_near, face_far)):
                edge[pl.ds(8 * s + 7 * side, 1), :] = out[s, y : y + 1, :]
        send(edge, sent, sems.at[10 + n])
        lined = []
        for s in range(4):
            line = to_lanes(jnp.sum(edge_factors[n] * edge[8 * s : 8 * s + 8, :], axis=1, keepdims=True))
            lined.append(pltpu.roll(line, 8 * n, 1) if n else line)
        edge_sums = edge_sums + jnp.concatenate(lined, axis=0)
    id_rows.append(edge_ids)
    values.append(edge_sums)

    total = (contact_in[...] + scatter(id_rows, values)) * (1.0 / 256.0)
    place = iota((64, 128), 0)
    electrode = (4 * ((place // 8) % 4) + 2 * (place // 32) + (place // 4) % 2) * 128 + iota((64, 128), 1)
    adds = jnp.logical_and(lax.axis_index("zx") == 0, lax.axis_index("elec") == 0)
    adds = jnp.logical_and(adds, lax.axis_index("core") == 0)
    for s in range(4):
        at = place % 4 == s
        amount = jnp.where(adds, amplitudes[0:1, s : s + 1], 0.0)
        total = total + jnp.where(at & (electrode == pairs[0:1, s : s + 1]), amount, 0.0)
        total = total - jnp.where(at & (electrode == pairs[1:2, s : s + 1]), amount, 0.0)
    first_half = lax.axis_index("core") == 0
    mine[...] = jnp.where(first_half, total[0:32], total[32:64])
    other[...] = jnp.where(first_half, total[32:64], total[0:32])
    for copy in copies:
        copy.wait()


def far_side(*args):
    outs = [
        stored(4, 128, 256), stored(32, 256), stored(32, 256),
        stored(2, 4, 128, 256), stored(8, 128, 256), stored(2, 128, 256), stored(16, 256), stored(128, 128),
        f32(32, 128), f32(32, 128),
    ]
    return pl.pallas_call(
        far_kernel,
        in_specs=[vmem()] * len(args),
        out_specs=[hbm()] * 8 + [vmem()] * 2,
        out_shape=outs,
        scratch_shapes=[
            pltpu.VMEM((4, 128, 256), F32),
            pltpu.VMEM((32, 256), F32),
            pltpu.VMEM((32, 256), F32),
            pltpu.VMEM((2, 4, 128, 256), F32),
            pltpu.VMEM((128, 256), F32),
            pltpu.VMEM((128, 256), F32),
            pltpu.VMEM((16, 256), F32),
            pltpu.VMEM((512, 128), F32),
            pltpu.SemaphoreType.DMA((12,)),
        ],
        compiler_params=params(12),
        cost_estimate=pl.CostEstimate(flops=25_000_000, bytes_accessed=8_000_000, transcendentals=0),
        name="far_side",
    )(*args)


def spread_kernel(mine, got, out, copies, sem):
    both = mine[...] + got[...]
    for n in range(out.shape[0]):
        copies[n] = both
    copy = pltpu.make_async_copy(copies, out, sem)
    copy.start()
    copy.wait()


def spread(mine, got, count):
    return pl.pallas_call(
        spread_kernel,
        in_specs=[vmem()] * 2,
        out_specs=hbm(),
        out_shape=stored(count, 32, 128),
        scratch_shapes=[pltpu.VMEM((count, 32, 128), F32), pltpu.SemaphoreType.DMA],
        compiler_params=params(2),
        name="spread",
    )(mine, got)


def gathered_kernel(parts_hbm, edge_lo, edge_hi, to_above, to_below, out, parts, sems, edge_sems):
    copies = [pltpu.make_async_copy(parts_hbm, parts, sems.at[0])]
    for n, (source, target) in enumerate(((edge_hi, to_above), (edge_lo, to_below))):
        copies.append(pltpu.make_async_copy(source, target.at[pl.ds(16, 32)], edge_sems.at[n]))
    for copy in copies:
        copy.start()
    for copy in copies:
        copy.wait()
    total = jnp.sum(parts[...], axis=0)
    for target in (out, to_above, to_below):
        target[0:16, 0:128] = total[0:16]
        target[0:16, 128:256] = total[16:32]


def gathered(parts, edge_lo, edge_hi):
    return pl.pallas_call(
        gathered_kernel,
        in_specs=[pl.BlockSpec(memory_space=pl.ANY)] + [hbm()] * 2,
        out_specs=[vmem()] * 3,
        out_shape=[f32(48, 256), f32(48, 256), f32(16, 256)],
        scratch_shapes=[
            pltpu.VMEM(parts.shape, F32),
            pltpu.SemaphoreType.DMA((1,)),
            pltpu.SemaphoreType.DMA((2,)),
        ],
        compiler_params=params(4),
        name="gathered",
    )(parts, edge_lo, edge_hi)


def blocks_kernel(a0, a1, a2, a3, i0, i1, i2, i3, pull, out, charges):
    elec = lax.axis_index("elec")
    total = a0[0:16, :] + a1[0:16, :] + a2[...] + a3[0:16, :]
    for e in range(4):
        charges[e] = total[8 * (e % 2) : 8 * (e % 2) + 8, 128 * (e // 2) : 128 * (e // 2) + 128]
    upper = iota((8, 128), 0) < 4

    def split(a):
        head = a.astype(jnp.bfloat16)
        return head, (a - head.astype(F32)).astype(jnp.bfloat16)

    def product(charge, block):
        head, rest = split(charge)
        block_head, block_rest = split(block)
        total = lax.dot_general(head, block_head, NT, preferred_element_type=F32)
        total = total + lax.dot_general(rest, block_head, NT, preferred_element_type=F32)
        return total + lax.dot_general(head, block_rest, NT, preferred_element_type=F32)

    for turn, blocks in ((3, i0), (1, i1), (0, i2), (2, i3)):
        e = lax.rem(elec + turn, 4)
        charge = charges[e]
        start = blocks.shape[0] - 128
        both = blocks[start : start + 128, :]
        first = product(charge, both[:, 0:128])
        second = product(charge, both[:, 128:256])
        out[e] = jnp.where(upper, first, second)


def blocks(parts, impedances, pull):
    return pl.pallas_call(
        blocks_kernel,
        in_specs=[vmem()] * 8 + [pl.BlockSpec(memory_space=pl.ANY)],
        out_specs=vmem(),
        out_shape=f32(4, 8, 128),
        scratch_shapes=[pltpu.VMEM((4, 8, 128), F32)],
        compiler_params=params(4),
        name="blocks",
    )(*parts, *impedances, pull)


def ready_kernel(
    after, inner_hbm, near_hbm, far_hbm, gain_hbm, wxf_hbm, misc_hbm, zeta_hbm, base, pull, sides_out, rows_out,
    gain, wxf, misc, zeta_t, sems, small_sems,
):
    order = (2, 3, 4, 5, 1, 6, 0, 7)
    middle = [pltpu.make_async_copy(inner_hbm, base.at[:, pl.ds(2, 4)], sems.at[0])]
    rest = []
    for n, (side, source) in enumerate(zip(sides(), (near_hbm, far_hbm))):
        for inside in range(2):
            x = 7 * side + inside * (1 - 2 * side)
            rest.append(pltpu.make_async_copy(source.at[inside], base.at[:, x], sems.at[1 + 2 * n + inside]))
    small = [
        pltpu.make_async_copy(source, target, small_sems.at[n])
        for n, (source, target) in enumerate(
            ((zeta_hbm, zeta_t), (misc_hbm, misc), (gain_hbm, gain), (wxf_hbm, wxf))
        )
    ]
    for copy in small:
        copy.start()
    for copy in middle + rest:
        copy.start()
    for copy in small:
        copy.wait()
    for x in order:
        g = gain[x]
        part = (1.0 / OMEGA) * zeta_t[:, x : x + 1] * g
        pull[x] = part
        sides_out[x : x + 1, :] = (1.0 - part[0:1]) * g[0:1] * misc[x : x + 1, :]
        sides_out[8 + x : 9 + x, :] = (1.0 - part[127:128]) * g[127:128] * misc[8 + x : 9 + x, :]
        for copy in {2: middle, 1: rest}.get(x, ()):
            copy.wait()
        if x in (0, 7):
            n = jnp.where(sides()[0] == x // 7, 0, 1)
            rows_out[x // 7] = (1.0 - part) * g * wxf[n]
        for s in range(4):
            u = base[s, x]
            base[s, x] = u - part * u


def ready(*args):
    return pl.pallas_call(
        ready_kernel,
        in_specs=[pl.BlockSpec(memory_space=pl.ANY)] + [hbm()] * 7,
        out_specs=[vmem()] * 4,
        out_shape=[kept(4, 8, 128, 256), kept(8, 128, 256), kept(16, 256), kept(2, 128, 256)],
        scratch_shapes=[
            pltpu.VMEM((8, 128, 256), F32),
            pltpu.VMEM((2, 128, 256), F32),
            pltpu.VMEM((16, 256), F32),
            pltpu.VMEM((128, 128), F32),
            pltpu.SemaphoreType.DMA((8,)),
            pltpu.SemaphoreType.DMA((4,)),
        ],
        compiler_params=params(8),
        cost_estimate=pl.CostEstimate(flops=10_000_000, bytes_accessed=8_000_000, transcendentals=0),
        name="ready",
    )(*args)


def look_up(ids, half, volts):
    block = lax.shift_right_logical(ids, 7)
    lane = lax.bitwise_and(ids, 127)
    touched = []
    for s in range(4):
        found = jnp.zeros((8, 128), F32)
        for e in range(4):
            for j in range(2):
                row = jnp.broadcast_to(volts[e, 4 * j + s : 4 * j + s + 1, :], (8, 128))
                there = jnp.take_along_axis(row, lane, axis=1)
                found = jnp.where(block == 4 * e + 2 * half + j, there, found)
        touched.append(found)
    return touched


def own_half_kernel(cmap, own, out):
    found = look_up(cmap[...], lax.axis_index("core"), own)
    for s in range(4):
        out[8 * s : 8 * s + 8, :] = found[s]


def own_half(cmap, own):
    return pl.pallas_call(
        own_half_kernel,
        in_specs=[vmem()] * 2,
        out_specs=vmem(),
        out_shape=f32(32, 128),
        compiler_params=params(2),
        name="own_half",
    )(cmap, own)


def correct_kernel(
    cmap, half, own, got, base, pull, weight, row_weight, e_lo, e_hi, h_near, h_far, out_hbm, volts, table, buf, sems
):
    core = lax.axis_index("core")
    elec = lax.axis_index("elec")
    table[core] = own[...]
    table[1 - core] = got[...]
    for h in range(2):
        for j in range(2):
            volts[:, 128 * (2 * h + j) : 128 * (2 * h + j) + 128] = table[h, elec, 4 * j : 4 * j + 4, :]
    found = look_up(cmap[...], 1 - core, got)
    touched = [found[s] + half[8 * s : 8 * s + 8, :] for s in range(4)]
    stacked = jnp.concatenate(touched + [jnp.zeros((96, 128), F32)], axis=0)
    volts_t = jnp.transpose(stacked)
    copies = []
    near_side = sides()[0]
    for x in (1, 2, 3, 4, 5, 6, 0, 7):
        for s in range(4):
            at = 8 * s + x
            new = base[s, x] + pull[x] * volts_t[:, at : at + 1]
            if x in (0, 7):
                halo = jnp.where(near_side == x // 7, h_near[s], h_far[s])
                new = new + row_weight[x // 7] * halo
            buf[s, x] = new
            low = weight[x : x + 1, :] * e_lo[16 + at : 17 + at, :]
            high = weight[8 + x : 9 + x, :] * e_hi[16 + at : 17 + at, :]
            buf[s, x, 0:1, :] = buf[s, x, 0:1, :] + low
            buf[s, x, 127:128, :] = buf[s, x, 127:128, :] + high
        copy = pltpu.make_async_copy(buf.at[:, x], out_hbm.at[:, x], sems.at[x])
        copy.start()
        copies.append(copy)
    for copy in copies:
        copy.wait()


def correct(*args):
    return pl.pallas_call(
        correct_kernel,
        in_specs=[vmem()] * 12,
        out_specs=[hbm(), vmem()],
        out_shape=[f32(4, 8, 128, 256), f32(4, 512)],
        scratch_shapes=[
            pltpu.VMEM((2, 4, 8, 128), F32),
            pltpu.VMEM((4, 8, 128, 256), F32),
            pltpu.SemaphoreType.DMA((8,)),
        ],
        compiler_params=params(8),
        name="correct",
    )(*args)


def per_device(u, f, c, cmap, admittance, impedance, pairs, amplitudes):
    tiles = lax.axis_size(TILE)
    groups = lax.axis_size("zx")
    elecs = lax.axis_size("elec")
    admittance = admittance.reshape(16, 128)
    u_hbm, c, impedance = in_hbm(u), in_hbm(c), in_hbm(impedance)

    def rotated(a, turn):
        return lax.ppermute(a, "elec", [(i, (i + turn) % elecs) for i in range(elecs)])

    def near(a):
        return lax.ppermute(a, "core", [(0, 1), (1, 0)])

    def far(a):
        pairs = [(i, i + 1) for i in range(1, tiles - 1, 2)]
        return lax.ppermute(a, TILE, pairs + [(j, i) for i, j in pairs])

    own_lo, own_hi, row_near, row_far, side = edges(u_hbm, c, impedance, in_hbm(cmap))
    y_lo = rotated(own_hi, 1)
    y_hi = rotated(own_lo, elecs - 1)
    x_far = far(row_far)
    x_near = near(row_near)
    opposite = rotated(side, 2)
    ends_near, ends_far = corners(y_lo, y_hi)
    ends_far = far(ends_far)
    ends_near = near(ends_near)

    u, wx, wy, wz, diag, zeta_t, rim, pulled1, keep1 = weights(u_hbm, f, c, in_hbm(cmap), in_hbm(admittance))
    u2, u2_inner, gain, wyl, wyh, pulled2, e_lo, e_hi, contact = inner(
        u, f, cmap, own_lo, own_hi, y_lo, y_hi, wx, wy, wz, diag
    )
    shared = (wx, wy, wz, gain, wyl, wyh, u2, pulled1, keep1, pulled2)
    face_near, u2_near, own_near, gain_near, outside_near, contact = near_side(
        cmap, admittance, rim, y_lo, y_hi, x_near, ends_near, *shared, contact
    )
    face_far, edge_lo, edge_hi, u2_far, gain, wxf, misc, zeta_t, mine, other = far_side(
        pairs.T, amplitudes.reshape(1, -1), own_near, gain_near, outside_near, ends_near, e_lo, e_hi, zeta_t,
        cmap, admittance, rim, y_lo, y_hi, x_far, ends_far, *shared, contact,
    )
    h_far = far(face_far)
    h_near = near(face_near)
    parts = spread(mine, near(other), groups)
    parts = lax.all_to_all(parts, "zx", 0, 0, tiled=True)
    to_above, to_below, summed = gathered(parts, in_hbm(edge_lo), in_hbm(edge_hi))
    base, pull, weight, row_weight = ready(
        summed, in_hbm(u2_inner), in_hbm(u2_near), in_hbm(u2_far), in_hbm(gain), in_hbm(wxf), in_hbm(misc), in_hbm(zeta_t)
    )
    e_lo = rotated(to_above, 1)
    e_hi = rotated(to_below, elecs - 1)
    own = blocks((e_lo, e_hi, summed, rotated(summed, 2)), (y_lo, y_hi, side, opposite), pull)
    got = near(own)
    out, volts = correct(cmap, own_half(cmap, own), own, got, base, pull, weight, row_weight, e_lo, e_hi, h_near, h_far)
    return out, volts


def solution(mesh):
    tile, src, elec = mesh.devices.shape
    cut = Mesh(mesh.devices.reshape(tile // 2, 2, src, elec), ("zx", "core", "src", "elec"))
    placed = (
        P("src", TILE, "elec", None),
        P("src", TILE, "elec", None),
        P(TILE, "elec", None),
        P(TILE, "elec"),
        P(),
        P("elec", None, None),
        P("src", None),
        P("src"),
    )
    return jax.shard_map(
        per_device,
        mesh=cut,
        in_specs=placed,
        out_specs=(P("src", TILE, "elec", None), P("src", "elec")),
        check_vma=False,
    )
```
